32 devices in a mesh: cube: 32 (over z, y, x, core).
Axes of the slice: x: 2, y: 2, z: 4, core: 2. Of those that a mesh axis runs over, the one named last changes fastest.
Arguments:
- gfront: float32 [8192, 2048], P('cube'), as said below
- cfront: float32 [8192, 4096], P('cube'), as said below
- rfront: float32 [8192, 8192], P('cube'), as said below
- gmap: int32 [4, 2048], replicated, may hold values from 0 to 4095, as said below
- cmap: int32 [2, 4096], replicated, may hold values from 0 to 8191, as said below
Outputs:
- gfactor: float32 [8192, 256], P('cube')
- cfactor: float32 [8192, 256], P('cube')
- rfactor: float32 [8192, 512], P('cube')
- rschur: float32 [8192, 8192], P('cube')
The draws below stay inside these ranges and needn't reach their ends.
Inputs may be any that keep to these rules, and one draw needn't show every extreme that they name: Entry i of row q goes to a row of the parent front in block b or block b + 8, where b = i // 256 and blocks have 256 rows; within one row of gmap the entries are distinct and increase along each block. Entry i of row c goes to a row of the root front in block b or block b + 16, where b = i // 256 and blocks have 256 rows; within one row of cmap the entries are distinct and increase along each block. `gfront`: every front is symmetric and positive definite. `cfront`: every front is symmetric and positive definite. `rfront`: the front is symmetric and positive definite.
All inputs are finite; a program needn't handle non-finite values.
Results may differ from the reference program's by a relative error of at most 0.0003.
Values sent between devices are 32-bit elements; how exact they have to be, the bound alone decides.
No kernel may reach another device: no remote copies, remote signals or barrier semaphores. Data moves between devices by JAX's collectives and lax.ppermute only.
A program may use at most 128 MiB of HBM per device.

```python
import math
import jax
import jax.numpy as jnp
from jax import lax

TILE = 256
NG = 2048
PG = 1
PC = 1
PR = 2
NC = 4096
NR = 8192
SG = 256
SC = 256
SR = 512
ROWS = 256


def make_fronts(key, count, order):
    key_points = jax.random.fold_in(jax.random.fold_in(key, 7), 0)
    key_sign = jax.random.fold_in(jax.random.fold_in(key, 7), 1)
    key_diag = jax.random.fold_in(jax.random.fold_in(key, 7), 2)
    key_common = jax.random.fold_in(jax.random.fold_in(key, 7), 4)
    points = jax.random.uniform(key_points, (3, count, order), jnp.float32)
    reach = 0.5
    dist = jnp.abs(points[0][:, :, None] - points[0][:, None, :])
    dist = dist + jnp.abs(points[1][:, :, None] - points[1][:, None, :])
    dist = dist + jnp.abs(points[2][:, :, None] - points[2][:, None, :])
    signs = jnp.where(jax.random.bernoulli(key_sign, 0.5, (count, order)), 1.0, -1.0).astype(jnp.float32)
    sign_pair = signs[:, :, None] * signs[:, None, :]
    coupled = jnp.exp(dist * (-1.0 / reach)) * sign_pair
    common = jnp.exp(jax.random.uniform(key_common, (count, order), jnp.float32, math.log(0.5), 0.0))
    coupled = coupled + 0.25 * (common[:, :, None] * common[:, None, :])
    shift = jnp.exp(jax.random.uniform(key_diag, (count, order), jnp.float32, math.log(0.03), math.log(1.5)))
    ids = jnp.arange(order)
    on_diag = (ids[:, None] == ids[None, :])[None, :, :]
    fronts = coupled + jnp.where(on_diag, shift[:, :, None], 0.0)
    return fronts.reshape(count * order, order)


def make_map(key, count, order, rows):
    blocks = order // rows
    keys = jax.random.split(jax.random.fold_in(key, 11), count * blocks)

    def one_block(block_key):
        picked = jax.random.permutation(block_key, 2 * rows - 2)[:rows - 2] + 1
        slots = jnp.concatenate([jnp.zeros((1,), jnp.int32), picked.astype(jnp.int32), jnp.full((1,), 2 * rows - 1, jnp.int32)])
        return jnp.sort(slots)
    slots = jax.vmap(one_block)(keys).reshape(count, blocks, rows)
    block_ids = jnp.arange(blocks, dtype=jnp.int32)[None, :, None]
    mapped = jnp.where(slots < rows, block_ids * rows + slots, (blocks + block_ids) * rows + slots - rows)
    return mapped.reshape(count, order).astype(jnp.int32)


def draw_gfront(key, part):
    return make_fronts(key, 4, NG)


def draw_cfront(key, part):
    return make_fronts(key, 2, NC)


def draw_rfront(key, part):
    return make_fronts(key, 1, NR)


def draw_gmap(key, part):
    return make_map(key, 4, NG, ROWS)


def draw_cmap(key, part):
    return make_map(key, 2, NC, ROWS)


def setup_inputs(seed: int = 0) -> dict:
    seeds = jax.random.split(jax.random.key(seed), 6)
    return {
        "gfront": draw_gfront(jax.random.fold_in(seeds[5], 71), 0),
        "cfront": draw_cfront(jax.random.fold_in(seeds[5], 71), 0),
        "rfront": draw_rfront(jax.random.fold_in(seeds[5], 71), 0),
        "gmap": draw_gmap(jax.random.fold_in(seeds[5], 71), 0),
        "cmap": draw_cmap(jax.random.fold_in(seeds[5], 71), 0),
    }


def partial_factor(front, panels):
    order = front.shape[0]
    ids = jnp.arange(order, dtype=jnp.int32)
    start = order - (panels + 1) * TILE
    pieces = []
    for panel_no in range(panels):
        col_low = start + panel_no * TILE
        col_high = col_low + TILE
        own_cols = front[:, col_low:col_high]
        lower_tri = jnp.linalg.cholesky(front[col_low:col_high, col_low:col_high])
        weights = jax.scipy.linalg.cho_solve((lower_tri, True), own_cols.T).T
        factor = jax.scipy.linalg.solve_triangular(lower_tri, own_cols.T, lower=True).T
        pieces.append(jnp.where(((ids >= col_low) | (ids < start))[:, None], factor, 0.0))
        product = jnp.einsum('rb,nb->rn', weights, own_cols, precision=lax.Precision.HIGHEST)
        remain = (ids >= col_high) | (ids < start)
        trailing = remain[:, None] & remain[None, :]
        front = front - jnp.where(trailing, product, 0.0)
    return (front, jnp.concatenate(pieces, 1))

def kept_ids(order, separator):
    ids = jnp.arange(order, dtype=jnp.int32)
    return (ids < order - separator - TILE) | (ids >= order - TILE)

def place_front(front, separator, front_map):
    order = front.shape[0]
    keep_ids = kept_ids(order, separator)
    keep_mask = keep_ids[:, None] & keep_ids[None, :]
    masked = jnp.where(keep_mask, front, 0.0)
    placed = jnp.zeros((2 * order, 2 * order), front.dtype)
    return placed.at[front_map[:, None], front_map[None, :]].add(masked)

def reference(gfront, cfront, rfront, gmap, cmap):
    g_factors = []
    g_placed = []
    for front_no in range(4):
        block = gfront[front_no * NG:(front_no + 1) * NG]
        done, factor = partial_factor(block, PG)
        g_factors.append(factor)
        g_placed.append(place_front(done, SG, gmap[front_no]))
    c_factors = []
    c_placed = []
    for front_no in range(2):
        block = cfront[front_no * NC:(front_no + 1) * NC] + g_placed[2 * front_no] + g_placed[2 * front_no + 1]
        done, factor = partial_factor(block, PC)
        c_factors.append(factor)
        c_placed.append(place_front(done, SC, cmap[front_no]))
    root = rfront + c_placed[0] + c_placed[1]
    done, rfactor = partial_factor(root, PR)
    rest_ids = kept_ids(NR, SR)
    rest_mask = rest_ids[:, None] & rest_ids[None, :]
    rschur = jnp.where(rest_mask, done, 0.0)
    return (jnp.concatenate(g_factors, 0), jnp.concatenate(c_factors, 0), rfactor, rschur)
```

```python
import functools

import jax
import jax.numpy as jnp
from jax import lax
from jax.experimental import pallas as pl
from jax.experimental.pallas import tpu as pltpu
from jax.sharding import PartitionSpec as P

TILE = 256
STRIP = 32
SUB = 8
LANES = 128
HIGH = lax.Precision.HIGH
HIGHEST = lax.Precision.HIGHEST
NT = (((1,), (1,)), ((), ()))
MIB = 1024 * 1024


def widen(column, width):
    return jnp.concatenate([column] * (width // LANES), 1)


def factor_strip(strip, base):
    width = strip[0].shape[1]
    sub_ids = lax.broadcasted_iota(jnp.int32, (SUB, 1), 0)
    count = len(strip)
    for p in range(count):
        first = base + p * SUB
        cols = [
            [jnp.broadcast_to(strip[q][:, first + j : first + j + 1], (SUB, LANES)) for j in range(SUB)]
            for q in range(p, count)
        ]
        for j in range(SUB):
            pivot = cols[0][j][j : j + 1, :]
            inv = lax.rsqrt(pivot)
            inv = inv * (1.5 - 0.5 * pivot * inv * inv)
            unit = strip[p][j : j + 1, :] * widen(inv, width)
            scaled = [col[j] * inv for col in cols]
            below = jnp.where(sub_ids > j, scaled[0], 0.0)
            strip[p] = jnp.where(sub_ids == j, unit, strip[p] - widen(below, width) * unit)
            for q in range(p + 1, count):
                strip[q] = strip[q] - widen(scaled[q - p], width) * unit
            for m in range(j + 1, SUB):
                head = scaled[0][m : m + 1, :]
                for q in range(p, count):
                    cols[q - p][m] = cols[q - p][m] - scaled[q - p] * head
    return jnp.concatenate(strip, 0)


def inverse_kernel(count, blocks_ref, inverse_ref, work):
    row_ids = lax.broadcasted_iota(jnp.int32, (TILE, TILE), 0)
    col_ids = lax.broadcasted_iota(jnp.int32, (TILE, TILE), 1)
    for t in range(count):
        work[t, :, :TILE] = blocks_ref[t]
        work[t, :, TILE:] = (row_ids == col_ids).astype(jnp.float32)
    for low in range(0, TILE, STRIP):
        high = low + STRIP
        left = low // LANES * LANES
        right = TILE + (high + LANES - 1) // LANES * LANES
        done = []
        for t in range(count):
            strip = [work[t, low + SUB * q : low + SUB * (q + 1), left:right] for q in range(STRIP // SUB)]
            done.append(factor_strip(strip, low - left))
        for t in range(count):
            inverse_ref[t, low:high, : right - TILE] = done[t][:, TILE - left :]
            if right < 2 * TILE:
                inverse_ref[t, low:high, right - TILE :] = jnp.zeros((STRIP, 2 * TILE - right), jnp.float32)
            if high < TILE:
                rest = high // LANES * LANES
                update = lax.dot_general(
                    done[t][:, rest - left : TILE - left],
                    done[t],
                    (((0,), (0,)), ((), ())),
                    precision=HIGHEST,
                    preferred_element_type=jnp.float32,
                )
                work[t, high:, left:right] = work[t, high:, left:right] - update[high - rest :]


def inverse_factors(blocks):
    count = blocks.shape[0]
    return pl.pallas_call(
        functools.partial(inverse_kernel, count),
        out_shape=jax.ShapeDtypeStruct(blocks.shape, jnp.float32),
        in_specs=[pl.BlockSpec(memory_space=pltpu.VMEM)],
        out_specs=pl.BlockSpec(memory_space=pltpu.VMEM),
        scratch_shapes=[pltpu.VMEM((count, TILE, 2 * TILE), jnp.float32)],
        compiler_params=pltpu.CompilerParams(vmem_limit_bytes=16 * MIB),
        cost_estimate=pl.CostEstimate(flops=30_000_000_000, bytes_accessed=1_000_000, transcendentals=0),
    )(blocks)


def halves(value):
    top = value.astype(jnp.bfloat16)
    return top, (value - top.astype(jnp.float32)).astype(jnp.bfloat16)


def dot_nt(left, right):
    return lax.dot_general(left, right, NT, preferred_element_type=jnp.float32)


def dot_nn(left, right):
    return jnp.dot(left, right, preferred_element_type=jnp.float32)


def assemble_kernel(base_ref, keep_ref, recv_ref, place_ref, keep_map_ref, recv_map_ref, out_ref):
    first = pl.program_id(0) * TILE
    targets = first + lax.broadcasted_iota(jnp.int32, (TILE, TILE), 0)
    keep_hot = jnp.where(keep_map_ref[...] == targets, 1.0, 0.0).astype(jnp.bfloat16)
    recv_hot = jnp.where(recv_map_ref[...] == targets, 1.0, 0.0).astype(jnp.bfloat16)
    top, rest = halves(keep_ref[...])
    total = base_ref[...] + (dot_nt(top, keep_hot) + dot_nt(rest, keep_hot))
    top, rest = halves(recv_ref[...])
    moved = dot_nt(top, recv_hot) + dot_nt(rest, recv_hot)
    top, rest = halves(moved)
    place = place_ref[...]
    out_ref[...] = total + (dot_nn(place, top) + dot_nn(place, rest))


def assemble(base, keep, recv, place, keep_map, recv_map):
    rows, order = base.shape
    sent = recv.shape[0]
    child_blocks = order // 2 // TILE
    return pl.pallas_call(
        assemble_kernel,
        grid=(order // TILE,),
        out_shape=jax.ShapeDtypeStruct(base.shape, jnp.float32),
        in_specs=[
            pl.BlockSpec((rows, TILE), lambda n: (0, n)),
            pl.BlockSpec((rows, TILE), lambda n: (0, n % child_blocks)),
            pl.BlockSpec((sent, TILE), lambda n: (0, n % child_blocks)),
            pl.BlockSpec((rows, sent), lambda n: (0, 0)),
            pl.BlockSpec((1, TILE), lambda n: (0, n % child_blocks)),
            pl.BlockSpec((1, TILE), lambda n: (0, n % child_blocks)),
        ],
        out_specs=pl.BlockSpec((rows, TILE), lambda n: (0, n)),
        compiler_params=pltpu.CompilerParams(vmem_limit_bytes=24 * MIB),
        cost_estimate=pl.CostEstimate(
            flops=2 * rows * order * TILE * 6, bytes_accessed=rows * order * 12, transcendentals=0
        ),
    )(base, keep, recv, place, keep_map, recv_map)


def finish_kernel(low, high, base_ref, rows_ref, first_ref, second_ref, weights_ref, out_ref, top_ref, rest_ref):
    block = pl.program_id(0)

    @pl.when(block == 0)
    def _():
        top_ref[...], rest_ref[...] = halves(weights_ref[...])

    rows = rows_ref.shape[0]
    row_ids = base_ref[0] + lax.broadcasted_iota(jnp.int32, (rows, 1), 0)
    kept = (row_ids < low) | (row_ids >= high)
    inside = (block >= low // TILE) & (block < high // TILE)

    @pl.when(inside)
    def _():
        out_ref[...] = jnp.zeros_like(out_ref)

    @pl.when(jnp.logical_not(inside))
    def _():
        product = jnp.zeros((rows, TILE), jnp.float32)
        for k, ref in enumerate((first_ref, second_ref)):
            panel_top, panel_rest = halves(ref[...])
            top = top_ref[:, k * TILE : (k + 1) * TILE]
            rest = rest_ref[:, k * TILE : (k + 1) * TILE]
            product += dot_nt(top, panel_top) + (dot_nt(top, panel_rest) + dot_nt(rest, panel_top))
        out_ref[...] = jnp.where(kept, rows_ref[...] - product, 0.0)


def finish(rows_mat, first, second, weights, first_row):
    rows, order = rows_mat.shape
    low, high = order - 3 * TILE, order - TILE
    return pl.pallas_call(
        functools.partial(finish_kernel, low, high),
        out_shape=jax.ShapeDtypeStruct(rows_mat.shape, jnp.float32),
        grid_spec=pltpu.PrefetchScalarGridSpec(
            num_scalar_prefetch=1,
            grid=(order // TILE,),
            in_specs=[
                pl.BlockSpec((rows, TILE), lambda n, _: (0, n)),
                pl.BlockSpec((TILE, TILE), lambda n, _: (n, 0)),
                pl.BlockSpec((TILE, TILE), lambda n, _: (n, 0)),
                pl.BlockSpec((rows, 2 * TILE), lambda n, _: (0, 0)),
            ],
            out_specs=pl.BlockSpec((rows, TILE), lambda n, _: (0, n)),
            scratch_shapes=[pltpu.VMEM((rows, 2 * TILE), jnp.bfloat16)] * 2,
        ),
        compiler_params=pltpu.CompilerParams(vmem_limit_bytes=24 * MIB),
        cost_estimate=pl.CostEstimate(
            flops=2 * rows * order * TILE * 6, bytes_accessed=rows * order * 16, transcendentals=0
        ),
    )(first_row, rows_mat, first, second, weights)


def product(left, right, precision=HIGHEST):
    return jnp.dot(left, right, precision=precision, preferred_element_type=jnp.float32)


def product_nt(left, right, precision=HIGHEST):
    return lax.dot_general(left, right, NT, precision=precision, preferred_element_type=jnp.float32)


def swap(value, mask):
    pairs = [(source, source ^ mask) for source in range(lax.axis_size("cube"))]
    return lax.ppermute(value, "cube", pairs)


def group_gather(value, group):
    size = lax.axis_size("cube")
    groups = [[g * group + i for i in range(group)] for g in range(size // group)]
    return lax.all_gather(value, "cube", axis=0, tiled=True, axis_index_groups=groups)


def one_hot(positions, count):
    return (positions[None, :] == jnp.arange(count, dtype=jnp.int32)[:, None]).astype(jnp.float32)


def column_targets(front_map):
    order = front_map.shape[0]
    ids = jnp.arange(order, dtype=jnp.int32)
    gone = (ids >= order - 2 * TILE) & (ids < order - TILE)
    return jnp.where(gone, -1, front_map)


class Plan:
    def __init__(self, maps, group, rows):
        me = lax.axis_index("cube")
        front = me // group
        block = me % group
        side = front % 2
        self.own_map = column_targets(lax.dynamic_index_in_dim(maps, front, 0, keepdims=False))
        self.other_map = column_targets(lax.dynamic_index_in_dim(maps, front ^ 1, 0, keepdims=False))
        own = lax.dynamic_slice_in_dim(self.own_map, block * rows, rows, 0)
        other = lax.dynamic_slice_in_dim(self.other_map, block * rows, rows, 0)
        here = (block + group * side) * rows
        there = (block + group * (1 - side)) * rows
        self.keep = one_hot(own - here, rows)
        self.give = one_hot(own - there, rows)
        leaves = (own >= there) & (own < there + rows)
        rank = jnp.where(leaves, jnp.cumsum(leaves.astype(jnp.int32)) - 1, -1)
        self.send = one_hot(rank, rows)
        comes = (other >= here) & (other < here + rows)
        rank = jnp.where(comes, jnp.cumsum(comes.astype(jnp.int32)) - 1, -1)
        self.place = lax.dot_general(one_hot(other - here, rows), one_hot(rank, rows), NT).astype(jnp.bfloat16)


def local(gfront, cfront, rfront, gmap, cmap):
    devices = lax.axis_size("cube")
    me = lax.axis_index("cube")
    quarter = devices // 4
    half = devices // 2
    rows = gfront.shape[0]
    order_g, order_c, order_r = gfront.shape[1], cfront.shape[1], rfront.shape[1]
    g_low, c_low = order_g - 2 * TILE, order_c - 2 * TILE
    r_low = order_r - 3 * TILE
    plan_g = Plan(gmap, quarter, rows)
    plan_c = Plan(cmap, half, rows)

    own_g = gfront[:, g_low : g_low + TILE]
    own_c = cfront[:, c_low : c_low + TILE]
    panel_g = group_gather(own_g, quarter)
    panel_c = group_gather(own_c, half)
    second = lax.all_gather(rfront[:, r_low + TILE : r_low + 2 * TILE], "cube", axis=0, tiled=True)
    diag = jnp.stack([panel_g[g_low : g_low + TILE], panel_c[c_low : c_low + TILE]])
    inverse = inverse_factors(diag)

    def factors(own, inv, order):
        factor = product_nt(own, inv)
        weights = product(factor, inv)
        row_ids = me * rows % order + jnp.arange(rows, dtype=jnp.int32)
        low = order - 2 * TILE
        return factor, weights, row_ids

    gfactor, weights_g, _ = factors(own_g, inverse[0], order_g)
    cfactor, weights_c, _ = factors(own_c, inverse[1], order_c)

    g_edge = gfront[:, g_low - TILE : g_low] - product_nt(weights_g, panel_g[g_low - TILE : g_low])
    edge_map = plan_g.own_map[g_low - TILE : g_low]
    g_edge = product_nt(g_edge, one_hot(edge_map - (c_low - TILE), TILE))
    c_edge = cfront[:, c_low - TILE : c_low] - product_nt(weights_c, panel_c[c_low - TILE : c_low])
    c_edge = c_edge + product(plan_g.keep, g_edge) + swap(product(plan_g.give, g_edge), quarter)
    edge_map = plan_c.own_map[c_low - TILE : c_low]
    c_edge = product_nt(c_edge, one_hot(edge_map - r_low, TILE))
    r_edge = rfront[:, r_low : r_low + TILE]
    r_edge = r_edge + product(plan_c.keep, c_edge) + swap(product(plan_c.give, c_edge), half)
    first = lax.all_gather(r_edge, "cube", axis=0, tiled=True)

    g_done = gfront - product_nt(weights_g, panel_g, HIGH)
    g_recv = swap(product(plan_g.send, g_done, HIGH), quarter)
    g_keep = product(plan_g.keep, g_done, HIGH)
    c_base = cfront - product_nt(weights_c, panel_c, HIGH)
    c_done = assemble(
        c_base, g_keep, g_recv, plan_g.place, plan_g.own_map[None], plan_g.other_map[None]
    )
    c_recv = swap(product(plan_c.send, c_done, HIGH), half)
    c_keep = product(plan_c.keep, c_done, HIGH)
    r_rows = assemble(
        rfront, c_keep, c_recv, plan_c.place, plan_c.own_map[None], plan_c.other_map[None]
    )

    r_high = r_low + TILE
    inv_11 = inverse_factors(first[r_low:r_high][None])[0]
    low_21 = product_nt(first[r_high : r_high + TILE], inv_11)
    inv_22 = inverse_factors((second[r_high : r_high + TILE] - product_nt(low_21, low_21))[None])[0]
    inv_21 = -product(inv_22, product(low_21, inv_11))
    own_first, own_second = r_edge, rfront[:, r_high : r_high + TILE]
    factor_1 = product_nt(own_first, inv_11)
    factor_2 = product_nt(own_first, inv_21) + product_nt(own_second, inv_22)
    weights_1 = product(factor_1, inv_11) + product(factor_2, inv_21)
    weights_2 = product(factor_2, inv_22)
    row_ids = me * rows + jnp.arange(rows, dtype=jnp.int32)
    above = (row_ids >= r_low) & (row_ids < r_high)
    factor_2 = jnp.where(above[:, None], 0.0, factor_2)
    rfactor = jnp.concatenate([factor_1, factor_2], 1)
    first_row = (me * rows).astype(jnp.int32).reshape(1)
    rschur = finish(r_rows, first, second, jnp.concatenate([weights_1, weights_2], 1), first_row)
    return (gfactor, cfactor, rfactor, rschur)


def solution(mesh):
    placed = (P("cube", None), P("cube", None), P("cube", None), P(), P())
    return jax.shard_map(
        local,
        mesh=mesh,
        in_specs=placed,
        out_specs=(P("cube", None), P("cube", None), P("cube", None), P("cube", None)),
        check_vma=False,
    )
```

```python
import functools

import jax
import jax.numpy as jnp
from jax import lax
from jax.experimental import pallas as pl
from jax.experimental.pallas import tpu as pltpu
from jax.sharding import PartitionSpec as P

TILE = 256
STRIP = 32
SUB = 8
LANES = 128
HIGH = lax.Precision.HIGH
HIGHEST = lax.Precision.HIGHEST
NT = (((1,), (1,)), ((), ()))
MIB = 1024 * 1024


def widen(column, width):
    return jnp.concatenate([column] * (width // LANES), 1)


def factor_strip(strip, base):
    width = strip[0].shape[1]
    sub_ids = lax.broadcasted_iota(jnp.int32, (SUB, 1), 0)
    count = len(strip)
    for p in range(count):
        first = base + p * SUB
        cols = [
            [jnp.broadcast_to(strip[q][:, first + j : first + j + 1], (SUB, LANES)) for j in range(SUB)]
            for q in range(p, count)
        ]
        for j in range(SUB):
            pivot = cols[0][j][j : j + 1, :]
            inv = lax.rsqrt(pivot)
            inv = inv * (1.5 - 0.5 * pivot * inv * inv)
            unit = strip[p][j : j + 1, :] * widen(inv, width)
            scaled = [col[j] * inv for col in cols]
            below = jnp.where(sub_ids > j, scaled[0], 0.0)
            strip[p] = jnp.where(sub_ids == j, unit, strip[p] - widen(below, width) * unit)
            for q in range(p + 1, count):
                strip[q] = strip[q] - widen(scaled[q - p], width) * unit
            for m in range(j + 1, SUB):
                head = scaled[0][m : m + 1, :]
                for q in range(p, count):
                    cols[q - p][m] = cols[q - p][m] - scaled[q - p] * head
    return jnp.concatenate(strip, 0)


def inverse_kernel(count, blocks_ref, inverse_ref, work):
    row_ids = lax.broadcasted_iota(jnp.int32, (TILE, TILE), 0)
    col_ids = lax.broadcasted_iota(jnp.int32, (TILE, TILE), 1)
    for t in range(count):
        work[t, :, :TILE] = blocks_ref[t]
        work[t, :, TILE:] = (row_ids == col_ids).astype(jnp.float32)
    for low in range(0, TILE, STRIP):
        high = low + STRIP
        left = low // LANES * LANES
        right = TILE + (high + LANES - 1) // LANES * LANES
        done = []
        for t in range(count):
            strip = [work[t, low + SUB * q : low + SUB * (q + 1), left:right] for q in range(STRIP // SUB)]
            done.append(factor_strip(strip, low - left))
        for t in range(count):
            inverse_ref[t, low:high, : right - TILE] = done[t][:, TILE - left :]
            if right < 2 * TILE:
                inverse_ref[t, low:high, right - TILE :] = jnp.zeros((STRIP, 2 * TILE - right), jnp.float32)
            if high < TILE:
                rest = high // LANES * LANES
                update = lax.dot_general(
                    done[t][:, rest - left : TILE - left],
                    done[t],
                    (((0,), (0,)), ((), ())),
                    precision=HIGHEST,
                    preferred_element_type=jnp.float32,
                )
                work[t, high:, left:right] = work[t, high:, left:right] - update[high - rest :]


def inverse_factors(blocks):
    count = blocks.shape[0]
    return pl.pallas_call(
        functools.partial(inverse_kernel, count),
        out_shape=jax.ShapeDtypeStruct(blocks.shape, jnp.float32),
        in_specs=[pl.BlockSpec(memory_space=pltpu.VMEM)],
        out_specs=pl.BlockSpec(memory_space=pltpu.VMEM),
        scratch_shapes=[pltpu.VMEM((count, TILE, 2 * TILE), jnp.float32)],
        compiler_params=pltpu.CompilerParams(vmem_limit_bytes=16 * MIB),
        cost_estimate=pl.CostEstimate(flops=30_000_000_000, bytes_accessed=1_000_000, transcendentals=0),
    )(blocks)


def halves(value):
    top = value.astype(jnp.bfloat16)
    return top, (value - top.astype(jnp.float32)).astype(jnp.bfloat16)


def dot_nt(left, right):
    return lax.dot_general(left, right, NT, preferred_element_type=jnp.float32)


def dot_nn(left, right):
    return jnp.dot(left, right, preferred_element_type=jnp.float32)


def pad_rows(value, count):
    short = count - value.shape[0]
    return value if short == 0 else jnp.concatenate([value, jnp.zeros((short, value.shape[1]), value.dtype)], 0)


def add_moved(total_ref, recv_ref, place_ref, hot):
    top, rest = halves(pad_rows(recv_ref[...], place_ref.shape[1]))
    top = dot_nt(top, hot).astype(jnp.bfloat16)
    rest = dot_nt(rest, hot).astype(jnp.bfloat16)
    total_ref[...] += dot_nn(place_ref[...], top) + dot_nn(place_ref[...], rest)


def pick_rows(total, select_ref, outs):
    keep_top_ref, keep_rest_ref, send_ref, spare_ref = outs
    rows = total.shape[0]
    sent = send_ref.shape[0]
    top, rest = halves(total)
    top = dot_nn(select_ref[...], top)
    rest = dot_nn(select_ref[...], rest)
    keep_top_ref[...] = top[:rows].astype(jnp.bfloat16)
    keep_rest_ref[...] = rest[:rows].astype(jnp.bfloat16)
    both = top[rows:] + rest[rows:]
    send_ref[...] = both[:sent]
    spare_ref[...] = both[sent:]


def update_kernel(rows_ref, panel_ref, weights_ref, select_ref, *refs):
    outs, (top_ref, rest_ref) = refs[:4], refs[4:]

    @pl.when(pl.program_id(0) == 0)
    def _():
        top_ref[...], rest_ref[...] = halves(weights_ref[...])

    panel_top, panel_rest = halves(panel_ref[...])
    top = top_ref[...]
    change = dot_nt(top, panel_top) + (dot_nt(top, panel_rest) + dot_nt(rest_ref[...], panel_top))
    pick_rows(rows_ref[...] - change, select_ref, outs)


def assemble_kernel(picks, first_block, children, flag, *refs):
    base_ref, keep_top_ref, keep_rest_ref, recv_ref, spare_ref, place_ref, place_spare_ref = refs[:7]
    keep_map_ref, recv_map_ref = refs[7:9]
    total_ref = refs[-1]
    n = pl.program_id(0)
    per = pl.num_programs(0) // 2
    block = first_block + n % per + children * (n // per)
    targets = block * TILE + lax.broadcasted_iota(jnp.int32, (TILE, TILE), 0)
    keep_hot = jnp.where(keep_map_ref[...] == targets, 1.0, 0.0).astype(jnp.bfloat16)
    recv_hot = jnp.where(recv_map_ref[...] == targets, 1.0, 0.0).astype(jnp.bfloat16)
    total_ref[...] = base_ref[...] + (dot_nt(keep_top_ref[...], keep_hot) + dot_nt(keep_rest_ref[...], keep_hot))
    add_moved(total_ref, recv_ref, place_ref, recv_hot)

    @pl.when(flag[0] != 0)
    def _():
        add_moved(total_ref, spare_ref, place_spare_ref, recv_hot)

    if picks:
        pick_rows(total_ref[...], refs[9], refs[10:14])
    else:
        refs[9][...] = total_ref[...]


def pick_shapes(rows, sent, width):
    return (
        jax.ShapeDtypeStruct((rows, width), jnp.bfloat16),
        jax.ShapeDtypeStruct((rows, width), jnp.bfloat16),
        jax.ShapeDtypeStruct((sent, width), jnp.float32),
        jax.ShapeDtypeStruct((rows - sent, width), jnp.float32),
    )


def update_and_pick(rows_mat, panel, weights, plan):
    rows, order = rows_mat.shape
    sent = plan.sent
    fixed = lambda shape: pl.BlockSpec(shape, lambda n: (0, 0))
    moving = lambda count: pl.BlockSpec((count, TILE), lambda n: (0, n))
    return pl.pallas_call(
        update_kernel,
        grid=(order // TILE,),
        out_shape=pick_shapes(rows, sent, order),
        in_specs=[
            moving(rows),
            pl.BlockSpec((TILE, TILE), lambda n: (n, 0)),
            fixed((rows, TILE)),
            fixed((2 * rows, rows)),
        ],
        out_specs=(moving(rows), moving(rows), moving(sent), moving(rows - sent)),
        scratch_shapes=[pltpu.VMEM((rows, TILE), jnp.bfloat16)] * 2,
        compiler_params=pltpu.CompilerParams(vmem_limit_bytes=48 * MIB),
        cost_estimate=pl.CostEstimate(
            flops=2 * rows * order * TILE * 8, bytes_accessed=rows * order * 16, transcendentals=0
        ),
    )(rows_mat, panel, weights, plan.select)


def assemble(base, keep, recv, spare, plan, first_block, picks=None):
    rows, order = base.shape
    sent = recv.shape[0]
    children = order // 2 // TILE
    per = recv.shape[1] // TILE
    fixed = lambda shape: pl.BlockSpec(shape, lambda n, _: (0, 0))
    child = lambda count: pl.BlockSpec((count, TILE), lambda n, _: (0, n % per))
    mapped = pl.BlockSpec((1, TILE), lambda n, _: (0, first_block + n % per))
    wide = lambda count: pl.BlockSpec((count, TILE), lambda n, _: (0, n))
    in_specs = [
        pl.BlockSpec((rows, TILE), lambda n, _: (0, first_block + n % per + children * (n // per))),
        child(rows),
        child(rows),
        child(sent),
        pl.BlockSpec((rows - sent, TILE), lambda n, flag: (0, n % per * flag[0])),
        fixed(plan.place.shape),
        fixed(plan.place_spare.shape),
        mapped,
        mapped,
    ]
    args = [base, *keep, recv, spare, plan.place, plan.place_spare, plan.own_map[None], plan.other_map[None]]
    width = 2 * per * TILE
    if picks is None:
        out_shape = jax.ShapeDtypeStruct((rows, width), jnp.float32)
        out_specs = wide(rows)
    else:
        in_specs.append(fixed((2 * rows, rows)))
        args.append(picks.select)
        out_shape = pick_shapes(rows, picks.sent, width)
        out_specs = (wide(rows), wide(rows), wide(picks.sent), wide(rows - picks.sent))
    return pl.pallas_call(
        functools.partial(assemble_kernel, picks is not None, first_block, children),
        out_shape=out_shape,
        grid_spec=pltpu.PrefetchScalarGridSpec(
            num_scalar_prefetch=1,
            grid=(2 * per,),
            in_specs=in_specs,
            out_specs=out_specs,
            scratch_shapes=[pltpu.VMEM((rows, TILE), jnp.float32)],
        ),
        compiler_params=pltpu.CompilerParams(vmem_limit_bytes=48 * MIB),
        cost_estimate=pl.CostEstimate(
            flops=2 * rows * width * TILE * 8, bytes_accessed=rows * width * 16, transcendentals=0
        ),
    )(plan.overflow, *args)


def finish_kernel(low, high, base_ref, near_ref, far_ref, first_ref, second_ref, weights_ref, out_ref, top_ref, rest_ref):
    n = pl.program_id(0)
    count = pl.num_programs(0)
    block = column_block(n, count)

    @pl.when(n == 0)
    def _():
        top_ref[...], rest_ref[...] = halves(weights_ref[...])

    rows = near_ref.shape[0]
    row_ids = base_ref[0] + lax.broadcasted_iota(jnp.int32, (rows, 1), 0)
    kept = (row_ids < low) | (row_ids >= high)
    inside = (block >= low // TILE) & (block < high // TILE)

    @pl.when(inside)
    def _():
        out_ref[...] = jnp.zeros_like(out_ref)

    @pl.when(jnp.logical_not(inside))
    def _():
        change = jnp.zeros((rows, TILE), jnp.float32)
        for k, ref in enumerate((first_ref, second_ref)):
            panel_top, panel_rest = halves(ref[...])
            top = top_ref[:, k * TILE : (k + 1) * TILE]
            rest = rest_ref[:, k * TILE : (k + 1) * TILE]
            change += dot_nt(top, panel_top) + (dot_nt(top, panel_rest) + dot_nt(rest, panel_top))
        before = jnp.where(n < count // 2, near_ref[...], far_ref[...])
        out_ref[...] = jnp.where(kept, before - change, 0.0)


def column_block(n, count):
    quarter = count // 4
    part = n // (2 * quarter)
    return n % quarter + 2 * quarter * (n // quarter % 2) + quarter * part


def finish(near, far, first, second, weights, first_row):
    rows = near.shape[0]
    order = 2 * near.shape[1]
    low, high = order - 3 * TILE, order - TILE
    count = order // TILE
    return pl.pallas_call(
        functools.partial(finish_kernel, low, high),
        out_shape=jax.ShapeDtypeStruct((rows, order), jnp.float32),
        grid_spec=pltpu.PrefetchScalarGridSpec(
            num_scalar_prefetch=1,
            grid=(count,),
            in_specs=[
                pl.BlockSpec((rows, TILE), lambda n, _: (0, jnp.minimum(n, count // 2 - 1))),
                pl.BlockSpec((rows, TILE), lambda n, _: (0, jnp.maximum(n - count // 2, 0))),
                pl.BlockSpec((TILE, TILE), lambda n, _: (column_block(n, count), 0)),
                pl.BlockSpec((TILE, TILE), lambda n, _: (column_block(n, count), 0)),
                pl.BlockSpec((rows, 2 * TILE), lambda n, _: (0, 0)),
            ],
            out_specs=pl.BlockSpec((rows, TILE), lambda n, _: (0, column_block(n, count))),
            scratch_shapes=[pltpu.VMEM((rows, 2 * TILE), jnp.bfloat16)] * 2,
        ),
        compiler_params=pltpu.CompilerParams(vmem_limit_bytes=48 * MIB),
        cost_estimate=pl.CostEstimate(
            flops=2 * rows * order * TILE * 6, bytes_accessed=rows * order * 16, transcendentals=0
        ),
    )(first_row, near, far, first, second, weights)


def product(left, right, precision=HIGHEST):
    return jnp.dot(left, right, precision=precision, preferred_element_type=jnp.float32)


def product_nt(left, right, precision=HIGHEST):
    return lax.dot_general(left, right, NT, precision=precision, preferred_element_type=jnp.float32)


def swap(value, mask):
    pairs = [(source, source ^ mask) for source in range(lax.axis_size("cube"))]
    return lax.ppermute(value, "cube", pairs)


def group_gather(value, group):
    size = lax.axis_size("cube")
    groups = [[g * group + i for i in range(group)] for g in range(size // group)]
    return lax.all_gather(value, "cube", axis=0, tiled=True, axis_index_groups=groups)


def one_hot(positions, count):
    return (positions[None, :] == jnp.arange(count, dtype=jnp.int32)[:, None]).astype(jnp.float32)


def column_targets(front_map):
    order = front_map.shape[0]
    ids = jnp.arange(order, dtype=jnp.int32)
    gone = (ids >= order - 2 * TILE) & (ids < order - TILE)
    return jnp.where(gone, -1, front_map)


def leaving(front_map, front, group, rows):
    target = (front_map // rows) // group
    return (front_map >= 0) & (target != front % 2)


class Plan:
    def __init__(self, maps, group, rows):
        me = lax.axis_index("cube")
        front = me // group
        block = me % group
        side = front % 2
        targets = jax.vmap(column_targets)(maps)
        self.sent = (rows * 19 // 32 + 7) // 8 * 8
        fronts = jnp.arange(maps.shape[0], dtype=jnp.int32)
        leaves = leaving(targets, fronts[:, None], group, rows).reshape(maps.shape[0], group, rows)
        most = jnp.max(jnp.sum(leaves.astype(jnp.int32), -1))
        self.overflow = (most > self.sent).astype(jnp.int32).reshape(1)
        self.own_map = lax.dynamic_index_in_dim(targets, front, 0, keepdims=False)
        self.other_map = lax.dynamic_index_in_dim(targets, front ^ 1, 0, keepdims=False)
        own = lax.dynamic_slice_in_dim(self.own_map, block * rows, rows, 0)
        other = lax.dynamic_slice_in_dim(self.other_map, block * rows, rows, 0)
        here = (block + group * side) * rows
        there = (block + group * (1 - side)) * rows
        self.keep = one_hot(own - here, rows)
        self.give = one_hot(own - there, rows)
        ids = jnp.arange(rows, dtype=jnp.int32)
        upper = (ids[:, None] <= ids[None, :]).astype(jnp.bfloat16)
        leaves = (own >= there) & (own < there + rows)
        comes = (other >= here) & (other < here + rows)
        flags = jnp.stack([leaves, comes]).astype(jnp.bfloat16)
        ranks = jnp.dot(flags, upper, preferred_element_type=jnp.float32).astype(jnp.int32) - 1
        send = one_hot(jnp.where(leaves, ranks[0], -1), rows)
        self.select = jnp.concatenate([self.keep, send], 0).astype(jnp.bfloat16)
        taken = one_hot(jnp.where(comes, ranks[1], -1), rows).astype(jnp.bfloat16)
        slots = one_hot(other - here, rows).astype(jnp.bfloat16)
        place = lax.dot_general(slots, taken, NT, preferred_element_type=jnp.float32).astype(jnp.bfloat16)
        fill = lambda part: jnp.pad(part, ((0, 0), (0, -part.shape[1] % 16)))
        self.place = fill(place[:, : self.sent])
        self.place_spare = fill(place[:, self.sent :])


def spread_block(block, group, owner_low, rows):
    size = lax.axis_size("cube")
    me = lax.axis_index("cube")
    holders = max(1, TILE // rows)
    has = {d for d in range(size) if owner_low <= d % group < owner_low + holders}
    inside = (me % group >= owner_low) & (me % group < owner_low + holders)
    block = jnp.where(inside, block, 0.0)
    mask = group // 2
    while mask >= holders:
        pairs = [(d, d ^ mask) for d in sorted(has)]
        block = block + lax.ppermute(block, "cube", pairs)
        has |= {d ^ mask for d in has}
        mask //= 2
    return block


def whole_block(part, rows):
    if rows >= TILE:
        return part
    return group_gather(part, TILE // rows)


def local(gfront, cfront, rfront, gmap, cmap):
    devices = lax.axis_size("cube")
    me = lax.axis_index("cube")
    quarter = devices // 4
    half = devices // 2
    rows = gfront.shape[0]
    order_g, order_c, order_r = gfront.shape[1], cfront.shape[1], rfront.shape[1]
    g_low, c_low = order_g - 2 * TILE, order_c - 2 * TILE
    r_low = order_r - 3 * TILE
    r_high = r_low + TILE

    own_g = gfront[:, g_low : g_low + TILE]
    own_c = cfront[:, c_low : c_low + TILE]
    own_second = rfront[:, r_high : r_high + TILE]
    panel_g = group_gather(own_g, quarter)
    panel_c = group_gather(own_c, half)
    second = lax.all_gather(own_second, "cube", axis=0, tiled=True)
    inverse = inverse_factors(jnp.stack([whole_block(own_g, rows), whole_block(own_c, rows)]))
    inverse_g = spread_block(inverse[0], quarter, g_low // rows, rows)
    inverse_c = spread_block(inverse[1], half, c_low // rows, rows)
    plan_g = Plan(gmap, quarter, rows)
    plan_c = Plan(cmap, half, rows)

    gfactor = product_nt(own_g, inverse_g)
    weights_g = product(gfactor, inverse_g)
    cfactor = product_nt(own_c, inverse_c)
    weights_c = product(cfactor, inverse_c)

    g_edge = gfront[:, g_low - TILE : g_low] - product_nt(weights_g, panel_g[g_low - TILE : g_low])
    edge_map = plan_g.own_map[g_low - TILE : g_low]
    g_edge = product_nt(g_edge, one_hot(edge_map - (c_low - TILE), TILE))
    c_edge = cfront[:, c_low - TILE : c_low] - product_nt(weights_c, panel_c[c_low - TILE : c_low])
    c_edge = c_edge + product(plan_g.keep, g_edge) + swap(product(plan_g.give, g_edge), quarter)
    edge_map = plan_c.own_map[c_low - TILE : c_low]
    c_edge = product_nt(c_edge, one_hot(edge_map - r_low, TILE))
    r_edge = rfront[:, r_low : r_low + TILE]
    r_edge = r_edge + product(plan_c.keep, c_edge) + swap(product(plan_c.give, c_edge), half)
    first = lax.all_gather(r_edge, "cube", axis=0, tiled=True)

    def exchange(send, spare, plan, mask):
        rest = lax.cond(plan.overflow[0] != 0, lambda part: swap(part, mask), jnp.zeros_like, spare)
        return swap(send, mask), rest

    *g_keep, send, spare = update_and_pick(gfront, panel_g, weights_g, plan_g)
    g_recv, g_spare = exchange(send, spare, plan_g, quarter)
    c_base = cfront - product_nt(weights_c, panel_c, HIGH)
    parts = []
    *c_keep, send, spare = assemble(c_base, g_keep, g_recv, g_spare, plan_g, 0, plan_c)
    for part in range(2):
        low, high = part * order_c // 2, (part + 1) * order_c // 2
        recv, rest = exchange(send[:, low:high], spare[:, low:high], plan_c, half)
        keep = [side[:, low:high] for side in c_keep]
        parts.append(assemble(rfront, keep, recv, rest, plan_c, low // TILE))

    inv_11 = inverse_factors(first[r_low:r_high][None])[0]
    low_21 = product_nt(first[r_high : r_high + TILE], inv_11)
    inv_22 = inverse_factors((second[r_high : r_high + TILE] - product_nt(low_21, low_21))[None])[0]
    inv_21 = -product(inv_22, product(low_21, inv_11))
    factor_1 = product_nt(r_edge, inv_11)
    factor_2 = product_nt(r_edge, inv_21) + product_nt(own_second, inv_22)
    weights_1 = product(factor_1, inv_11) + product(factor_2, inv_21)
    weights_2 = product(factor_2, inv_22)
    row_ids = me * rows + jnp.arange(rows, dtype=jnp.int32)
    above = (row_ids >= r_low) & (row_ids < r_high)
    factor_2 = jnp.where(above[:, None], 0.0, factor_2)
    rfactor = jnp.concatenate([factor_1, factor_2], 1)
    first_row = (me * rows).astype(jnp.int32).reshape(1)
    rschur = finish(*parts, first, second, jnp.concatenate([weights_1, weights_2], 1), first_row)
    return (gfactor, cfactor, rfactor, rschur)


def solution(mesh):
    placed = (P("cube", None), P("cube", None), P("cube", None), P(), P())
    return jax.shard_map(
        local,
        mesh=mesh,
        in_specs=placed,
        out_specs=(P("cube", None), P("cube", None), P("cube", None), P("cube", None)),
        check_vma=False,
    )
```

```python
import functools

import jax
import jax.numpy as jnp
from jax import lax
from jax.experimental import pallas as pl
from jax.experimental.pallas import tpu as pltpu
from jax.sharding import PartitionSpec as P

TILE = 256
STRIP = 32
SUB = 8
LANES = 128
HIGH = lax.Precision.HIGH
HIGHEST = lax.Precision.HIGHEST
NT = (((1,), (1,)), ((), ()))
MIB = 1024 * 1024


def widen(column, width):
    return jnp.concatenate([column] * (width // LANES), 1)


def factor_strip(strip, base):
    width = strip[0].shape[1]
    sub_ids = lax.broadcasted_iota(jnp.int32, (SUB, 1), 0)
    count = len(strip)
    for p in range(count):
        first = base + p * SUB
        cols = [
            [jnp.broadcast_to(strip[q][:, first + j : first + j + 1], (SUB, LANES)) for j in range(SUB)]
            for q in range(p, count)
        ]
        for j in range(SUB):
            pivot = cols[0][j][j : j + 1, :]
            inv = lax.rsqrt(pivot)
            inv = inv * (1.5 - 0.5 * pivot * inv * inv)
            unit = strip[p][j : j + 1, :] * widen(inv, width)
            scaled = [col[j] * inv for col in cols]
            below = jnp.where(sub_ids > j, scaled[0], 0.0)
            strip[p] = jnp.where(sub_ids == j, unit, strip[p] - widen(below, width) * unit)
            for q in range(p + 1, count):
                strip[q] = strip[q] - widen(scaled[q - p], width) * unit
            for m in range(j + 1, SUB):
                head = scaled[0][m : m + 1, :]
                for q in range(p, count):
                    cols[q - p][m] = cols[q - p][m] - scaled[q - p] * head
    return jnp.concatenate(strip, 0)


def inverse_kernel(count, blocks_ref, inverse_ref, work):
    row_ids = lax.broadcasted_iota(jnp.int32, (TILE, TILE), 0)
    col_ids = lax.broadcasted_iota(jnp.int32, (TILE, TILE), 1)
    for t in range(count):
        work[t, :, :TILE] = blocks_ref[t]
        work[t, :, TILE:] = (row_ids == col_ids).astype(jnp.float32)
    for low in range(0, TILE, STRIP):
        high = low + STRIP
        left = low // LANES * LANES
        right = TILE + (high + LANES - 1) // LANES * LANES
        done = []
        for t in range(count):
            strip = [work[t, low + SUB * q : low + SUB * (q + 1), left:right] for q in range(STRIP // SUB)]
            done.append(factor_strip(strip, low - left))
        for t in range(count):
            inverse_ref[t, low:high, : right - TILE] = done[t][:, TILE - left :]
            if right < 2 * TILE:
                inverse_ref[t, low:high, right - TILE :] = jnp.zeros((STRIP, 2 * TILE - right), jnp.float32)
            if high < TILE:
                rest = high // LANES * LANES
                update = lax.dot_general(
                    done[t][:, rest - left : TILE - left],
                    done[t],
                    (((0,), (0,)), ((), ())),
                    precision=HIGHEST,
                    preferred_element_type=jnp.float32,
                )
                work[t, high:, left:right] = work[t, high:, left:right] - update[high - rest :]


def inverse_factors(blocks):
    count = blocks.shape[0]
    return pl.pallas_call(
        functools.partial(inverse_kernel, count),
        out_shape=jax.ShapeDtypeStruct(blocks.shape, jnp.float32),
        in_specs=[pl.BlockSpec(memory_space=pltpu.VMEM)],
        out_specs=pl.BlockSpec(memory_space=pltpu.VMEM),
        scratch_shapes=[pltpu.VMEM((count, TILE, 2 * TILE), jnp.float32)],
        compiler_params=pltpu.CompilerParams(vmem_limit_bytes=16 * MIB),
        cost_estimate=pl.CostEstimate(flops=30_000_000_000, bytes_accessed=1_000_000, transcendentals=0),
    )(blocks)


def halves(value):
    top = value.astype(jnp.bfloat16)
    return top, (value - top.astype(jnp.float32)).astype(jnp.bfloat16)


def dot_nt(left, right):
    return lax.dot_general(left, right, NT, preferred_element_type=jnp.float32)


def dot_nn(left, right):
    return jnp.dot(left, right, preferred_element_type=jnp.float32)


def pad_rows(value, count):
    short = count - value.shape[0]
    return value if short == 0 else jnp.concatenate([value, jnp.zeros((short, value.shape[1]), value.dtype)], 0)


def stacked(value):
    return jnp.concatenate(halves(value), 0)


def add_moved(total_ref, recv_ref, place_ref, hot):
    count = place_ref.shape[1]
    moved = dot_nt(stacked(pad_rows(recv_ref[...], count)), hot).astype(jnp.bfloat16)
    total_ref[...] += dot_nn(place_ref[...], moved[:count]) + dot_nn(place_ref[...], moved[count:])


def pick_rows(total, select_ref, outs):
    keep_ref, send_ref, spare_ref = outs
    rows = total.shape[0]
    sent = send_ref.shape[0]
    top, rest = halves(total)
    top = dot_nn(select_ref[...], top)
    rest = dot_nn(select_ref[...], rest)
    keep_ref[:rows] = top[:rows].astype(jnp.bfloat16)
    keep_ref[rows:] = rest[:rows].astype(jnp.bfloat16)
    both = top[rows:] + rest[rows:]
    send_ref[...] = both[:sent]
    spare_ref[...] = both[sent:]


def low_rank(weights_ref, panel):
    rows = weights_ref.shape[0] // 2
    top, rest = halves(panel)
    main = dot_nt(weights_ref[...], top)
    return main[:rows] + (main[rows:] + dot_nt(weights_ref[:rows], rest))


def update_kernel(rows_ref, panel_ref, weights_ref, select_ref, keep_ref, send_ref, spare_ref, split_ref):
    @pl.when(pl.program_id(0) == 0)
    def _():
        split_ref[...] = stacked(weights_ref[...])

    total = rows_ref[...] - low_rank(split_ref, panel_ref[...])
    pick_rows(total, select_ref, (keep_ref, send_ref, spare_ref))


def assemble_kernel(picks, target, flag, *refs):
    base_ref, keep_ref, recv_ref, spare_ref, place_ref, place_spare_ref, keep_map_ref, recv_map_ref = refs[:8]
    total_ref = refs[-1]
    rows = base_ref.shape[0]
    targets = target(pl.program_id(0)) * TILE + lax.broadcasted_iota(jnp.int32, (TILE, TILE), 0)
    keep_hot = jnp.where(keep_map_ref[...] == targets, 1.0, 0.0).astype(jnp.bfloat16)
    recv_hot = jnp.where(recv_map_ref[...] == targets, 1.0, 0.0).astype(jnp.bfloat16)
    kept = dot_nt(keep_ref[...], keep_hot)
    total_ref[...] = base_ref[...] + (kept[:rows] + kept[rows:])
    add_moved(total_ref, recv_ref, place_ref, recv_hot)

    @pl.when(flag[0] != 0)
    def _():
        add_moved(total_ref, spare_ref, place_spare_ref, recv_hot)

    if picks:
        pick_rows(total_ref[...], refs[8], refs[9:12])
    else:
        refs[8][...] = total_ref[...]


def pick_shapes(rows, sent, width):
    return (
        jax.ShapeDtypeStruct((2 * rows, width), jnp.bfloat16),
        jax.ShapeDtypeStruct((sent, width), jnp.float32),
        jax.ShapeDtypeStruct((rows - sent, width), jnp.float32),
    )


def update_and_pick(rows_mat, panel, weights, plan):
    rows, order = rows_mat.shape
    sent = plan.sent
    fixed = lambda shape: pl.BlockSpec(shape, lambda n: (0, 0))
    moving = lambda count: pl.BlockSpec((count, TILE), lambda n: (0, n))
    return pl.pallas_call(
        update_kernel,
        grid=(order // TILE,),
        out_shape=pick_shapes(rows, sent, order),
        in_specs=[
            moving(rows),
            pl.BlockSpec((TILE, TILE), lambda n: (n, 0)),
            fixed((rows, TILE)),
            fixed((2 * rows, rows)),
        ],
        out_specs=(moving(2 * rows), moving(sent), moving(rows - sent)),
        scratch_shapes=[pltpu.VMEM((2 * rows, TILE), jnp.bfloat16)],
        compiler_params=pltpu.CompilerParams(vmem_limit_bytes=48 * MIB),
        cost_estimate=pl.CostEstimate(
            flops=2 * rows * order * TILE * 8, bytes_accessed=rows * order * 16, transcendentals=0
        ),
    )(rows_mat, panel, weights, plan.select)


def assemble(base, keep, recv, spare, plan, child_block, picks=None):
    rows, order = base.shape
    sent = recv.shape[0]
    children = order // 2 // TILE
    per = recv.shape[1] // TILE
    target = lambda n: child_block(n % per) + children * (n // per)
    fixed = lambda shape: pl.BlockSpec(shape, lambda n, _: (0, 0))
    child = lambda count: pl.BlockSpec((count, TILE), lambda n, _: (0, n % per))
    mapped = pl.BlockSpec((1, TILE), lambda n, _: (0, child_block(n % per)))
    wide = lambda count: pl.BlockSpec((count, TILE), lambda n, _: (0, n))
    in_specs = [
        pl.BlockSpec((rows, TILE), lambda n, _: (0, target(n))),
        child(2 * rows),
        child(sent),
        pl.BlockSpec((rows - sent, TILE), lambda n, flag: (0, n % per * flag[0])),
        fixed(plan.place.shape),
        fixed(plan.place_spare.shape),
        mapped,
        mapped,
    ]
    args = [base, keep, recv, spare, plan.place, plan.place_spare, plan.own_map[None], plan.other_map[None]]
    width = 2 * per * TILE
    if picks is None:
        out_shape = jax.ShapeDtypeStruct((rows, width), jnp.float32)
        out_specs = wide(rows)
    else:
        in_specs.append(fixed((2 * rows, rows)))
        args.append(picks.select)
        out_shape = pick_shapes(rows, picks.sent, width)
        out_specs = (wide(2 * rows), wide(picks.sent), wide(rows - picks.sent))
    return pl.pallas_call(
        functools.partial(assemble_kernel, picks is not None, target),
        out_shape=out_shape,
        grid_spec=pltpu.PrefetchScalarGridSpec(
            num_scalar_prefetch=1,
            grid=(2 * per,),
            in_specs=in_specs,
            out_specs=out_specs,
            scratch_shapes=[pltpu.VMEM((rows, TILE), jnp.float32)],
        ),
        compiler_params=pltpu.CompilerParams(vmem_limit_bytes=48 * MIB),
        cost_estimate=pl.CostEstimate(
            flops=2 * rows * width * TILE * 8, bytes_accessed=rows * width * 16, transcendentals=0
        ),
    )(plan.overflow, *args)


def finish_kernel(
    low, high, pair, where_ref, near_ref, far_ref, even_ref, odd_ref, second_ref, weights_ref, out_ref, split_ref
):
    n = pl.program_id(0)

    @pl.when(n == 0)
    def _():
        split_ref[...] = stacked(weights_ref[...])

    rows = near_ref.shape[0]
    row_ids = where_ref[0] + lax.broadcasted_iota(jnp.int32, (rows, 1), 0)
    col_ids = pair(n) * 2 * TILE + lax.broadcasted_iota(jnp.int32, (1, 2 * TILE), 1)
    outside = lambda ids: (ids < low) | (ids >= high)
    turned = where_ref[1] % 2 != 0
    even = jnp.where(turned, odd_ref[...], even_ref[...])
    odd = jnp.where(turned, even_ref[...], odd_ref[...])
    panel = jnp.concatenate([jnp.concatenate([even, odd], 0), second_ref[...]], 1)
    before = jnp.where(n < pl.num_programs(0) // 2, near_ref[...], far_ref[...])
    out_ref[...] = jnp.where(outside(row_ids) & outside(col_ids), before - low_rank(split_ref, panel), 0.0)


def finish(near, far, even, odd, turn, second, weights, first_row, pair):
    rows = near.shape[0]
    order = 2 * near.shape[1]
    low, high = order - 3 * TILE, order - TILE
    count = order // (2 * TILE)
    layers = count // 4
    wide = lambda index: pl.BlockSpec((rows, 2 * TILE), index)
    piece = pl.BlockSpec((TILE, TILE), lambda n, s: (place_of((2 * pair(n)) ^ s[1], layers), 0))
    return pl.pallas_call(
        functools.partial(finish_kernel, low, high, pair),
        out_shape=jax.ShapeDtypeStruct((rows, order), jnp.float32),
        grid_spec=pltpu.PrefetchScalarGridSpec(
            num_scalar_prefetch=1,
            grid=(count,),
            in_specs=[
                wide(lambda n, _: (0, jnp.minimum(n, count // 2 - 1))),
                wide(lambda n, _: (0, jnp.maximum(n - count // 2, 0))),
                piece,
                piece,
                pl.BlockSpec((2 * TILE, TILE), lambda n, _: (pair(n), 0)),
                wide(lambda n, _: (0, 0)),
            ],
            out_specs=wide(lambda n, _: (0, pair(n))),
            scratch_shapes=[pltpu.VMEM((2 * rows, 2 * TILE), jnp.bfloat16)],
        ),
        compiler_params=pltpu.CompilerParams(vmem_limit_bytes=48 * MIB),
        cost_estimate=pl.CostEstimate(
            flops=2 * rows * order * TILE * 6, bytes_accessed=rows * order * 16, transcendentals=0
        ),
    )(jnp.stack([first_row, turn]).astype(jnp.int32), near, far, even, odd, second, weights)


def product(left, right, precision=HIGHEST):
    return jnp.dot(left, right, precision=precision, preferred_element_type=jnp.float32)


def product_nt(left, right, precision=HIGHEST):
    return lax.dot_general(left, right, NT, precision=precision, preferred_element_type=jnp.float32)


def swap(value, mask):
    pairs = [(source, source ^ mask) for source in range(lax.axis_size("cube"))]
    return lax.ppermute(value, "cube", pairs)


def group_gather(value, group):
    size = lax.axis_size("cube")
    groups = [[g * group + i for i in range(group)] for g in range(size // group)]
    return lax.all_gather(value, "cube", axis=0, tiled=True, axis_index_groups=groups)


def one_hot(positions, count):
    return (positions[None, :] == jnp.arange(count, dtype=jnp.int32)[:, None]).astype(jnp.float32)


def column_targets(front_map):
    order = front_map.shape[0]
    ids = jnp.arange(order, dtype=jnp.int32)
    gone = (ids >= order - 2 * TILE) & (ids < order - TILE)
    return jnp.where(gone, -1, front_map)


def leaving(front_map, front, group, rows):
    target = (front_map // rows) // group
    return (front_map >= 0) & (target != front % 2)


class Plan:
    def __init__(self, maps, group, rows):
        me = lax.axis_index("cube")
        front = me // group
        block = me % group
        side = front % 2
        targets = jax.vmap(column_targets)(maps)
        self.sent = (rows * 19 // 32 + 7) // 8 * 8
        fronts = jnp.arange(maps.shape[0], dtype=jnp.int32)
        leaves = leaving(targets, fronts[:, None], group, rows).reshape(maps.shape[0], group, rows)
        most = jnp.max(jnp.sum(leaves.astype(jnp.int32), -1))
        self.overflow = (most > self.sent).astype(jnp.int32).reshape(1)
        self.own_map = lax.dynamic_index_in_dim(targets, front, 0, keepdims=False)
        self.other_map = lax.dynamic_index_in_dim(targets, front ^ 1, 0, keepdims=False)
        own = lax.dynamic_slice_in_dim(self.own_map, block * rows, rows, 0)
        other = lax.dynamic_slice_in_dim(self.other_map, block * rows, rows, 0)
        here = (block + group * side) * rows
        there = (block + group * (1 - side)) * rows
        self.keep = one_hot(own - here, rows)
        self.give = one_hot(own - there, rows)
        ids = jnp.arange(rows, dtype=jnp.int32)
        upper = (ids[:, None] <= ids[None, :]).astype(jnp.bfloat16)
        leaves = (own >= there) & (own < there + rows)
        comes = (other >= here) & (other < here + rows)
        flags = jnp.stack([leaves, comes]).astype(jnp.bfloat16)
        ranks = jnp.dot(flags, upper, preferred_element_type=jnp.float32).astype(jnp.int32) - 1
        send = one_hot(jnp.where(leaves, ranks[0], -1), rows)
        self.select = jnp.concatenate([self.keep, send], 0).astype(jnp.bfloat16)
        taken = one_hot(jnp.where(comes, ranks[1], -1), rows).astype(jnp.bfloat16)
        slots = one_hot(other - here, rows).astype(jnp.bfloat16)
        place = lax.dot_general(slots, taken, NT, preferred_element_type=jnp.float32).astype(jnp.bfloat16)
        fill = lambda part: jnp.pad(part, ((0, 0), (0, -part.shape[1] % 16)))
        self.place = fill(place[:, : self.sent])
        self.place_spare = fill(place[:, self.sent :])


def spread_block(block, group, owner_low, rows):
    size = lax.axis_size("cube")
    me = lax.axis_index("cube")
    holders = max(1, TILE // rows)
    has = {d for d in range(size) if owner_low <= d % group < owner_low + holders}
    inside = (me % group >= owner_low) & (me % group < owner_low + holders)
    block = jnp.where(inside, block, 0.0)
    mask = group // 2
    while mask >= holders:
        pairs = [(d, d ^ mask) for d in sorted(has)]
        block = block + lax.ppermute(block, "cube", pairs)
        has |= {d ^ mask for d in has}
        mask //= 2
    return block


def whole_block(part, rows):
    if rows >= TILE:
        return part
    return group_gather(part, TILE // rows)


def place_of(turned, layers):
    span = layers // 2
    layer, y, x = turned // 8, turned // 4 % 2, turned // 2 % 2
    lower = (2 * y + x) * span + layer
    upper = (4 + 2 * x + y) * span + layer - span
    return jnp.where(layer < span, lower, upper)


def gather_first(block):
    size = lax.axis_size("cube")
    layers = size // 8
    rows = block.shape[0]
    if rows != TILE:
        whole = lax.all_gather(block, "cube", axis=0, tiled=True)
        order = whole.shape[0]
        layers = order // TILE // 8
        spots = [0] * (4 * layers)
        for m in range(4 * layers):
            layer, y, x = m // 4, m // 2 % 2, m % 2
            span = layers // 2
            spot = (2 * y + x) * span + layer if layer < span else (4 + 2 * x + y) * span + layer - span
            spots[spot] = m
        blocks = whole.reshape(order // TILE, TILE, TILE)
        sides = [jnp.concatenate([blocks[2 * m + side] for m in spots], 0) for side in range(2)]
        return sides, lambda low: whole[low : low + TILE], jnp.int32(0)
    me = lax.axis_index("cube")
    stack = [block] + [swap(block, 8 * layer) for layer in range(1, layers)]
    one = jnp.concatenate(stack[: layers // 2], 0)
    two = jnp.concatenate(stack[layers // 2 :], 0)
    one = jnp.concatenate([one, swap(one, 2)], 0)
    two = jnp.concatenate([two, swap(two, 4)], 0)
    even = jnp.concatenate([one, swap(one, 4), two, swap(two, 2)], 0)
    odd = swap(even, 1)

    def read(low):
        turned = (low // TILE) ^ me
        start = place_of(turned, layers) * TILE
        sides = [lax.dynamic_slice_in_dim(side, start, TILE, 0) for side in (even, odd)]
        return jnp.where(turned % 2 == 0, sides[0], sides[1])

    return (even, odd), read, me


def local(gfront, cfront, rfront, gmap, cmap):
    devices = lax.axis_size("cube")
    me = lax.axis_index("cube")
    quarter = devices // 4
    half = devices // 2
    rows = gfront.shape[0]
    order_g, order_c, order_r = gfront.shape[1], cfront.shape[1], rfront.shape[1]
    g_low, c_low = order_g - 2 * TILE, order_c - 2 * TILE
    r_low = order_r - 3 * TILE
    r_high = r_low + TILE

    own_g = gfront[:, g_low : g_low + TILE]
    own_c = cfront[:, c_low : c_low + TILE]
    own_second = rfront[:, r_high : r_high + TILE]
    panel_g = group_gather(own_g, quarter)
    panel_c = group_gather(own_c, half)
    second = lax.all_gather(own_second, "cube", axis=0, tiled=True)
    inverse = inverse_factors(jnp.stack([whole_block(own_g, rows), whole_block(own_c, rows)]))
    inverse_g = spread_block(inverse[0], quarter, g_low // rows, rows)
    inverse_c = spread_block(inverse[1], half, c_low // rows, rows)
    plan_g = Plan(gmap, quarter, rows)
    plan_c = Plan(cmap, half, rows)

    gfactor = product_nt(own_g, inverse_g)
    weights_g = product(gfactor, inverse_g)
    cfactor = product_nt(own_c, inverse_c)
    weights_c = product(cfactor, inverse_c)

    g_keep, g_send, g_spare = update_and_pick(gfront, panel_g, weights_g, plan_g)
    panel_c, g_send = lax.optimization_barrier((panel_c, g_send))

    g_edge = gfront[:, g_low - TILE : g_low] - product_nt(weights_g, panel_g[g_low - TILE : g_low])
    edge_map = plan_g.own_map[g_low - TILE : g_low]
    g_edge = product_nt(g_edge, one_hot(edge_map - (c_low - TILE), TILE))
    c_edge = cfront[:, c_low - TILE : c_low] - product_nt(weights_c, panel_c[c_low - TILE : c_low])
    c_edge = c_edge + product(plan_g.keep, g_edge) + swap(product(plan_g.give, g_edge), quarter)
    edge_map = plan_c.own_map[c_low - TILE : c_low]
    c_edge = product_nt(c_edge, one_hot(edge_map - r_low, TILE))
    r_edge = rfront[:, r_low : r_low + TILE]
    r_edge = r_edge + product(plan_c.keep, c_edge) + swap(product(plan_c.give, c_edge), half)
    def exchange(send, spare, plan, mask):
        rest = lax.cond(plan.overflow[0] != 0, lambda part: swap(part, mask), jnp.zeros_like, spare)
        return swap(send, mask), rest

    g_recv, g_rest = exchange(g_send, g_spare, plan_g, quarter)
    c_base = cfront - product_nt(weights_c, panel_c, HIGH)
    blocks_g = order_g // TILE
    per = blocks_g // 2
    child_of_c = lambda part: lambda p: part * per + p
    child_of_r = lambda part: lambda p: part * per + p % per + blocks_g * (p // per)
    pieces = []
    for part in range(2):
        low, high = part * per * TILE, (part + 1) * per * TILE
        g_part = [value[:, low:high] for value in (g_keep, g_recv, g_rest)]
        keep, send, spare = assemble(c_base, *g_part, plan_g, child_of_c(part), plan_c)
        pieces.append((keep, *exchange(send, spare, plan_c, half)))
    first, at_first, turn = gather_first(r_edge)
    parts = []
    for part in range(2):
        if part == 0:
            plan_c.place, second = lax.optimization_barrier((plan_c.place, second))
        parts.append(assemble(rfront, *pieces[part], plan_c, child_of_r(part)))

    inv_11 = inverse_factors(at_first(r_low)[None])[0]
    low_21 = product_nt(at_first(r_high), inv_11)
    inv_22 = inverse_factors((second[r_high : r_high + TILE] - product_nt(low_21, low_21))[None])[0]
    inv_21 = -product(inv_22, product(low_21, inv_11))
    factor_1 = product_nt(r_edge, inv_11)
    factor_2 = product_nt(r_edge, inv_21) + product_nt(own_second, inv_22)
    weights_1 = product(factor_1, inv_11) + product(factor_2, inv_21)
    weights_2 = product(factor_2, inv_22)
    row_ids = me * rows + jnp.arange(rows, dtype=jnp.int32)
    above = (row_ids >= r_low) & (row_ids < r_high)
    factor_2 = jnp.where(above[:, None], 0.0, factor_2)
    rfactor = jnp.concatenate([factor_1, factor_2], 1)
    pairs = per // 2

    def pair(n):
        m = n % (4 * pairs)
        return m % pairs + 2 * pairs * (m // pairs) + pairs * (n // (4 * pairs))

    rschur = finish(*parts, *first, turn, second, jnp.concatenate([weights_1, weights_2], 1), me * rows, pair)
    return (gfactor, cfactor, rfactor, rschur)


def solution(mesh):
    placed = (P("cube", None), P("cube", None), P("cube", None), P(), P())
    return jax.shard_map(
        local,
        mesh=mesh,
        in_specs=placed,
        out_specs=(P("cube", None), P("cube", None), P("cube", None), P("cube", None)),
        check_vma=False,
    )
```

```python
import functools

import jax
import jax.numpy as jnp
from jax import lax
from jax.experimental import pallas as pl
from jax.experimental.pallas import tpu as pltpu
from jax.sharding import PartitionSpec as P

TILE = 256
STRIP = 32
SUB = 8
LANES = 128
HIGH = lax.Precision.HIGH
HIGHEST = lax.Precision.HIGHEST
NT = (((1,), (1,)), ((), ()))
MIB = 1024 * 1024


def widen(column, width):
    return jnp.concatenate([column] * (width // LANES), 1)


def factor_strip(strip, base):
    width = strip[0].shape[1]
    sub_ids = lax.broadcasted_iota(jnp.int32, (SUB, 1), 0)
    count = len(strip)
    for p in range(count):
        first = base + p * SUB
        cols = [
            [jnp.broadcast_to(strip[q][:, first + j : first + j + 1], (SUB, LANES)) for j in range(SUB)]
            for q in range(p, count)
        ]
        for j in range(SUB):
            pivot = cols[0][j][j : j + 1, :]
            inv = lax.rsqrt(pivot)
            inv = inv * (1.5 - 0.5 * pivot * inv * inv)
            unit = strip[p][j : j + 1, :] * widen(inv, width)
            scaled = [col[j] * inv for col in cols]
            below = jnp.where(sub_ids > j, scaled[0], 0.0)
            strip[p] = jnp.where(sub_ids == j, unit, strip[p] - widen(below, width) * unit)
            for q in range(p + 1, count):
                strip[q] = strip[q] - widen(scaled[q - p], width) * unit
            for m in range(j + 1, SUB):
                head = scaled[0][m : m + 1, :]
                for q in range(p, count):
                    cols[q - p][m] = cols[q - p][m] - scaled[q - p] * head
    return jnp.concatenate(strip, 0)


def inverse_kernel(count, blocks_ref, inverse_ref, work):
    row_ids = lax.broadcasted_iota(jnp.int32, (TILE, TILE), 0)
    col_ids = lax.broadcasted_iota(jnp.int32, (TILE, TILE), 1)
    for t in range(count):
        work[t, :, :TILE] = blocks_ref[t]
        work[t, :, TILE:] = (row_ids == col_ids).astype(jnp.float32)
    for low in range(0, TILE, STRIP):
        high = low + STRIP
        left = low // LANES * LANES
        right = TILE + (high + LANES - 1) // LANES * LANES
        done = []
        for t in range(count):
            strip = [work[t, low + SUB * q : low + SUB * (q + 1), left:right] for q in range(STRIP // SUB)]
            done.append(factor_strip(strip, low - left))
        for t in range(count):
            inverse_ref[t, low:high, : right - TILE] = done[t][:, TILE - left :]
            if right < 2 * TILE:
                inverse_ref[t, low:high, right - TILE :] = jnp.zeros((STRIP, 2 * TILE - right), jnp.float32)
            if high < TILE:
                rest = high // LANES * LANES
                update = lax.dot_general(
                    done[t][:, rest - left : TILE - left],
                    done[t],
                    (((0,), (0,)), ((), ())),
                    precision=HIGHEST,
                    preferred_element_type=jnp.float32,
                )
                work[t, high:, left:right] = work[t, high:, left:right] - update[high - rest :]


def inverse_factors(blocks):
    count = blocks.shape[0]
    return pl.pallas_call(
        functools.partial(inverse_kernel, count),
        out_shape=jax.ShapeDtypeStruct(blocks.shape, jnp.float32),
        in_specs=[pl.BlockSpec(memory_space=pltpu.VMEM)],
        out_specs=pl.BlockSpec(memory_space=pltpu.VMEM),
        scratch_shapes=[pltpu.VMEM((count, TILE, 2 * TILE), jnp.float32)],
        compiler_params=pltpu.CompilerParams(vmem_limit_bytes=16 * MIB),
        cost_estimate=pl.CostEstimate(flops=30_000_000_000, bytes_accessed=1_000_000, transcendentals=0),
    )(blocks)


def halves(value):
    top = value.astype(jnp.bfloat16)
    return top, (value - top.astype(jnp.float32)).astype(jnp.bfloat16)


def dot_nt(left, right):
    return lax.dot_general(left, right, NT, preferred_element_type=jnp.float32)


def dot_nn(left, right):
    return jnp.dot(left, right, preferred_element_type=jnp.float32)


def pad_rows(value, count):
    short = count - value.shape[0]
    return value if short == 0 else jnp.concatenate([value, jnp.zeros((short, value.shape[1]), value.dtype)], 0)


def stacked(value):
    return jnp.concatenate(halves(value), 0)


def add_moved(total_ref, recv_ref, place_ref, hot):
    count = place_ref.shape[1]
    moved = dot_nt(stacked(pad_rows(recv_ref[...], count)), hot).astype(jnp.bfloat16)
    total_ref[...] += dot_nn(place_ref[...], moved[:count]) + dot_nn(place_ref[...], moved[count:])


def pick_rows(total, select_ref, outs):
    keep_ref, send_ref, spare_ref = outs
    rows = total.shape[0]
    sent = send_ref.shape[0]
    top, rest = halves(total)
    top = dot_nn(select_ref[...], top)
    rest = dot_nn(select_ref[...], rest)
    keep_ref[:rows] = top[:rows].astype(jnp.bfloat16)
    keep_ref[rows:] = rest[:rows].astype(jnp.bfloat16)
    both = top[rows:] + rest[rows:]
    send_ref[...] = both[:sent]
    spare_ref[...] = both[sent:]


def low_rank(weights_ref, panel):
    rows = weights_ref.shape[0] // 2
    top, rest = halves(panel)
    main = dot_nt(weights_ref[...], top)
    return main[:rows] + (main[rows:] + dot_nt(weights_ref[:rows], rest))


def update_kernel(rows_ref, panel_ref, weights_ref, select_ref, keep_ref, send_ref, spare_ref, split_ref):
    @pl.when(pl.program_id(0) == 0)
    def _():
        split_ref[...] = stacked(weights_ref[...])

    total = rows_ref[...] - low_rank(split_ref, panel_ref[...])
    pick_rows(total, select_ref, (keep_ref, send_ref, spare_ref))


def assemble_kernel(picks, target, flag, *refs):
    base_ref, keep_ref, recv_ref, spare_ref, place_ref, place_spare_ref, keep_map_ref, recv_map_ref = refs[:8]
    total_ref = refs[-1]
    rows = base_ref.shape[0]
    targets = target(pl.program_id(0)) * TILE + lax.broadcasted_iota(jnp.int32, (TILE, TILE), 0)
    keep_hot = jnp.where(keep_map_ref[...] == targets, 1.0, 0.0).astype(jnp.bfloat16)
    recv_hot = jnp.where(recv_map_ref[...] == targets, 1.0, 0.0).astype(jnp.bfloat16)
    kept = dot_nt(keep_ref[...], keep_hot)
    total_ref[...] = base_ref[...] + (kept[:rows] + kept[rows:])
    add_moved(total_ref, recv_ref, place_ref, recv_hot)

    @pl.when(flag[0] != 0)
    def _():
        add_moved(total_ref, spare_ref, place_spare_ref, recv_hot)

    if picks:
        pick_rows(total_ref[...], refs[8], refs[9:12])
    else:
        refs[8][...] = total_ref[...]


def pick_shapes(rows, sent, width):
    return (
        jax.ShapeDtypeStruct((2 * rows, width), jnp.bfloat16),
        jax.ShapeDtypeStruct((sent, width), jnp.float32),
        jax.ShapeDtypeStruct((rows - sent, width), jnp.float32),
    )


def update_and_pick(rows_mat, panel, weights, plan):
    rows, order = rows_mat.shape
    sent = plan.sent
    fixed = lambda shape: pl.BlockSpec(shape, lambda n: (0, 0))
    moving = lambda count: pl.BlockSpec((count, TILE), lambda n: (0, n))
    return pl.pallas_call(
        update_kernel,
        grid=(order // TILE,),
        out_shape=pick_shapes(rows, sent, order),
        in_specs=[
            moving(rows),
            pl.BlockSpec((TILE, TILE), lambda n: (n, 0)),
            fixed((rows, TILE)),
            fixed((2 * rows, rows)),
        ],
        out_specs=(moving(2 * rows), moving(sent), moving(rows - sent)),
        scratch_shapes=[pltpu.VMEM((2 * rows, TILE), jnp.bfloat16)],
        compiler_params=pltpu.CompilerParams(vmem_limit_bytes=48 * MIB),
        cost_estimate=pl.CostEstimate(
            flops=2 * rows * order * TILE * 8, bytes_accessed=rows * order * 16, transcendentals=0
        ),
    )(rows_mat, panel, weights, plan.select)


def assemble(base, keep, recv, spare, plan, child_block, picks=None):
    rows, order = base.shape
    sent = recv.shape[0]
    children = order // 2 // TILE
    per = recv.shape[1] // TILE
    target = lambda n: child_block(n % per) + children * (n // per)
    fixed = lambda shape: pl.BlockSpec(shape, lambda n, _: (0, 0))
    child = lambda count: pl.BlockSpec((count, TILE), lambda n, _: (0, n % per))
    mapped = pl.BlockSpec((1, TILE), lambda n, _: (0, child_block(n % per)))
    wide = lambda count: pl.BlockSpec((count, TILE), lambda n, _: (0, n))
    in_specs = [
        pl.BlockSpec((rows, TILE), lambda n, _: (0, target(n))),
        child(2 * rows),
        child(sent),
        pl.BlockSpec((rows - sent, TILE), lambda n, flag: (0, n % per * flag[0])),
        fixed(plan.place.shape),
        fixed(plan.place_spare.shape),
        mapped,
        mapped,
    ]
    args = [base, keep, recv, spare, plan.place, plan.place_spare, plan.own_map[None], plan.other_map[None]]
    width = 2 * per * TILE
    if picks is None:
        out_shape = jax.ShapeDtypeStruct((rows, width), jnp.float32)
        out_specs = wide(rows)
    else:
        in_specs.append(fixed((2 * rows, rows)))
        args.append(picks.select)
        out_shape = pick_shapes(rows, picks.sent, width)
        out_specs = (wide(2 * rows), wide(picks.sent), wide(rows - picks.sent))
    return pl.pallas_call(
        functools.partial(assemble_kernel, picks is not None, target),
        out_shape=out_shape,
        grid_spec=pltpu.PrefetchScalarGridSpec(
            num_scalar_prefetch=1,
            grid=(2 * per,),
            in_specs=in_specs,
            out_specs=out_specs,
            scratch_shapes=[pltpu.VMEM((rows, TILE), jnp.float32)],
        ),
        compiler_params=pltpu.CompilerParams(vmem_limit_bytes=48 * MIB),
        cost_estimate=pl.CostEstimate(
            flops=2 * rows * width * TILE * 8, bytes_accessed=rows * width * 16, transcendentals=0
        ),
    )(plan.overflow, *args)


def finish_kernel(
    low, high, pair, where_ref, near_ref, far_ref, even_ref, odd_ref, second_ref, weights_ref, out_ref, split_ref
):
    n = pl.program_id(0)

    @pl.when(n == 0)
    def _():
        split_ref[...] = stacked(weights_ref[...])

    rows = near_ref.shape[0]
    row_ids = where_ref[0] + lax.broadcasted_iota(jnp.int32, (rows, 1), 0)
    col_ids = pair(n) * 2 * TILE + lax.broadcasted_iota(jnp.int32, (1, 2 * TILE), 1)
    outside = lambda ids: (ids < low) | (ids >= high)
    turned = where_ref[1] % 2 != 0
    even = jnp.where(turned, odd_ref[...], even_ref[...])
    odd = jnp.where(turned, even_ref[...], odd_ref[...])
    panel = jnp.concatenate([jnp.concatenate([even, odd], 0), second_ref[...]], 1)
    before = jnp.where(n < pl.num_programs(0) // 2, near_ref[...], far_ref[...])
    out_ref[...] = jnp.where(outside(row_ids) & outside(col_ids), before - low_rank(split_ref, panel), 0.0)


def finish(near, far, even, odd, turn, second, weights, first_row, pair):
    rows = near.shape[0]
    order = 2 * near.shape[1]
    low, high = order - 3 * TILE, order - TILE
    count = order // (2 * TILE)
    layers = count // 4
    wide = lambda index: pl.BlockSpec((rows, 2 * TILE), index)
    piece = pl.BlockSpec((TILE, TILE), lambda n, s: (place_of((2 * pair(n)) ^ s[1], layers), 0))
    return pl.pallas_call(
        functools.partial(finish_kernel, low, high, pair),
        out_shape=jax.ShapeDtypeStruct((rows, order), jnp.float32),
        grid_spec=pltpu.PrefetchScalarGridSpec(
            num_scalar_prefetch=1,
            grid=(count,),
            in_specs=[
                wide(lambda n, _: (0, jnp.minimum(n, count // 2 - 1))),
                wide(lambda n, _: (0, jnp.maximum(n - count // 2, 0))),
                piece,
                piece,
                pl.BlockSpec((2 * TILE, TILE), lambda n, _: (pair(n), 0)),
                wide(lambda n, _: (0, 0)),
            ],
            out_specs=wide(lambda n, _: (0, pair(n))),
            scratch_shapes=[pltpu.VMEM((2 * rows, 2 * TILE), jnp.bfloat16)],
        ),
        compiler_params=pltpu.CompilerParams(vmem_limit_bytes=48 * MIB),
        cost_estimate=pl.CostEstimate(
            flops=2 * rows * order * TILE * 6, bytes_accessed=rows * order * 16, transcendentals=0
        ),
    )(jnp.stack([first_row, turn]).astype(jnp.int32), near, far, even, odd, second, weights)


def product(left, right, precision=HIGHEST):
    return jnp.dot(left, right, precision=precision, preferred_element_type=jnp.float32)


def product_nt(left, right, precision=HIGHEST):
    return lax.dot_general(left, right, NT, precision=precision, preferred_element_type=jnp.float32)


def swap(value, mask):
    pairs = [(source, source ^ mask) for source in range(lax.axis_size("cube"))]
    return lax.ppermute(value, "cube", pairs)


def group_gather(value, group):
    size = lax.axis_size("cube")
    groups = [[g * group + i for i in range(group)] for g in range(size // group)]
    return lax.all_gather(value, "cube", axis=0, tiled=True, axis_index_groups=groups)


def one_hot(positions, count):
    return (positions[None, :] == jnp.arange(count, dtype=jnp.int32)[:, None]).astype(jnp.float32)


def column_targets(front_map):
    order = front_map.shape[0]
    ids = jnp.arange(order, dtype=jnp.int32)
    gone = (ids >= order - 2 * TILE) & (ids < order - TILE)
    return jnp.where(gone, -1, front_map)


def leaving(front_map, front, group, rows):
    target = (front_map // rows) // group
    return (front_map >= 0) & (target != front % 2)


class Plan:
    def __init__(self, maps, group, rows):
        me = lax.axis_index("cube")
        front = me // group
        block = me % group
        side = front % 2
        targets = jax.vmap(column_targets)(maps)
        self.sent = (rows * 19 // 32 + 7) // 8 * 8
        fronts = jnp.arange(maps.shape[0], dtype=jnp.int32)
        leaves = leaving(targets, fronts[:, None], group, rows).reshape(maps.shape[0], group, rows)
        most = jnp.max(jnp.sum(leaves.astype(jnp.int32), -1))
        self.overflow = (most > self.sent).astype(jnp.int32).reshape(1)
        self.own_map = lax.dynamic_index_in_dim(targets, front, 0, keepdims=False)
        self.other_map = lax.dynamic_index_in_dim(targets, front ^ 1, 0, keepdims=False)
        own = lax.dynamic_slice_in_dim(self.own_map, block * rows, rows, 0)
        other = lax.dynamic_slice_in_dim(self.other_map, block * rows, rows, 0)
        here = (block + group * side) * rows
        there = (block + group * (1 - side)) * rows
        self.keep = one_hot(own - here, rows)
        self.give = one_hot(own - there, rows)
        ids = jnp.arange(rows, dtype=jnp.int32)
        upper = (ids[:, None] <= ids[None, :]).astype(jnp.bfloat16)
        leaves = (own >= there) & (own < there + rows)
        comes = (other >= here) & (other < here + rows)
        flags = jnp.stack([leaves, comes]).astype(jnp.bfloat16)
        ranks = jnp.dot(flags, upper, preferred_element_type=jnp.float32).astype(jnp.int32) - 1
        send = one_hot(jnp.where(leaves, ranks[0], -1), rows)
        self.select = jnp.concatenate([self.keep, send], 0).astype(jnp.bfloat16)
        taken = one_hot(jnp.where(comes, ranks[1], -1), rows).astype(jnp.bfloat16)
        slots = one_hot(other - here, rows).astype(jnp.bfloat16)
        place = lax.dot_general(slots, taken, NT, preferred_element_type=jnp.float32).astype(jnp.bfloat16)
        fill = lambda part: jnp.pad(part, ((0, 0), (0, -part.shape[1] % 16)))
        self.place = fill(place[:, : self.sent])
        self.place_spare = fill(place[:, self.sent :])


def spread_block(block, group, owner_low, rows):
    size = lax.axis_size("cube")
    me = lax.axis_index("cube")
    holders = max(1, TILE // rows)
    has = {d for d in range(size) if owner_low <= d % group < owner_low + holders}
    inside = (me % group >= owner_low) & (me % group < owner_low + holders)
    block = jnp.where(inside, block, 0.0)
    mask = group // 2
    while mask >= holders:
        pairs = [(d, d ^ mask) for d in sorted(has)]
        block = block + lax.ppermute(block, "cube", pairs)
        has |= {d ^ mask for d in has}
        mask //= 2
    return block


def whole_block(part, rows):
    if rows >= TILE:
        return part
    return group_gather(part, TILE // rows)


def place_of(turned, layers):
    span = layers // 2
    layer, y, x = turned // 8, turned // 4 % 2, turned // 2 % 2
    lower = (2 * y + x) * span + layer
    upper = (4 + 2 * x + y) * span + layer - span
    return jnp.where(layer < span, lower, upper)


def gather_first(block, after):
    size = lax.axis_size("cube")
    layers = size // 8
    rows = block.shape[0]
    if rows != TILE:
        whole = lax.all_gather(block, "cube", axis=0, tiled=True)
        order = whole.shape[0]
        layers = order // TILE // 8
        spots = [0] * (4 * layers)
        for m in range(4 * layers):
            layer, y, x = m // 4, m // 2 % 2, m % 2
            span = layers // 2
            spot = (2 * y + x) * span + layer if layer < span else (4 + 2 * x + y) * span + layer - span
            spots[spot] = m
        blocks = whole.reshape(order // TILE, TILE, TILE)
        sides = [jnp.concatenate([blocks[2 * m + side] for m in spots], 0) for side in range(2)]
        return sides, jnp.int32(0)
    me = lax.axis_index("cube")
    stack = [block] + [swap(block, 8 * layer) for layer in range(1, layers)]
    stack, after = lax.optimization_barrier((stack, after))
    one = jnp.concatenate(stack[: layers // 2], 0)
    two = jnp.concatenate(stack[layers // 2 :], 0)
    one = jnp.concatenate([one, swap(one, 2)], 0)
    two = jnp.concatenate([two, swap(two, 4)], 0)
    even = jnp.concatenate([one, swap(one, 4), two, swap(two, 2)], 0)
    odd = swap(even, 1)
    return (even, odd), me


def local(gfront, cfront, rfront, gmap, cmap):
    devices = lax.axis_size("cube")
    me = lax.axis_index("cube")
    quarter = devices // 4
    half = devices // 2
    rows = gfront.shape[0]
    order_g, order_c, order_r = gfront.shape[1], cfront.shape[1], rfront.shape[1]
    g_low, c_low = order_g - 2 * TILE, order_c - 2 * TILE
    r_low = order_r - 3 * TILE
    r_high = r_low + TILE

    def exchange(send, spare, plan, mask):
        rest = lax.cond(plan.overflow[0] != 0, lambda part: swap(part, mask), jnp.zeros_like, spare)
        return swap(send, mask), rest

    own_g = gfront[:, g_low : g_low + TILE]
    own_c = cfront[:, c_low : c_low + TILE]
    own_second = rfront[:, r_high : r_high + TILE]
    panel_g = group_gather(own_g, quarter)
    panel_c = group_gather(own_c, half)
    second = lax.all_gather(own_second, "cube", axis=0, tiled=True)
    inverse = inverse_factors(jnp.stack([whole_block(own_g, rows), whole_block(own_c, rows)]))
    inverse_g = spread_block(inverse[0], quarter, g_low // rows, rows)
    inverse_c = spread_block(inverse[1], half, c_low // rows, rows)
    root_2 = jnp.stack([whole_block(rfront[:, low : low + TILE], rows) for low in (r_low, r_high)])
    root_2 = spread_block(root_2, devices, r_high // rows, rows)
    plan_g = Plan(gmap, quarter, rows)
    plan_c = Plan(cmap, half, rows)

    gfactor = product_nt(own_g, inverse_g)
    weights_g = product(gfactor, inverse_g)
    cfactor = product_nt(own_c, inverse_c)
    weights_c = product(cfactor, inverse_c)

    g_keep, g_send, g_spare = update_and_pick(gfront, panel_g, weights_g, plan_g)
    panel_c, g_send = lax.optimization_barrier((panel_c, g_send))

    g_edge = gfront[:, g_low - TILE : g_low] - product_nt(weights_g, panel_g[g_low - TILE : g_low])
    edge_map = plan_g.own_map[g_low - TILE : g_low]
    g_edge = product_nt(g_edge, one_hot(edge_map - (c_low - TILE), TILE))
    c_edge = cfront[:, c_low - TILE : c_low] - product_nt(weights_c, panel_c[c_low - TILE : c_low])
    c_edge = c_edge + product(plan_g.keep, g_edge) + swap(product(plan_g.give, g_edge), quarter)
    g_recv, g_rest = exchange(g_send, g_spare, plan_g, quarter)
    c_edge, g_recv, root_2 = lax.optimization_barrier((c_edge, g_recv, root_2))
    edge_map = plan_c.own_map[c_low - TILE : c_low]
    c_edge = product_nt(c_edge, one_hot(edge_map - r_low, TILE))
    r_edge = rfront[:, r_low : r_low + TILE]
    r_edge = r_edge + product(plan_c.keep, c_edge) + swap(product(plan_c.give, c_edge), half)
    c_base = cfront - product_nt(weights_c, panel_c, HIGH)
    blocks_g = order_g // TILE
    per = blocks_g // 2
    child_of_c = lambda part: lambda p: part * per + p
    child_of_r = lambda part: lambda p: part * per + p % per + blocks_g * (p // per)
    pieces = []
    for part in range(2):
        low, high = part * per * TILE, (part + 1) * per * TILE
        g_part = [value[:, low:high] for value in (g_keep, g_recv, g_rest)]
        keep, send, spare = assemble(c_base, *g_part, plan_g, child_of_c(part), plan_c)
        pieces.append((keep, send, spare))
    root_1 = spread_block(whole_block(r_edge, rows), devices, r_low // rows, rows)
    first, turn = gather_first(r_edge, [piece[1] for piece in pieces])
    plan_c.place, second = lax.optimization_barrier((plan_c.place, second))
    parts = []
    for part, (keep, send, spare) in enumerate(pieces):
        parts.append(assemble(rfront, keep, *exchange(send, spare, plan_c, half), plan_c, child_of_r(part)))

    inv_11 = inverse_factors(root_1[None])[0]
    low_21 = product_nt(root_2[0], inv_11)
    inv_22 = inverse_factors((root_2[1] - product_nt(low_21, low_21))[None])[0]
    inv_21 = -product(inv_22, product(low_21, inv_11))
    factor_1 = product_nt(r_edge, inv_11)
    factor_2 = product_nt(r_edge, inv_21) + product_nt(own_second, inv_22)
    weights_1 = product(factor_1, inv_11) + product(factor_2, inv_21)
    weights_2 = product(factor_2, inv_22)
    row_ids = me * rows + jnp.arange(rows, dtype=jnp.int32)
    above = (row_ids >= r_low) & (row_ids < r_high)
    factor_2 = jnp.where(above[:, None], 0.0, factor_2)
    rfactor = jnp.concatenate([factor_1, factor_2], 1)
    pairs = per // 2

    def pair(n):
        m = n % (4 * pairs)
        return m % pairs + 2 * pairs * (m // pairs) + pairs * (n // (4 * pairs))

    rschur = finish(*parts, *first, turn, second, jnp.concatenate([weights_1, weights_2], 1), me * rows, pair)
    return (gfactor, cfactor, rfactor, rschur)


def solution(mesh):
    placed = (P("cube", None), P("cube", None), P("cube", None), P(), P())
    return jax.shard_map(
        local,
        mesh=mesh,
        in_specs=placed,
        out_specs=(P("cube", None), P("cube", None), P("cube", None), P("cube", None)),
        check_vma=False,
    )
```

```python
import functools

import jax
import jax.numpy as jnp
from jax import lax
from jax.experimental import pallas as pl
from jax.experimental.pallas import tpu as pltpu
from jax.sharding import PartitionSpec as P

TILE = 256
STRIP = 32
SUB = 8
LANES = 128
HIGH = lax.Precision.HIGH
HIGHEST = lax.Precision.HIGHEST
NT = (((1,), (1,)), ((), ()))
MIB = 1024 * 1024


def widen(column, width):
    return jnp.concatenate([column] * (width // LANES), 1)


def factor_strip(strip, base):
    width = strip[0].shape[1]
    sub_ids = lax.broadcasted_iota(jnp.int32, (SUB, 1), 0)
    count = len(strip)
    for p in range(count):
        first = base + p * SUB
        cols = [
            [jnp.broadcast_to(strip[q][:, first + j : first + j + 1], (SUB, LANES)) for j in range(SUB)]
            for q in range(p, count)
        ]
        for j in range(SUB):
            pivot = cols[0][j][j : j + 1, :]
            inv = lax.rsqrt(pivot)
            inv = inv * (1.5 - 0.5 * pivot * inv * inv)
            unit = strip[p][j : j + 1, :] * widen(inv, width)
            scaled = [col[j] * inv for col in cols]
            below = jnp.where(sub_ids > j, scaled[0], 0.0)
            strip[p] = jnp.where(sub_ids == j, unit, strip[p] - widen(below, width) * unit)
            for q in range(p + 1, count):
                strip[q] = strip[q] - widen(scaled[q - p], width) * unit
            for m in range(j + 1, SUB):
                head = scaled[0][m : m + 1, :]
                for q in range(p, count):
                    cols[q - p][m] = cols[q - p][m] - scaled[q - p] * head
    return jnp.concatenate(strip, 0)


def inverse_kernel(count, blocks_ref, inverse_ref, work):
    row_ids = lax.broadcasted_iota(jnp.int32, (TILE, TILE), 0)
    col_ids = lax.broadcasted_iota(jnp.int32, (TILE, TILE), 1)
    for t in range(count):
        work[t, :, :TILE] = blocks_ref[t]
        work[t, :, TILE:] = (row_ids == col_ids).astype(jnp.float32)
    for low in range(0, TILE, STRIP):
        high = low + STRIP
        left = low // LANES * LANES
        right = TILE + (high + LANES - 1) // LANES * LANES
        done = []
        for t in range(count):
            strip = [work[t, low + SUB * q : low + SUB * (q + 1), left:right] for q in range(STRIP // SUB)]
            done.append(factor_strip(strip, low - left))
        for t in range(count):
            inverse_ref[t, low:high, : right - TILE] = done[t][:, TILE - left :]
            if right < 2 * TILE:
                inverse_ref[t, low:high, right - TILE :] = jnp.zeros((STRIP, 2 * TILE - right), jnp.float32)
            if high < TILE:
                rest = high // LANES * LANES
                update = lax.dot_general(
                    done[t][:, rest - left : TILE - left],
                    done[t],
                    (((0,), (0,)), ((), ())),
                    precision=HIGHEST,
                    preferred_element_type=jnp.float32,
                )
                work[t, high:, left:right] = work[t, high:, left:right] - update[high - rest :]


def inverse_factors(blocks):
    count = blocks.shape[0]
    return pl.pallas_call(
        functools.partial(inverse_kernel, count),
        out_shape=jax.ShapeDtypeStruct(blocks.shape, jnp.float32),
        in_specs=[pl.BlockSpec(memory_space=pltpu.VMEM)],
        out_specs=pl.BlockSpec(memory_space=pltpu.VMEM),
        scratch_shapes=[pltpu.VMEM((count, TILE, 2 * TILE), jnp.float32)],
        compiler_params=pltpu.CompilerParams(vmem_limit_bytes=16 * MIB),
        cost_estimate=pl.CostEstimate(flops=30_000_000_000, bytes_accessed=1_000_000, transcendentals=0),
    )(blocks)


def halves(value):
    top = value.astype(jnp.bfloat16)
    return top, (value - top.astype(jnp.float32)).astype(jnp.bfloat16)


def dot_nt(left, right):
    return lax.dot_general(left, right, NT, preferred_element_type=jnp.float32)


def dot_nn(left, right):
    return jnp.dot(left, right, preferred_element_type=jnp.float32)


def pad_rows(value, count):
    short = count - value.shape[0]
    return value if short == 0 else jnp.concatenate([value, jnp.zeros((short, value.shape[1]), value.dtype)], 0)


def stacked(value):
    return jnp.concatenate(halves(value), 0)


def add_moved(total_ref, recv_ref, place_ref, hot):
    count = place_ref.shape[1]
    moved = dot_nt(stacked(pad_rows(recv_ref[...], count)), hot).astype(jnp.bfloat16)
    total_ref[...] += dot_nn(place_ref[...], moved[:count]) + dot_nn(place_ref[...], moved[count:])


def pick_rows(total, select_ref, outs):
    keep_ref, send_ref, spare_ref = outs
    rows = total.shape[0]
    sent = send_ref.shape[0]
    top, rest = halves(total)
    top = dot_nn(select_ref[...], top)
    rest = dot_nn(select_ref[...], rest)
    keep_ref[:rows] = top[:rows].astype(jnp.bfloat16)
    keep_ref[rows:] = rest[:rows].astype(jnp.bfloat16)
    both = top[rows:] + rest[rows:]
    send_ref[...] = both[:sent]
    spare_ref[...] = both[sent:]


def low_rank(weights_ref, panel):
    rows = weights_ref.shape[0] // 2
    top, rest = halves(panel)
    main = dot_nt(weights_ref[...], top)
    return main[:rows] + (main[rows:] + dot_nt(weights_ref[:rows], rest))


def update_kernel(rows_ref, panel_ref, weights_ref, select_ref, keep_ref, send_ref, spare_ref, split_ref):
    @pl.when(pl.program_id(0) == 0)
    def _():
        split_ref[...] = stacked(weights_ref[...])

    total = rows_ref[...] - low_rank(split_ref, panel_ref[...])
    pick_rows(total, select_ref, (keep_ref, send_ref, spare_ref))


def assemble_kernel(picks, target, flag, *refs):
    base_ref, keep_ref, recv_ref, spare_ref, place_ref, place_spare_ref, keep_map_ref, recv_map_ref = refs[:8]
    total_ref = refs[-1]
    rows = base_ref.shape[0]
    targets = target(pl.program_id(0)) * TILE + lax.broadcasted_iota(jnp.int32, (TILE, TILE), 0)
    keep_hot = jnp.where(keep_map_ref[...] == targets, 1.0, 0.0).astype(jnp.bfloat16)
    recv_hot = jnp.where(recv_map_ref[...] == targets, 1.0, 0.0).astype(jnp.bfloat16)
    kept = dot_nt(keep_ref[...], keep_hot)
    total_ref[...] = base_ref[...] + (kept[:rows] + kept[rows:])
    add_moved(total_ref, recv_ref, place_ref, recv_hot)

    @pl.when(flag[0] != 0)
    def _():
        add_moved(total_ref, spare_ref, place_spare_ref, recv_hot)

    if picks:
        pick_rows(total_ref[...], refs[8], refs[9:12])
    else:
        refs[8][...] = total_ref[...]


def pick_shapes(rows, sent, width):
    return (
        jax.ShapeDtypeStruct((2 * rows, width), jnp.bfloat16),
        jax.ShapeDtypeStruct((sent, width), jnp.float32),
        jax.ShapeDtypeStruct((rows - sent, width), jnp.float32),
    )


def update_and_pick(rows_mat, panel, weights, plan):
    rows, order = rows_mat.shape
    sent = plan.sent
    fixed = lambda shape: pl.BlockSpec(shape, lambda n: (0, 0))
    moving = lambda count: pl.BlockSpec((count, TILE), lambda n: (0, n))
    return pl.pallas_call(
        update_kernel,
        grid=(order // TILE,),
        out_shape=pick_shapes(rows, sent, order),
        in_specs=[
            moving(rows),
            pl.BlockSpec((TILE, TILE), lambda n: (n, 0)),
            fixed((rows, TILE)),
            fixed((2 * rows, rows)),
        ],
        out_specs=(moving(2 * rows), moving(sent), moving(rows - sent)),
        scratch_shapes=[pltpu.VMEM((2 * rows, TILE), jnp.bfloat16)],
        compiler_params=pltpu.CompilerParams(vmem_limit_bytes=48 * MIB),
        cost_estimate=pl.CostEstimate(
            flops=2 * rows * order * TILE * 8, bytes_accessed=rows * order * 16, transcendentals=0
        ),
    )(rows_mat, panel, weights, plan.select)


def assemble(base, keep, recv, spare, plan, child_block, picks=None):
    rows, order = base.shape
    sent = recv.shape[0]
    children = order // 2 // TILE
    per = recv.shape[1] // TILE
    target = lambda n: child_block(n % per) + children * (n // per)
    fixed = lambda shape: pl.BlockSpec(shape, lambda n, _: (0, 0))
    child = lambda count: pl.BlockSpec((count, TILE), lambda n, _: (0, n % per))
    mapped = pl.BlockSpec((1, TILE), lambda n, _: (0, child_block(n % per)))
    wide = lambda count: pl.BlockSpec((count, TILE), lambda n, _: (0, n))
    in_specs = [
        pl.BlockSpec((rows, TILE), lambda n, _: (0, target(n))),
        child(2 * rows),
        child(sent),
        pl.BlockSpec((rows - sent, TILE), lambda n, flag: (0, n % per * flag[0])),
        fixed(plan.place.shape),
        fixed(plan.place_spare.shape),
        mapped,
        mapped,
    ]
    args = [base, keep, recv, spare, plan.place, plan.place_spare, plan.own_map[None], plan.other_map[None]]
    width = 2 * per * TILE
    if picks is None:
        out_shape = jax.ShapeDtypeStruct((rows, width), jnp.float32)
        out_specs = wide(rows)
    else:
        in_specs.append(fixed((2 * rows, rows)))
        args.append(picks.select)
        out_shape = pick_shapes(rows, picks.sent, width)
        out_specs = (wide(2 * rows), wide(picks.sent), wide(rows - picks.sent))
    return pl.pallas_call(
        functools.partial(assemble_kernel, picks is not None, target),
        out_shape=out_shape,
        grid_spec=pltpu.PrefetchScalarGridSpec(
            num_scalar_prefetch=1,
            grid=(2 * per,),
            in_specs=in_specs,
            out_specs=out_specs,
            scratch_shapes=[pltpu.VMEM((rows, TILE), jnp.float32)],
        ),
        compiler_params=pltpu.CompilerParams(vmem_limit_bytes=48 * MIB),
        cost_estimate=pl.CostEstimate(
            flops=2 * rows * width * TILE * 8, bytes_accessed=rows * width * 16, transcendentals=0
        ),
    )(plan.overflow, *args)


def finish_kernel(low, high, pair, where_ref, rows_ref, *refs):
    first_refs, second_refs, weights_ref = refs[:2], refs[2:4], refs[4]
    out_ref, split_ref = refs[-2:]
    n = pl.program_id(0)

    @pl.when(n == 0)
    def _():
        split_ref[...] = stacked(weights_ref[...])

    rows = rows_ref.shape[0]
    row_ids = where_ref[0] + lax.broadcasted_iota(jnp.int32, (rows, 1), 0)
    col_ids = pair(n) * 2 * TILE + lax.broadcasted_iota(jnp.int32, (1, 2 * TILE), 1)
    outside = lambda ids: (ids < low) | (ids >= high)
    turned = where_ref[1] % 2 != 0
    even = jnp.where(turned, first_refs[1][...], first_refs[0][...])
    odd = jnp.where(turned, first_refs[0][...], first_refs[1][...])
    panel = jnp.concatenate(
        [jnp.concatenate([even, odd], 0), jnp.concatenate([ref[...] for ref in second_refs], 0)], 1
    )
    change = low_rank(split_ref, panel)
    out_ref[...] = jnp.where(outside(row_ids) & outside(col_ids), rows_ref[...] - change, 0.0)


def finish(before, first, second, second_at, weights, scalars, pair, out=None):
    rows = before.shape[0]
    order = 2 * before.shape[1]
    low, high = order - 3 * TILE, order - TILE
    count = order // (4 * TILE)
    layers = order // TILE // 8
    wide = lambda index: pl.BlockSpec((rows, 2 * TILE), index)
    piece = pl.BlockSpec((TILE, TILE), lambda n, s: (place_of((2 * pair(n)) ^ s[1], layers), 0))
    later = lambda side: pl.BlockSpec((TILE, TILE), lambda n, s: (second_at(2 * pair(n) + side, s[1]), 0))
    in_specs = [wide(lambda n, _: (0, n)), piece, piece, later(0), later(1), wide(lambda n, _: (0, 0))]
    args = [before, *first, second, second, weights]
    if out is not None:
        in_specs.append(pl.BlockSpec(memory_space=pl.ANY))
        args.append(out)
    return pl.pallas_call(
        functools.partial(finish_kernel, low, high, pair),
        out_shape=jax.ShapeDtypeStruct((rows, order), jnp.float32),
        grid_spec=pltpu.PrefetchScalarGridSpec(
            num_scalar_prefetch=1,
            grid=(count,),
            in_specs=in_specs,
            out_specs=wide(lambda n, _: (0, pair(n))),
            scratch_shapes=[pltpu.VMEM((2 * rows, 2 * TILE), jnp.bfloat16)],
        ),
        input_output_aliases={} if out is None else {7: 0},
        compiler_params=pltpu.CompilerParams(vmem_limit_bytes=48 * MIB),
        cost_estimate=pl.CostEstimate(
            flops=rows * order * TILE * 6, bytes_accessed=rows * order * 8, transcendentals=0
        ),
    )(scalars, *args)


def product(left, right, precision=HIGHEST):
    return jnp.dot(left, right, precision=precision, preferred_element_type=jnp.float32)


def product_nt(left, right, precision=HIGHEST):
    return lax.dot_general(left, right, NT, precision=precision, preferred_element_type=jnp.float32)


def swap(value, mask):
    pairs = [(source, source ^ mask) for source in range(lax.axis_size("cube"))]
    return lax.ppermute(value, "cube", pairs)


def group_gather(value, group):
    size = lax.axis_size("cube")
    groups = [[g * group + i for i in range(group)] for g in range(size // group)]
    return lax.all_gather(value, "cube", axis=0, tiled=True, axis_index_groups=groups)


def one_hot(positions, count):
    return (positions[None, :] == jnp.arange(count, dtype=jnp.int32)[:, None]).astype(jnp.float32)


def column_targets(front_map):
    order = front_map.shape[0]
    ids = jnp.arange(order, dtype=jnp.int32)
    gone = (ids >= order - 2 * TILE) & (ids < order - TILE)
    return jnp.where(gone, -1, front_map)


def leaving(front_map, front, group, rows):
    target = (front_map // rows) // group
    return (front_map >= 0) & (target != front % 2)


class Plan:
    def __init__(self, maps, group, rows):
        me = lax.axis_index("cube")
        front = me // group
        block = me % group
        side = front % 2
        targets = jax.vmap(column_targets)(maps)
        self.sent = (rows * 19 // 32 + 7) // 8 * 8
        fronts = jnp.arange(maps.shape[0], dtype=jnp.int32)
        leaves = leaving(targets, fronts[:, None], group, rows).reshape(maps.shape[0], group, rows)
        most = jnp.max(jnp.sum(leaves.astype(jnp.int32), -1))
        self.overflow = (most > self.sent).astype(jnp.int32).reshape(1)
        self.own_map = lax.dynamic_index_in_dim(targets, front, 0, keepdims=False)
        self.other_map = lax.dynamic_index_in_dim(targets, front ^ 1, 0, keepdims=False)
        own = lax.dynamic_slice_in_dim(self.own_map, block * rows, rows, 0)
        other = lax.dynamic_slice_in_dim(self.other_map, block * rows, rows, 0)
        here = (block + group * side) * rows
        there = (block + group * (1 - side)) * rows
        self.keep = one_hot(own - here, rows)
        self.give = one_hot(own - there, rows)
        ids = jnp.arange(rows, dtype=jnp.int32)
        upper = (ids[:, None] <= ids[None, :]).astype(jnp.bfloat16)
        leaves = (own >= there) & (own < there + rows)
        comes = (other >= here) & (other < here + rows)
        flags = jnp.stack([leaves, comes]).astype(jnp.bfloat16)
        ranks = jnp.dot(flags, upper, preferred_element_type=jnp.float32).astype(jnp.int32) - 1
        send = one_hot(jnp.where(leaves, ranks[0], -1), rows)
        self.select = jnp.concatenate([self.keep, send], 0).astype(jnp.bfloat16)
        taken = one_hot(jnp.where(comes, ranks[1], -1), rows).astype(jnp.bfloat16)
        slots = one_hot(other - here, rows).astype(jnp.bfloat16)
        place = lax.dot_general(slots, taken, NT, preferred_element_type=jnp.float32).astype(jnp.bfloat16)
        fill = lambda part: jnp.pad(part, ((0, 0), (0, -part.shape[1] % 16)))
        self.place = fill(place[:, : self.sent])
        self.place_spare = fill(place[:, self.sent :])


def spread_block(block, group, owner_low, rows):
    size = lax.axis_size("cube")
    me = lax.axis_index("cube")
    holders = max(1, TILE // rows)
    has = {d for d in range(size) if owner_low <= d % group < owner_low + holders}
    inside = (me % group >= owner_low) & (me % group < owner_low + holders)
    block = jnp.where(inside, block, 0.0)
    mask = group // 2
    while mask >= holders:
        pairs = [(d, d ^ mask) for d in sorted(has)]
        block = block + lax.ppermute(block, "cube", pairs)
        has |= {d ^ mask for d in has}
        mask //= 2
    return block


def whole_block(part, rows):
    if rows >= TILE:
        return part
    return group_gather(part, TILE // rows)


def place_of(turned, layers):
    span = layers // 2
    layer, y, x = turned // 8, turned // 4 % 2, turned // 2 % 2
    lower = (2 * y + x) * span + layer
    upper = (4 + 2 * x + y) * span + layer - span
    return jnp.where(layer < span, lower, upper)


def cross_planes(block):
    layers = lax.axis_size("cube") // 8
    if block.shape[0] != TILE:
        return [block]
    return [block] + [swap(block, 8 * layer) for layer in range(1, layers)]


def gather_second(stack):
    layers = lax.axis_size("cube") // 8
    if stack[0].shape[0] != TILE:
        return lax.all_gather(stack[0], "cube", axis=0, tiled=True), lambda cb, me: cb
    return group_gather(jnp.concatenate(stack, 0), 8), lambda cb, me: cb % 8 * layers + (cb // 8 ^ me // 8)


def gather_first(block, after):
    size = lax.axis_size("cube")
    layers = size // 8
    rows = block.shape[0]
    if rows != TILE:
        whole = lax.all_gather(block, "cube", axis=0, tiled=True)
        order = whole.shape[0]
        layers = order // TILE // 8
        spots = [0] * (4 * layers)
        for m in range(4 * layers):
            layer, y, x = m // 4, m // 2 % 2, m % 2
            span = layers // 2
            spot = (2 * y + x) * span + layer if layer < span else (4 + 2 * x + y) * span + layer - span
            spots[spot] = m
        blocks = whole.reshape(order // TILE, TILE, TILE)
        sides = [jnp.concatenate([blocks[2 * m + side] for m in spots], 0) for side in range(2)]
        return sides, jnp.int32(0)
    me = lax.axis_index("cube")
    stack = cross_planes(block)
    stack, after = lax.optimization_barrier((stack, after))
    one = jnp.concatenate(stack[: layers // 2], 0)
    two = jnp.concatenate(stack[layers // 2 :], 0)
    one = jnp.concatenate([one, swap(one, 2)], 0)
    two = jnp.concatenate([two, swap(two, 4)], 0)
    even = jnp.concatenate([one, swap(one, 4), two, swap(two, 2)], 0)
    odd = swap(even, 1)
    return (even, odd), me


def local(gfront, cfront, rfront, gmap, cmap):
    devices = lax.axis_size("cube")
    me = lax.axis_index("cube")
    quarter = devices // 4
    half = devices // 2
    rows = gfront.shape[0]
    order_g, order_c, order_r = gfront.shape[1], cfront.shape[1], rfront.shape[1]
    g_low, c_low = order_g - 2 * TILE, order_c - 2 * TILE
    r_low = order_r - 3 * TILE
    r_high = r_low + TILE

    def exchange(send, spare, plan, mask):
        rest = lax.cond(plan.overflow[0] != 0, lambda part: swap(part, mask), jnp.zeros_like, spare)
        return swap(send, mask), rest

    own_g = gfront[:, g_low : g_low + TILE]
    own_c = cfront[:, c_low : c_low + TILE]
    own_second = rfront[:, r_high : r_high + TILE]
    panel_g = group_gather(own_g, quarter)
    panel_c = group_gather(own_c, half)
    crossed = cross_planes(own_second)
    panel_g, crossed = lax.optimization_barrier((panel_g, crossed))
    second, second_at = gather_second(crossed)
    inverse_g = inverse_factors(panel_g[g_low : g_low + TILE][None])[0]
    inverse_c = spread_block(inverse_factors(whole_block(own_c, rows)[None])[0], half, c_low // rows, rows)
    root_2 = jnp.stack([whole_block(rfront[:, low : low + TILE], rows) for low in (r_low, r_high)])
    root_2 = spread_block(root_2, devices, r_high // rows, rows)
    plan_g = Plan(gmap, quarter, rows)
    plan_c = Plan(cmap, half, rows)

    gfactor = product_nt(own_g, inverse_g)
    weights_g = product(gfactor, inverse_g)
    cfactor = product_nt(own_c, inverse_c)
    weights_c = product(cfactor, inverse_c)

    g_keep, g_send, g_spare = update_and_pick(gfront, panel_g, weights_g, plan_g)
    panel_c, g_send = lax.optimization_barrier((panel_c, g_send))

    g_edge = gfront[:, g_low - TILE : g_low] - product_nt(weights_g, panel_g[g_low - TILE : g_low])
    edge_map = plan_g.own_map[g_low - TILE : g_low]
    g_edge = product_nt(g_edge, one_hot(edge_map - (c_low - TILE), TILE))
    c_edge = cfront[:, c_low - TILE : c_low] - product_nt(weights_c, panel_c[c_low - TILE : c_low])
    c_edge = c_edge + product(plan_g.keep, g_edge) + swap(product(plan_g.give, g_edge), quarter)
    g_recv, g_rest = exchange(g_send, g_spare, plan_g, quarter)
    c_edge, g_recv = lax.optimization_barrier((c_edge, g_recv))
    edge_map = plan_c.own_map[c_low - TILE : c_low]
    c_edge = product_nt(c_edge, one_hot(edge_map - r_low, TILE))
    r_edge = rfront[:, r_low : r_low + TILE] + product(plan_c.keep, c_edge)
    r_come = swap(product(plan_c.give, c_edge), half)
    c_base = cfront - product_nt(weights_c, panel_c, HIGH)
    blocks_g = order_g // TILE
    per = blocks_g // 2
    child_of_c = lambda part: lambda p: part * per + p
    child_of_r = lambda part: lambda p: part * per + p % per + blocks_g * (p // per)
    pieces = []
    for part in range(2):
        low, high = part * per * TILE, (part + 1) * per * TILE
        g_part = [value[:, low:high] for value in (g_keep, g_recv, g_rest)]
        keep, send, spare = assemble(c_base, *g_part, plan_g, child_of_c(part), plan_c)
        pieces.append((keep, send, spare))
    r_come, sends, root_2 = lax.optimization_barrier((r_come, [piece[1] for piece in pieces], root_2))
    r_edge = r_edge + r_come
    root_1 = spread_block(whole_block(r_edge, rows), devices, r_low // rows, rows)
    first, turn = gather_first(r_edge, sends)
    plan_c.place, second = lax.optimization_barrier((plan_c.place, second))
    parts = []
    for part, (keep, _, spare) in enumerate(pieces):
        parts.append(assemble(rfront, keep, *exchange(sends[part], spare, plan_c, half), plan_c, child_of_r(part)))

    inv_11 = inverse_factors(root_1[None])[0]
    low_21 = product_nt(root_2[0], inv_11)
    inv_22 = inverse_factors((root_2[1] - product_nt(low_21, low_21))[None])[0]
    inv_21 = -product(inv_22, product(low_21, inv_11))
    factor_1 = product_nt(r_edge, inv_11)
    factor_2 = product_nt(r_edge, inv_21) + product_nt(own_second, inv_22)
    weights_1 = product(factor_1, inv_11) + product(factor_2, inv_21)
    weights_2 = product(factor_2, inv_22)
    row_ids = me * rows + jnp.arange(rows, dtype=jnp.int32)
    above = (row_ids >= r_low) & (row_ids < r_high)
    factor_2 = jnp.where(above[:, None], 0.0, factor_2)
    rfactor = jnp.concatenate([factor_1, factor_2], 1)
    pairs = per // 2

    pair_of = lambda part: lambda n: n % pairs + 2 * pairs * (n // pairs) + pairs * part
    scalars = jnp.stack([me * rows, turn]).astype(jnp.int32)
    weights_r = jnp.concatenate([weights_1, weights_2], 1)
    rschur = None
    for part in range(2):
        rschur = finish(parts[part], first, second, second_at, weights_r, scalars, pair_of(part), rschur)
    return (gfactor, cfactor, rfactor, rschur)


def solution(mesh):
    placed = (P("cube", None), P("cube", None), P("cube", None), P(), P())
    return jax.shard_map(
        local,
        mesh=mesh,
        in_specs=placed,
        out_specs=(P("cube", None), P("cube", None), P("cube", None), P("cube", None)),
        check_vma=False,
    )
```

```python
import functools

import jax
import jax.numpy as jnp
from jax import lax
from jax.experimental import pallas as pl
from jax.experimental.pallas import tpu as pltpu
from jax.sharding import PartitionSpec as P

TILE = 256
STRIP = 32
SUB = 8
LANES = 128
HIGH = lax.Precision.HIGH
HIGHEST = lax.Precision.HIGHEST
NT = (((1,), (1,)), ((), ()))
MIB = 1024 * 1024


def widen(column, width):
    return jnp.concatenate([column] * (width // LANES), 1)


def factor_strip(strip, base):
    width = strip[0].shape[1]
    sub_ids = lax.broadcasted_iota(jnp.int32, (SUB, 1), 0)
    count = len(strip)
    for p in range(count):
        first = base + p * SUB
        cols = [
            [jnp.broadcast_to(strip[q][:, first + j : first + j + 1], (SUB, LANES)) for j in range(SUB)]
            for q in range(p, count)
        ]
        for j in range(SUB):
            pivot = cols[0][j][j : j + 1, :]
            inv = lax.rsqrt(pivot)
            inv = inv * (1.5 - 0.5 * pivot * inv * inv)
            unit = strip[p][j : j + 1, :] * widen(inv, width)
            scaled = [col[j] * inv for col in cols]
            below = jnp.where(sub_ids > j, scaled[0], 0.0)
            strip[p] = jnp.where(sub_ids == j, unit, strip[p] - widen(below, width) * unit)
            for q in range(p + 1, count):
                strip[q] = strip[q] - widen(scaled[q - p], width) * unit
            for m in range(j + 1, SUB):
                head = scaled[0][m : m + 1, :]
                for q in range(p, count):
                    cols[q - p][m] = cols[q - p][m] - scaled[q - p] * head
    return jnp.concatenate(strip, 0)


def inverse_kernel(count, blocks_ref, inverse_ref, work):
    row_ids = lax.broadcasted_iota(jnp.int32, (TILE, TILE), 0)
    col_ids = lax.broadcasted_iota(jnp.int32, (TILE, TILE), 1)
    for t in range(count):
        work[t, :, :TILE] = blocks_ref[t]
        work[t, :, TILE:] = (row_ids == col_ids).astype(jnp.float32)
    for low in range(0, TILE, STRIP):
        high = low + STRIP
        left = low // LANES * LANES
        right = TILE + (high + LANES - 1) // LANES * LANES
        done = []
        for t in range(count):
            strip = [work[t, low + SUB * q : low + SUB * (q + 1), left:right] for q in range(STRIP // SUB)]
            done.append(factor_strip(strip, low - left))
        for t in range(count):
            inverse_ref[t, low:high, : right - TILE] = done[t][:, TILE - left :]
            if right < 2 * TILE:
                inverse_ref[t, low:high, right - TILE :] = jnp.zeros((STRIP, 2 * TILE - right), jnp.float32)
            if high < TILE:
                rest = high // LANES * LANES
                update = lax.dot_general(
                    done[t][:, rest - left : TILE - left],
                    done[t],
                    (((0,), (0,)), ((), ())),
                    precision=HIGHEST,
                    preferred_element_type=jnp.float32,
                )
                work[t, high:, left:right] = work[t, high:, left:right] - update[high - rest :]


def inverse_factors(blocks):
    count = blocks.shape[0]
    return pl.pallas_call(
        functools.partial(inverse_kernel, count),
        out_shape=jax.ShapeDtypeStruct(blocks.shape, jnp.float32),
        in_specs=[pl.BlockSpec(memory_space=pltpu.VMEM)],
        out_specs=pl.BlockSpec(memory_space=pltpu.VMEM),
        scratch_shapes=[pltpu.VMEM((count, TILE, 2 * TILE), jnp.float32)],
        compiler_params=pltpu.CompilerParams(vmem_limit_bytes=16 * MIB),
        cost_estimate=pl.CostEstimate(flops=30_000_000_000, bytes_accessed=1_000_000, transcendentals=0),
    )(blocks)


def halves(value):
    top = value.astype(jnp.bfloat16)
    return top, (value - top.astype(jnp.float32)).astype(jnp.bfloat16)


def dot_nt(left, right):
    return lax.dot_general(left, right, NT, preferred_element_type=jnp.float32)


def dot_nn(left, right):
    return jnp.dot(left, right, preferred_element_type=jnp.float32)


def pad_rows(value, count):
    short = count - value.shape[0]
    return value if short == 0 else jnp.concatenate([value, jnp.zeros((short, value.shape[1]), value.dtype)], 0)


def stacked(value):
    return jnp.concatenate(halves(value), 0)


def add_moved(total_ref, recv_ref, place_ref, hot):
    count = place_ref.shape[1]
    moved = dot_nt(stacked(pad_rows(recv_ref[...], count)), hot).astype(jnp.bfloat16)
    total_ref[...] += dot_nn(place_ref[...], moved[:count]) + dot_nn(place_ref[...], moved[count:])


def pick_rows(total, select_ref, outs):
    keep_ref, send_ref, spare_ref = outs
    rows = total.shape[0]
    sent = send_ref.shape[0]
    top, rest = halves(total)
    top = dot_nn(select_ref[...], top)
    rest = dot_nn(select_ref[...], rest)
    keep_ref[:rows] = top[:rows].astype(jnp.bfloat16)
    keep_ref[rows:] = rest[:rows].astype(jnp.bfloat16)
    both = top[rows:] + rest[rows:]
    send_ref[...] = both[:sent]
    spare_ref[...] = both[sent:]


def low_rank(weights_ref, panel):
    rows = weights_ref.shape[0] // 2
    top, rest = halves(panel)
    main = dot_nt(weights_ref[...], top)
    return main[:rows] + (main[rows:] + dot_nt(weights_ref[:rows], rest))


def update_kernel(rows_ref, panel_ref, weights_ref, select_ref, keep_ref, send_ref, spare_ref, split_ref):
    @pl.when(pl.program_id(0) == 0)
    def _():
        split_ref[...] = stacked(weights_ref[...])

    total = rows_ref[...] - low_rank(split_ref, panel_ref[...])
    pick_rows(total, select_ref, (keep_ref, send_ref, spare_ref))


def assemble_kernel(picks, target, flag, *refs):
    base_ref, keep_ref, recv_ref, spare_ref, place_ref, place_spare_ref, keep_map_ref, recv_map_ref = refs[:8]
    total_ref = refs[-1]
    rows = base_ref.shape[0]
    targets = target(pl.program_id(0)) * TILE + lax.broadcasted_iota(jnp.int32, (TILE, TILE), 0)
    keep_hot = jnp.where(keep_map_ref[...] == targets, 1.0, 0.0).astype(jnp.bfloat16)
    recv_hot = jnp.where(recv_map_ref[...] == targets, 1.0, 0.0).astype(jnp.bfloat16)
    kept = dot_nt(keep_ref[...], keep_hot)
    total_ref[...] = base_ref[...] + (kept[:rows] + kept[rows:])
    add_moved(total_ref, recv_ref, place_ref, recv_hot)

    @pl.when(flag[0] != 0)
    def _():
        add_moved(total_ref, spare_ref, place_spare_ref, recv_hot)

    if picks:
        pick_rows(total_ref[...], refs[8], refs[9:12])
    else:
        refs[8][...] = total_ref[...]


def pick_shapes(rows, sent, width):
    return (
        jax.ShapeDtypeStruct((2 * rows, width), jnp.bfloat16),
        jax.ShapeDtypeStruct((sent, width), jnp.float32),
        jax.ShapeDtypeStruct((rows - sent, width), jnp.float32),
    )


def update_and_pick(rows_mat, panel, weights, plan):
    rows, order = rows_mat.shape
    sent = plan.sent
    fixed = lambda shape: pl.BlockSpec(shape, lambda n: (0, 0))
    moving = lambda count: pl.BlockSpec((count, TILE), lambda n: (0, n))
    return pl.pallas_call(
        update_kernel,
        grid=(order // TILE,),
        out_shape=pick_shapes(rows, sent, order),
        in_specs=[
            moving(rows),
            pl.BlockSpec((TILE, TILE), lambda n: (n, 0)),
            fixed((rows, TILE)),
            fixed((2 * rows, rows)),
        ],
        out_specs=(moving(2 * rows), moving(sent), moving(rows - sent)),
        scratch_shapes=[pltpu.VMEM((2 * rows, TILE), jnp.bfloat16)],
        compiler_params=pltpu.CompilerParams(vmem_limit_bytes=48 * MIB),
        cost_estimate=pl.CostEstimate(
            flops=2 * rows * order * TILE * 8, bytes_accessed=rows * order * 16, transcendentals=0
        ),
    )(rows_mat, panel, weights, plan.select)


def assemble(base, keep, recv, spare, plan, child_block, picks=None):
    rows, order = base.shape
    sent = recv.shape[0]
    children = order // 2 // TILE
    per = recv.shape[1] // TILE
    target = lambda n: child_block(n % per) + children * (n // per)
    fixed = lambda shape: pl.BlockSpec(shape, lambda n, _: (0, 0))
    child = lambda count: pl.BlockSpec((count, TILE), lambda n, _: (0, n % per))
    mapped = pl.BlockSpec((1, TILE), lambda n, _: (0, child_block(n % per)))
    wide = lambda count: pl.BlockSpec((count, TILE), lambda n, _: (0, n))
    in_specs = [
        pl.BlockSpec((rows, TILE), lambda n, _: (0, target(n))),
        child(2 * rows),
        child(sent),
        pl.BlockSpec((rows - sent, TILE), lambda n, flag: (0, n % per * flag[0])),
        fixed(plan.place.shape),
        fixed(plan.place_spare.shape),
        mapped,
        mapped,
    ]
    args = [base, keep, recv, spare, plan.place, plan.place_spare, plan.own_map[None], plan.other_map[None]]
    width = 2 * per * TILE
    if picks is None:
        out_shape = jax.ShapeDtypeStruct((rows, width), jnp.float32)
        out_specs = wide(rows)
    else:
        in_specs.append(fixed((2 * rows, rows)))
        args.append(picks.select)
        out_shape = pick_shapes(rows, picks.sent, width)
        out_specs = (wide(2 * rows), wide(picks.sent), wide(rows - picks.sent))
    return pl.pallas_call(
        functools.partial(assemble_kernel, picks is not None, target),
        out_shape=out_shape,
        grid_spec=pltpu.PrefetchScalarGridSpec(
            num_scalar_prefetch=1,
            grid=(2 * per,),
            in_specs=in_specs,
            out_specs=out_specs,
            scratch_shapes=[pltpu.VMEM((rows, TILE), jnp.float32)],
        ),
        compiler_params=pltpu.CompilerParams(vmem_limit_bytes=48 * MIB),
        cost_estimate=pl.CostEstimate(
            flops=2 * rows * width * TILE * 8, bytes_accessed=rows * width * 16, transcendentals=0
        ),
    )(plan.overflow, *args)


def finish_kernel(low, high, pair, where_ref, rows_ref, *refs):
    first_refs, second_refs, weights_ref = refs[:2], refs[2:4], refs[4]
    out_ref, split_ref = refs[-2:]
    n = pl.program_id(0)

    @pl.when(n == 0)
    def _():
        split_ref[...] = stacked(weights_ref[...])

    rows = rows_ref.shape[0]
    row_ids = where_ref[0] + lax.broadcasted_iota(jnp.int32, (rows, 1), 0)
    col_ids = pair(n) * 2 * TILE + lax.broadcasted_iota(jnp.int32, (1, 2 * TILE), 1)
    outside = lambda ids: (ids < low) | (ids >= high)
    turned = where_ref[1] % 2 != 0
    even = jnp.where(turned, first_refs[1][...], first_refs[0][...])
    odd = jnp.where(turned, first_refs[0][...], first_refs[1][...])
    panel = jnp.concatenate(
        [jnp.concatenate([even, odd], 0), jnp.concatenate([ref[...] for ref in second_refs], 0)], 1
    )
    change = low_rank(split_ref, panel)
    out_ref[...] = jnp.where(outside(row_ids) & outside(col_ids), rows_ref[...] - change, 0.0)


def finish(before, first, second, second_at, weights, scalars, pair, out=None):
    rows = before.shape[0]
    order = 2 * before.shape[1]
    low, high = order - 3 * TILE, order - TILE
    count = order // (4 * TILE)
    layers = order // TILE // 8
    wide = lambda index: pl.BlockSpec((rows, 2 * TILE), index)
    piece = pl.BlockSpec((TILE, TILE), lambda n, s: (place_of((2 * pair(n)) ^ s[1], layers), 0))
    later = lambda side: pl.BlockSpec((TILE, TILE), lambda n, s: (second_at(2 * pair(n) + side, s[1]), 0))
    in_specs = [wide(lambda n, _: (0, n)), piece, piece, later(0), later(1), wide(lambda n, _: (0, 0))]
    args = [before, *first, second, second, weights]
    if out is not None:
        in_specs.append(pl.BlockSpec(memory_space=pl.ANY))
        args.append(out)
    return pl.pallas_call(
        functools.partial(finish_kernel, low, high, pair),
        out_shape=jax.ShapeDtypeStruct((rows, order), jnp.float32),
        grid_spec=pltpu.PrefetchScalarGridSpec(
            num_scalar_prefetch=1,
            grid=(count,),
            in_specs=in_specs,
            out_specs=wide(lambda n, _: (0, pair(n))),
            scratch_shapes=[pltpu.VMEM((2 * rows, 2 * TILE), jnp.bfloat16)],
        ),
        input_output_aliases={} if out is None else {7: 0},
        compiler_params=pltpu.CompilerParams(vmem_limit_bytes=48 * MIB),
        cost_estimate=pl.CostEstimate(
            flops=rows * order * TILE * 6, bytes_accessed=rows * order * 8, transcendentals=0
        ),
    )(scalars, *args)


def product(left, right, precision=HIGHEST):
    return jnp.dot(left, right, precision=precision, preferred_element_type=jnp.float32)


def product_nt(left, right, precision=HIGHEST):
    return lax.dot_general(left, right, NT, precision=precision, preferred_element_type=jnp.float32)


def swap(value, mask):
    pairs = [(source, source ^ mask) for source in range(lax.axis_size("cube"))]
    return lax.ppermute(value, "cube", pairs)


def group_gather(value, group):
    size = lax.axis_size("cube")
    groups = [[g * group + i for i in range(group)] for g in range(size // group)]
    return lax.all_gather(value, "cube", axis=0, tiled=True, axis_index_groups=groups)


def one_hot(positions, count):
    return (positions[None, :] == jnp.arange(count, dtype=jnp.int32)[:, None]).astype(jnp.float32)


def column_targets(front_map):
    order = front_map.shape[0]
    ids = jnp.arange(order, dtype=jnp.int32)
    gone = (ids >= order - 2 * TILE) & (ids < order - TILE)
    return jnp.where(gone, -1, front_map)


def leaving(front_map, front, group, rows):
    target = (front_map // rows) // group
    return (front_map >= 0) & (target != front % 2)


class Plan:
    def __init__(self, maps, group, rows):
        me = lax.axis_index("cube")
        front = me // group
        block = me % group
        side = front % 2
        targets = jax.vmap(column_targets)(maps)
        self.sent = (rows * 19 // 32 + 7) // 8 * 8
        fronts = jnp.arange(maps.shape[0], dtype=jnp.int32)
        leaves = leaving(targets, fronts[:, None], group, rows).reshape(maps.shape[0], group, rows)
        most = jnp.max(jnp.sum(leaves.astype(jnp.int32), -1))
        self.overflow = (most > self.sent).astype(jnp.int32).reshape(1)
        self.own_map = lax.dynamic_index_in_dim(targets, front, 0, keepdims=False)
        self.other_map = lax.dynamic_index_in_dim(targets, front ^ 1, 0, keepdims=False)
        own = lax.dynamic_slice_in_dim(self.own_map, block * rows, rows, 0)
        other = lax.dynamic_slice_in_dim(self.other_map, block * rows, rows, 0)
        here = (block + group * side) * rows
        there = (block + group * (1 - side)) * rows
        self.keep = one_hot(own - here, rows)
        self.give = one_hot(own - there, rows)
        ids = jnp.arange(rows, dtype=jnp.int32)
        upper = (ids[:, None] <= ids[None, :]).astype(jnp.bfloat16)
        leaves = (own >= there) & (own < there + rows)
        comes = (other >= here) & (other < here + rows)
        flags = jnp.stack([leaves, comes]).astype(jnp.bfloat16)
        ranks = jnp.dot(flags, upper, preferred_element_type=jnp.float32).astype(jnp.int32) - 1
        send = one_hot(jnp.where(leaves, ranks[0], -1), rows)
        self.select = jnp.concatenate([self.keep, send], 0).astype(jnp.bfloat16)
        taken = one_hot(jnp.where(comes, ranks[1], -1), rows).astype(jnp.bfloat16)
        slots = one_hot(other - here, rows).astype(jnp.bfloat16)
        place = lax.dot_general(slots, taken, NT, preferred_element_type=jnp.float32).astype(jnp.bfloat16)
        fill = lambda part: jnp.pad(part, ((0, 0), (0, -part.shape[1] % 16)))
        self.place = fill(place[:, : self.sent])
        self.place_spare = fill(place[:, self.sent :])


def spread_block(block, group, owner_low, rows):
    size = lax.axis_size("cube")
    me = lax.axis_index("cube")
    holders = max(1, TILE // rows)
    has = {d for d in range(size) if owner_low <= d % group < owner_low + holders}
    inside = (me % group >= owner_low) & (me % group < owner_low + holders)
    block = jnp.where(inside, block, 0.0)
    mask = group // 2
    while mask >= holders:
        pairs = [(d, d ^ mask) for d in sorted(has)]
        block = block + lax.ppermute(block, "cube", pairs)
        has |= {d ^ mask for d in has}
        mask //= 2
    return block


def whole_block(part, rows):
    if rows >= TILE:
        return part
    return group_gather(part, TILE // rows)


def place_of(turned, layers):
    span = layers // 2
    layer, y, x = turned // 8, turned // 4 % 2, turned // 2 % 2
    lower = (2 * y + x) * span + layer
    upper = (4 + 2 * x + y) * span + layer - span
    return jnp.where(layer < span, lower, upper)


def cross_planes(block):
    layers = lax.axis_size("cube") // 8
    if block.shape[0] != TILE:
        return [block]
    return [block] + [swap(block, 8 * layer) for layer in range(1, layers)]


def gather_second(stack):
    layers = lax.axis_size("cube") // 8
    if stack[0].shape[0] != TILE:
        return lax.all_gather(stack[0], "cube", axis=0, tiled=True), lambda cb, me: cb
    return group_gather(jnp.concatenate(stack, 0), 8), lambda cb, me: cb % 8 * layers + (cb // 8 ^ me // 8)


def gather_first(block, after):
    size = lax.axis_size("cube")
    layers = size // 8
    rows = block.shape[0]
    if rows != TILE:
        whole = lax.all_gather(block, "cube", axis=0, tiled=True)
        order = whole.shape[0]
        layers = order // TILE // 8
        spots = [0] * (4 * layers)
        for m in range(4 * layers):
            layer, y, x = m // 4, m // 2 % 2, m % 2
            span = layers // 2
            spot = (2 * y + x) * span + layer if layer < span else (4 + 2 * x + y) * span + layer - span
            spots[spot] = m
        blocks = whole.reshape(order // TILE, TILE, TILE)
        sides = [jnp.concatenate([blocks[2 * m + side] for m in spots], 0) for side in range(2)]
        return sides, jnp.int32(0)
    me = lax.axis_index("cube")
    stack = cross_planes(block)
    stack, after = lax.optimization_barrier((stack, after))
    one = jnp.concatenate(stack[: layers // 2], 0)
    two = jnp.concatenate(stack[layers // 2 :], 0)
    one = jnp.concatenate([one, swap(one, 2)], 0)
    two = jnp.concatenate([two, swap(two, 4)], 0)
    even = jnp.concatenate([one, swap(one, 4), two, swap(two, 2)], 0)
    odd = swap(even, 1)
    return (even, odd), me


def local(gfront, cfront, rfront, gmap, cmap):
    devices = lax.axis_size("cube")
    me = lax.axis_index("cube")
    quarter = devices // 4
    half = devices // 2
    rows = gfront.shape[0]
    order_g, order_c, order_r = gfront.shape[1], cfront.shape[1], rfront.shape[1]
    g_low, c_low = order_g - 2 * TILE, order_c - 2 * TILE
    r_low = order_r - 3 * TILE
    r_high = r_low + TILE

    def exchange(send, spare, plan, mask):
        rest = lax.cond(plan.overflow[0] != 0, lambda part: swap(part, mask), jnp.zeros_like, spare)
        return swap(send, mask), rest

    own_g = gfront[:, g_low : g_low + TILE]
    own_c = cfront[:, c_low : c_low + TILE]
    own_second = rfront[:, r_high : r_high + TILE]
    panel_g = group_gather(own_g, quarter)
    panel_c = group_gather(own_c, half)
    crossed = cross_planes(own_second)
    inverse_g = inverse_factors(panel_g[g_low : g_low + TILE][None])[0]
    inverse_c = spread_block(inverse_factors(whole_block(own_c, rows)[None])[0], half, c_low // rows, rows)
    root_2 = jnp.stack([whole_block(rfront[:, low : low + TILE], rows) for low in (r_low, r_high)])
    root_2 = spread_block(root_2, devices, r_high // rows, rows)
    plan_g = Plan(gmap, quarter, rows)
    plan_c = Plan(cmap, half, rows)

    gfactor = product_nt(own_g, inverse_g)
    weights_g = product(gfactor, inverse_g)

    g_keep, g_send, g_spare = update_and_pick(gfront, panel_g, weights_g, plan_g)
    panel_c, g_send, inverse_c, crossed = lax.optimization_barrier((panel_c, g_send, inverse_c, crossed))
    second, second_at = gather_second(crossed)
    cfactor = product_nt(own_c, inverse_c)
    weights_c = product(cfactor, inverse_c)

    g_edge = gfront[:, g_low - TILE : g_low] - product_nt(weights_g, panel_g[g_low - TILE : g_low])
    edge_map = plan_g.own_map[g_low - TILE : g_low]
    g_edge = product_nt(g_edge, one_hot(edge_map - (c_low - TILE), TILE))
    c_edge = cfront[:, c_low - TILE : c_low] - product_nt(weights_c, panel_c[c_low - TILE : c_low])
    c_edge = c_edge + product(plan_g.keep, g_edge) + swap(product(plan_g.give, g_edge), quarter)
    g_recv, g_rest = exchange(g_send, g_spare, plan_g, quarter)
    c_edge, g_recv = lax.optimization_barrier((c_edge, g_recv))
    edge_map = plan_c.own_map[c_low - TILE : c_low]
    c_edge = product_nt(c_edge, one_hot(edge_map - r_low, TILE))
    r_edge = rfront[:, r_low : r_low + TILE] + product(plan_c.keep, c_edge)
    r_come = swap(product(plan_c.give, c_edge), half)
    c_base = cfront - product_nt(weights_c, panel_c, HIGH)
    blocks_g = order_g // TILE
    per = blocks_g // 2
    child_of_c = lambda part: lambda p: part * per + p
    child_of_r = lambda part: lambda p: part * per + p % per + blocks_g * (p // per)
    pieces, sends = [], []
    for part in range(2):
        low, high = part * per * TILE, (part + 1) * per * TILE
        g_part = [value[:, low:high] for value in (g_keep, g_recv, g_rest)]
        keep, send, spare = assemble(c_base, *g_part, plan_g, child_of_c(part), plan_c)
        sends.append(send)
        pieces.append((keep, *exchange(send, spare, plan_c, half)))
    r_come, sends, root_2 = lax.optimization_barrier((r_come, sends, root_2))
    r_edge = r_edge + r_come
    root_1 = spread_block(whole_block(r_edge, rows), devices, r_low // rows, rows)
    first, turn = gather_first(r_edge, sends)
    plan_c.place, second = lax.optimization_barrier((plan_c.place, second))

    inv_11 = inverse_factors(root_1[None])[0]
    low_21 = product_nt(root_2[0], inv_11)
    inv_22 = inverse_factors((root_2[1] - product_nt(low_21, low_21))[None])[0]
    inv_21 = -product(inv_22, product(low_21, inv_11))
    factor_1 = product_nt(r_edge, inv_11)
    factor_2 = product_nt(r_edge, inv_21) + product_nt(own_second, inv_22)
    weights_1 = product(factor_1, inv_11) + product(factor_2, inv_21)
    weights_2 = product(factor_2, inv_22)
    row_ids = me * rows + jnp.arange(rows, dtype=jnp.int32)
    above = (row_ids >= r_low) & (row_ids < r_high)
    factor_2 = jnp.where(above[:, None], 0.0, factor_2)
    rfactor = jnp.concatenate([factor_1, factor_2], 1)
    pairs = per // 2

    pair_of = lambda part: lambda n: n % pairs + 2 * pairs * (n // pairs) + pairs * part
    scalars = jnp.stack([me * rows, turn]).astype(jnp.int32)
    weights_r = jnp.concatenate([weights_1, weights_2], 1)
    rschur = None
    for part, (keep, recv, rest) in enumerate(pieces):
        if part:
            rschur, recv = lax.optimization_barrier((rschur, recv))
        before = assemble(rfront, keep, recv, rest, plan_c, child_of_r(part))
        rschur = finish(before, first, second, second_at, weights_r, scalars, pair_of(part), rschur)
    return (gfactor, cfactor, rfactor, rschur)


def solution(mesh):
    placed = (P("cube", None), P("cube", None), P("cube", None), P(), P())
    return jax.shard_map(
        local,
        mesh=mesh,
        in_specs=placed,
        out_specs=(P("cube", None), P("cube", None), P("cube", None), P("cube", None)),
        check_vma=False,
    )
```

```python
import functools

import jax
import jax.numpy as jnp
from jax import lax
from jax.experimental import pallas as pl
from jax.experimental.pallas import tpu as pltpu
from jax.sharding import PartitionSpec as P

TILE = 256
STRIP = 32
SUB = 8
LANES = 128
HIGH = lax.Precision.HIGH
HIGHEST = lax.Precision.HIGHEST
NT = (((1,), (1,)), ((), ()))
MIB = 1024 * 1024
SMALL = pl.CostEstimate(flops=1, bytes_accessed=1, transcendentals=0)


def widen(column, width):
    return jnp.concatenate([column] * (width // LANES), 1)


def factor_strip(strip, base):
    width = strip[0].shape[1]
    sub_ids = lax.broadcasted_iota(jnp.int32, (SUB, 1), 0)
    count = len(strip)
    for p in range(count):
        first = base + p * SUB
        cols = [
            [jnp.broadcast_to(strip[q][:, first + j : first + j + 1], (SUB, LANES)) for j in range(SUB)]
            for q in range(p, count)
        ]
        for j in range(SUB):
            pivot = cols[0][j][j : j + 1, :]
            inv = lax.rsqrt(pivot)
            inv = inv * (1.5 - 0.5 * pivot * inv * inv)
            unit = strip[p][j : j + 1, :] * widen(inv, width)
            scaled = [col[j] * inv for col in cols]
            below = jnp.where(sub_ids > j, scaled[0], 0.0)
            strip[p] = jnp.where(sub_ids == j, unit, strip[p] - widen(below, width) * unit)
            for q in range(p + 1, count):
                strip[q] = strip[q] - widen(scaled[q - p], width) * unit
            for m in range(j + 1, SUB):
                head = scaled[0][m : m + 1, :]
                for q in range(p, count):
                    cols[q - p][m] = cols[q - p][m] - scaled[q - p] * head
    return jnp.concatenate(strip, 0)


def inverse_kernel(count, blocks_ref, inverse_ref, work):
    row_ids = lax.broadcasted_iota(jnp.int32, (TILE, TILE), 0)
    col_ids = lax.broadcasted_iota(jnp.int32, (TILE, TILE), 1)
    for t in range(count):
        work[t, :, :TILE] = blocks_ref[t]
        work[t, :, TILE:] = (row_ids == col_ids).astype(jnp.float32)
    for low in range(0, TILE, STRIP):
        high = low + STRIP
        left = low // LANES * LANES
        right = TILE + (high + LANES - 1) // LANES * LANES
        done = []
        for t in range(count):
            strip = [work[t, low + SUB * q : low + SUB * (q + 1), left:right] for q in range(STRIP // SUB)]
            done.append(factor_strip(strip, low - left))
        for t in range(count):
            inverse_ref[t, low:high, : right - TILE] = done[t][:, TILE - left :]
            if right < 2 * TILE:
                inverse_ref[t, low:high, right - TILE :] = jnp.zeros((STRIP, 2 * TILE - right), jnp.float32)
            if high < TILE:
                rest = high // LANES * LANES
                update = lax.dot_general(
                    done[t][:, rest - left : TILE - left],
                    done[t],
                    (((0,), (0,)), ((), ())),
                    precision=HIGHEST,
                    preferred_element_type=jnp.float32,
                )
                work[t, high:, left:right] = work[t, high:, left:right] - update[high - rest :]


def inverse_factors(blocks):
    count = blocks.shape[0]
    return pl.pallas_call(
        functools.partial(inverse_kernel, count),
        out_shape=jax.ShapeDtypeStruct(blocks.shape, jnp.float32),
        in_specs=[pl.BlockSpec(memory_space=pltpu.VMEM)],
        out_specs=pl.BlockSpec(memory_space=pltpu.VMEM),
        scratch_shapes=[pltpu.VMEM((count, TILE, 2 * TILE), jnp.float32)],
        compiler_params=pltpu.CompilerParams(vmem_limit_bytes=16 * MIB),
        cost_estimate=SMALL,
    )(blocks)


def halves(value):
    top = value.astype(jnp.bfloat16)
    return top, (value - top.astype(jnp.float32)).astype(jnp.bfloat16)


def dot_nt(left, right):
    return lax.dot_general(left, right, NT, preferred_element_type=jnp.float32)


def dot_nn(left, right):
    return jnp.dot(left, right, preferred_element_type=jnp.float32)


def pad_rows(value, count):
    short = count - value.shape[0]
    return value if short == 0 else jnp.concatenate([value, jnp.zeros((short, value.shape[1]), value.dtype)], 0)


def stacked(value):
    return jnp.concatenate(halves(value), 0)


def add_moved(total_ref, recv_ref, place_ref, hot):
    count = place_ref.shape[1]
    moved = dot_nt(stacked(pad_rows(recv_ref[...], count)), hot).astype(jnp.bfloat16)
    total_ref[...] += dot_nn(place_ref[...], moved[:count]) + dot_nn(place_ref[...], moved[count:])


def pick_rows(total, select_ref, outs):
    keep_ref, send_ref, spare_ref = outs
    rows = total.shape[0]
    sent = send_ref.shape[0]
    top, rest = halves(total)
    top = dot_nn(select_ref[...], top)
    rest = dot_nn(select_ref[...], rest)
    keep_ref[:rows] = top[:rows].astype(jnp.bfloat16)
    keep_ref[rows:] = rest[:rows].astype(jnp.bfloat16)
    both = top[rows:] + rest[rows:]
    send_ref[...] = both[:sent]
    spare_ref[...] = both[sent:]


def low_rank(weights_ref, panel):
    rows = weights_ref.shape[0] // 2
    top, rest = halves(panel)
    main = dot_nt(weights_ref[...], top)
    return main[:rows] + (main[rows:] + dot_nt(weights_ref[:rows], rest))


def update_kernel(rows_ref, panel_ref, weights_ref, select_ref, keep_ref, send_ref, spare_ref, split_ref):
    @pl.when(pl.program_id(0) == 0)
    def _():
        split_ref[...] = stacked(weights_ref[...])

    total = rows_ref[...] - low_rank(split_ref, panel_ref[...])
    pick_rows(total, select_ref, (keep_ref, send_ref, spare_ref))


def assemble_kernel(picks, target, flag, *refs):
    base_ref, keep_ref, recv_ref, spare_ref, place_ref, place_spare_ref, keep_map_ref, recv_map_ref = refs[:8]
    total_ref = refs[-1]
    rows = base_ref.shape[0]
    targets = target(pl.program_id(0)) * TILE + lax.broadcasted_iota(jnp.int32, (TILE, TILE), 0)
    keep_hot = jnp.where(keep_map_ref[...] == targets, 1.0, 0.0).astype(jnp.bfloat16)
    recv_hot = jnp.where(recv_map_ref[...] == targets, 1.0, 0.0).astype(jnp.bfloat16)
    kept = dot_nt(keep_ref[...], keep_hot)
    total_ref[...] = base_ref[...] + (kept[:rows] + kept[rows:])
    add_moved(total_ref, recv_ref, place_ref, recv_hot)

    @pl.when(flag[0] != 0)
    def _():
        add_moved(total_ref, spare_ref, place_spare_ref, recv_hot)

    if picks:
        pick_rows(total_ref[...], refs[8], refs[9:12])
    else:
        refs[8][...] = total_ref[...]


def pick_shapes(rows, sent, width):
    return (
        jax.ShapeDtypeStruct((2 * rows, width), jnp.bfloat16),
        jax.ShapeDtypeStruct((sent, width), jnp.float32),
        jax.ShapeDtypeStruct((rows - sent, width), jnp.float32),
    )


def update_and_pick(rows_mat, panel, weights, plan):
    rows, order = rows_mat.shape
    sent = plan.sent
    fixed = lambda shape: pl.BlockSpec(shape, lambda n: (0, 0))
    moving = lambda count: pl.BlockSpec((count, TILE), lambda n: (0, n))
    return pl.pallas_call(
        update_kernel,
        grid=(order // TILE,),
        out_shape=pick_shapes(rows, sent, order),
        in_specs=[
            moving(rows),
            pl.BlockSpec((TILE, TILE), lambda n: (n, 0)),
            fixed((rows, TILE)),
            fixed((2 * rows, rows)),
        ],
        out_specs=(moving(2 * rows), moving(sent), moving(rows - sent)),
        scratch_shapes=[pltpu.VMEM((2 * rows, TILE), jnp.bfloat16)],
        compiler_params=pltpu.CompilerParams(vmem_limit_bytes=48 * MIB),
        cost_estimate=SMALL,
    )(rows_mat, panel, weights, plan.select)


def assemble(base, keep, recv, spare, plan, child_block, picks=None):
    rows, order = base.shape
    sent = recv.shape[0]
    children = order // 2 // TILE
    per = recv.shape[1] // TILE
    target = lambda n: child_block(n % per) + children * (n // per)
    fixed = lambda shape: pl.BlockSpec(shape, lambda n, _: (0, 0))
    child = lambda count: pl.BlockSpec((count, TILE), lambda n, _: (0, n % per))
    mapped = pl.BlockSpec((1, TILE), lambda n, _: (0, child_block(n % per)))
    wide = lambda count: pl.BlockSpec((count, TILE), lambda n, _: (0, n))
    in_specs = [
        pl.BlockSpec((rows, TILE), lambda n, _: (0, target(n))),
        child(2 * rows),
        child(sent),
        pl.BlockSpec((rows - sent, TILE), lambda n, flag: (0, n % per * flag[0])),
        fixed(plan.place.shape),
        fixed(plan.place_spare.shape),
        mapped,
        mapped,
    ]
    args = [base, keep, recv, spare, plan.place, plan.place_spare, plan.own_map[None], plan.other_map[None]]
    width = 2 * per * TILE
    if picks is None:
        out_shape = jax.ShapeDtypeStruct((rows, width), jnp.float32)
        out_specs = wide(rows)
    else:
        in_specs.append(fixed((2 * rows, rows)))
        args.append(picks.select)
        out_shape = pick_shapes(rows, picks.sent, width)
        out_specs = (wide(2 * rows), wide(picks.sent), wide(rows - picks.sent))
    return pl.pallas_call(
        functools.partial(assemble_kernel, picks is not None, target),
        out_shape=out_shape,
        grid_spec=pltpu.PrefetchScalarGridSpec(
            num_scalar_prefetch=1,
            grid=(2 * per,),
            in_specs=in_specs,
            out_specs=out_specs,
            scratch_shapes=[pltpu.VMEM((rows, TILE), jnp.float32)],
        ),
        compiler_params=pltpu.CompilerParams(vmem_limit_bytes=48 * MIB),
        cost_estimate=SMALL,
    )(plan.overflow, *args)


def finish_kernel(low, high, pair, where_ref, rows_ref, *refs):
    first_refs, second_refs, weights_ref = refs[:2], refs[2:4], refs[4]
    out_ref, split_ref = refs[-2:]
    n = pl.program_id(0)

    @pl.when(n == 0)
    def _():
        split_ref[...] = stacked(weights_ref[...])

    rows = rows_ref.shape[0]
    row_ids = where_ref[0] + lax.broadcasted_iota(jnp.int32, (rows, 1), 0)
    col_ids = pair(n) * 2 * TILE + lax.broadcasted_iota(jnp.int32, (1, 2 * TILE), 1)
    outside = lambda ids: (ids < low) | (ids >= high)
    turned = where_ref[1] % 2 != 0
    even = jnp.where(turned, first_refs[1][...], first_refs[0][...])
    odd = jnp.where(turned, first_refs[0][...], first_refs[1][...])
    panel = jnp.concatenate(
        [jnp.concatenate([even, odd], 0), jnp.concatenate([ref[...] for ref in second_refs], 0)], 1
    )
    change = low_rank(split_ref, panel)
    out_ref[...] = jnp.where(outside(row_ids) & outside(col_ids), rows_ref[...] - change, 0.0)


def finish(before, first, second, second_at, weights, scalars, pair, out=None):
    rows = before.shape[0]
    order = 2 * before.shape[1]
    low, high = order - 3 * TILE, order - TILE
    count = order // (4 * TILE)
    layers = order // TILE // 8
    wide = lambda index: pl.BlockSpec((rows, 2 * TILE), index)
    piece = pl.BlockSpec((TILE, TILE), lambda n, s: (place_of((2 * pair(n)) ^ s[1], layers), 0))
    later = lambda side: pl.BlockSpec((TILE, TILE), lambda n, s: (second_at(2 * pair(n) + side, s[1]), 0))
    in_specs = [wide(lambda n, _: (0, n)), piece, piece, later(0), later(1), wide(lambda n, _: (0, 0))]
    args = [before, *first, second, second, weights]
    if out is not None:
        in_specs.append(pl.BlockSpec(memory_space=pl.ANY))
        args.append(out)
    return pl.pallas_call(
        functools.partial(finish_kernel, low, high, pair),
        out_shape=jax.ShapeDtypeStruct((rows, order), jnp.float32),
        grid_spec=pltpu.PrefetchScalarGridSpec(
            num_scalar_prefetch=1,
            grid=(count,),
            in_specs=in_specs,
            out_specs=wide(lambda n, _: (0, pair(n))),
            scratch_shapes=[pltpu.VMEM((2 * rows, 2 * TILE), jnp.bfloat16)],
        ),
        input_output_aliases={} if out is None else {7: 0},
        compiler_params=pltpu.CompilerParams(vmem_limit_bytes=48 * MIB),
        cost_estimate=SMALL,
    )(scalars, *args)


def product(left, right, precision=HIGHEST):
    return jnp.dot(left, right, precision=precision, preferred_element_type=jnp.float32)


def product_nt(left, right, precision=HIGHEST):
    return lax.dot_general(left, right, NT, precision=precision, preferred_element_type=jnp.float32)


def swap(value, mask):
    pairs = [(source, source ^ mask) for source in range(lax.axis_size("cube"))]
    return lax.ppermute(value, "cube", pairs)


def group_gather(value, group):
    size = lax.axis_size("cube")
    groups = [[g * group + i for i in range(group)] for g in range(size // group)]
    return lax.all_gather(value, "cube", axis=0, tiled=True, axis_index_groups=groups)


def one_hot(positions, count):
    return (positions[None, :] == jnp.arange(count, dtype=jnp.int32)[:, None]).astype(jnp.float32)


def column_targets(front_map):
    order = front_map.shape[0]
    ids = jnp.arange(order, dtype=jnp.int32)
    gone = (ids >= order - 2 * TILE) & (ids < order - TILE)
    return jnp.where(gone, -1, front_map)


def leaving(front_map, front, group, rows):
    target = (front_map // rows) // group
    return (front_map >= 0) & (target != front % 2)


class Plan:
    def __init__(self, maps, group, rows):
        me = lax.axis_index("cube")
        front = me // group
        block = me % group
        side = front % 2
        targets = jax.vmap(column_targets)(maps)
        self.sent = (rows * 19 // 32 + 7) // 8 * 8
        fronts = jnp.arange(maps.shape[0], dtype=jnp.int32)
        leaves = leaving(targets, fronts[:, None], group, rows).reshape(maps.shape[0], group, rows)
        most = jnp.max(jnp.sum(leaves.astype(jnp.int32), -1))
        self.overflow = (most > self.sent).astype(jnp.int32).reshape(1)
        self.own_map = lax.dynamic_index_in_dim(targets, front, 0, keepdims=False)
        self.other_map = lax.dynamic_index_in_dim(targets, front ^ 1, 0, keepdims=False)
        own = lax.dynamic_slice_in_dim(self.own_map, block * rows, rows, 0)
        other = lax.dynamic_slice_in_dim(self.other_map, block * rows, rows, 0)
        here = (block + group * side) * rows
        there = (block + group * (1 - side)) * rows
        self.keep = one_hot(own - here, rows)
        self.give = one_hot(own - there, rows)
        ids = jnp.arange(rows, dtype=jnp.int32)
        upper = (ids[:, None] <= ids[None, :]).astype(jnp.bfloat16)
        leaves = (own >= there) & (own < there + rows)
        comes = (other >= here) & (other < here + rows)
        flags = jnp.stack([leaves, comes]).astype(jnp.bfloat16)
        ranks = jnp.dot(flags, upper, preferred_element_type=jnp.float32).astype(jnp.int32) - 1
        send = one_hot(jnp.where(leaves, ranks[0], -1), rows)
        self.select = jnp.concatenate([self.keep, send], 0).astype(jnp.bfloat16)
        taken = one_hot(jnp.where(comes, ranks[1], -1), rows).astype(jnp.bfloat16)
        slots = one_hot(other - here, rows).astype(jnp.bfloat16)
        place = lax.dot_general(slots, taken, NT, preferred_element_type=jnp.float32).astype(jnp.bfloat16)
        fill = lambda part: jnp.pad(part, ((0, 0), (0, -part.shape[1] % 16)))
        self.place = fill(place[:, : self.sent])
        self.place_spare = fill(place[:, self.sent :])


def spread_block(block, group, owner_low, rows):
    size = lax.axis_size("cube")
    me = lax.axis_index("cube")
    holders = max(1, TILE // rows)
    has = {d for d in range(size) if owner_low <= d % group < owner_low + holders}
    inside = (me % group >= owner_low) & (me % group < owner_low + holders)
    block = jnp.where(inside, block, 0.0)
    mask = group // 2
    while mask >= holders:
        pairs = [(d, d ^ mask) for d in sorted(has)]
        block = block + lax.ppermute(block, "cube", pairs)
        has |= {d ^ mask for d in has}
        mask //= 2
    return block


def whole_block(part, rows):
    if rows >= TILE:
        return part
    return group_gather(part, TILE // rows)


def place_of(turned, layers):
    span = layers // 2
    layer, y, x = turned // 8, turned // 4 % 2, turned // 2 % 2
    lower = (2 * y + x) * span + layer
    upper = (4 + 2 * x + y) * span + layer - span
    return jnp.where(layer < span, lower, upper)


def cross_planes(block):
    layers = lax.axis_size("cube") // 8
    if block.shape[0] != TILE:
        return [block]
    return [block] + [swap(block, 8 * layer) for layer in range(1, layers)]


def gather_second(stack):
    layers = lax.axis_size("cube") // 8
    if stack[0].shape[0] != TILE:
        return lax.all_gather(stack[0], "cube", axis=0, tiled=True), lambda cb, me: cb
    return group_gather(jnp.concatenate(stack, 0), 8), lambda cb, me: cb % 8 * layers + (cb // 8 ^ me // 8)


def gather_first(block, after):
    size = lax.axis_size("cube")
    layers = size // 8
    rows = block.shape[0]
    if rows != TILE:
        whole = lax.all_gather(block, "cube", axis=0, tiled=True)
        order = whole.shape[0]
        layers = order // TILE // 8
        spots = [0] * (4 * layers)
        for m in range(4 * layers):
            layer, y, x = m // 4, m // 2 % 2, m % 2
            span = layers // 2
            spot = (2 * y + x) * span + layer if layer < span else (4 + 2 * x + y) * span + layer - span
            spots[spot] = m
        blocks = whole.reshape(order // TILE, TILE, TILE)
        sides = [jnp.concatenate([blocks[2 * m + side] for m in spots], 0) for side in range(2)]
        return sides, jnp.int32(0)
    me = lax.axis_index("cube")
    stack = cross_planes(block)
    stack, after = lax.optimization_barrier((stack, after))
    one = jnp.concatenate(stack[: layers // 2], 0)
    two = jnp.concatenate(stack[layers // 2 :], 0)
    one = jnp.concatenate([one, swap(one, 2)], 0)
    two = jnp.concatenate([two, swap(two, 4)], 0)
    even = jnp.concatenate([one, swap(one, 4), two, swap(two, 2)], 0)
    odd = swap(even, 1)
    return (even, odd), me


def local(gfront, cfront, rfront, gmap, cmap):
    devices = lax.axis_size("cube")
    me = lax.axis_index("cube")
    quarter = devices // 4
    half = devices // 2
    rows = gfront.shape[0]
    order_g, order_c, order_r = gfront.shape[1], cfront.shape[1], rfront.shape[1]
    g_low, c_low = order_g - 2 * TILE, order_c - 2 * TILE
    r_low = order_r - 3 * TILE
    r_high = r_low + TILE

    def exchange(send, spare, plan, mask):
        rest = lax.cond(plan.overflow[0] != 0, lambda part: swap(part, mask), jnp.zeros_like, spare)
        return swap(send, mask), rest

    own_g = gfront[:, g_low : g_low + TILE]
    own_c = cfront[:, c_low : c_low + TILE]
    own_second = rfront[:, r_high : r_high + TILE]
    panel_g = group_gather(own_g, quarter)
    panel_c = group_gather(own_c, half)
    crossed = cross_planes(own_second)
    inverse_g = inverse_factors(panel_g[g_low : g_low + TILE][None])[0]
    inverse_c = spread_block(inverse_factors(whole_block(own_c, rows)[None])[0], half, c_low // rows, rows)
    root_2 = jnp.stack([whole_block(rfront[:, low : low + TILE], rows) for low in (r_low, r_high)])
    root_2 = spread_block(root_2, devices, r_high // rows, rows)
    plan_g = Plan(gmap, quarter, rows)
    plan_c = Plan(cmap, half, rows)

    gfactor = product_nt(own_g, inverse_g)
    weights_g = product(gfactor, inverse_g)

    g_keep, g_send, g_spare = update_and_pick(gfront, panel_g, weights_g, plan_g)
    panel_c, g_send, inverse_c = lax.optimization_barrier((panel_c, g_send, inverse_c))
    second, second_at = gather_second(crossed)
    cfactor = product_nt(own_c, inverse_c)
    weights_c = product(cfactor, inverse_c)

    g_edge = gfront[:, g_low - TILE : g_low] - product_nt(weights_g, panel_g[g_low - TILE : g_low])
    edge_map = plan_g.own_map[g_low - TILE : g_low]
    g_edge = product_nt(g_edge, one_hot(edge_map - (c_low - TILE), TILE))
    c_edge = cfront[:, c_low - TILE : c_low] - product_nt(weights_c, panel_c[c_low - TILE : c_low])
    c_edge = c_edge + product(plan_g.keep, g_edge) + swap(product(plan_g.give, g_edge), quarter)
    g_recv, g_rest = exchange(g_send, g_spare, plan_g, quarter)
    c_edge, g_recv = lax.optimization_barrier((c_edge, g_recv))
    edge_map = plan_c.own_map[c_low - TILE : c_low]
    c_edge = product_nt(c_edge, one_hot(edge_map - r_low, TILE))
    r_edge = rfront[:, r_low : r_low + TILE] + product(plan_c.keep, c_edge)
    r_come = swap(product(plan_c.give, c_edge), half)
    c_base = cfront - product_nt(weights_c, panel_c, HIGH)
    blocks_g = order_g // TILE
    per = blocks_g // 2
    child_of_c = lambda part: lambda p: part * per + p
    child_of_r = lambda part: lambda p: part * per + p % per + blocks_g * (p // per)
    pieces, sends = [], []
    for part in range(2):
        low, high = part * per * TILE, (part + 1) * per * TILE
        g_part = [value[:, low:high] for value in (g_keep, g_recv, g_rest)]
        keep, send, spare = assemble(c_base, *g_part, plan_g, child_of_c(part), plan_c)
        sends.append(send)
        pieces.append((keep, *exchange(send, spare, plan_c, half)))
    r_come, sends, root_2 = lax.optimization_barrier((r_come, sends, root_2))
    r_edge = r_edge + r_come
    root_1 = spread_block(whole_block(r_edge, rows), devices, r_low // rows, rows)
    first, turn = gather_first(r_edge, sends)
    plan_c.place, second = lax.optimization_barrier((plan_c.place, second))

    inv_11 = inverse_factors(root_1[None])[0]
    low_21 = product_nt(root_2[0], inv_11)
    inv_22 = inverse_factors((root_2[1] - product_nt(low_21, low_21))[None])[0]
    inv_21 = -product(inv_22, product(low_21, inv_11))
    factor_1 = product_nt(r_edge, inv_11)
    factor_2 = product_nt(r_edge, inv_21) + product_nt(own_second, inv_22)
    weights_1 = product(factor_1, inv_11) + product(factor_2, inv_21)
    weights_2 = product(factor_2, inv_22)
    row_ids = me * rows + jnp.arange(rows, dtype=jnp.int32)
    above = (row_ids >= r_low) & (row_ids < r_high)
    factor_2 = jnp.where(above[:, None], 0.0, factor_2)
    rfactor = jnp.concatenate([factor_1, factor_2], 1)
    pairs = per // 2

    pair_of = lambda part: lambda n: n % pairs + 2 * pairs * (n // pairs) + pairs * part
    scalars = jnp.stack([me * rows, turn]).astype(jnp.int32)
    weights_r = jnp.concatenate([weights_1, weights_2], 1)
    rschur = None
    for part, (keep, recv, rest) in enumerate(pieces):
        if part:
            rschur, recv = lax.optimization_barrier((rschur, recv))
        before = assemble(rfront, keep, recv, rest, plan_c, child_of_r(part))
        rschur = finish(before, first, second, second_at, weights_r, scalars, pair_of(part), rschur)
    return (gfactor, cfactor, rfactor, rschur)


def solution(mesh):
    placed = (P("cube", None), P("cube", None), P("cube", None), P(), P())
    return jax.shard_map(
        local,
        mesh=mesh,
        in_specs=placed,
        out_specs=(P("cube", None), P("cube", None), P("cube", None), P("cube", None)),
        check_vma=False,
    )
```

```python
import functools

import jax
import jax.numpy as jnp
from jax import lax
from jax.experimental import pallas as pl
from jax.experimental.pallas import tpu as pltpu
from jax.sharding import PartitionSpec as P

TILE = 256
STRIP = 32
SUB = 8
LANES = 128
HIGH = lax.Precision.HIGH
HIGHEST = lax.Precision.HIGHEST
NT = (((1,), (1,)), ((), ()))
MIB = 1024 * 1024


def lasting(microseconds):
    return pl.CostEstimate(flops=1, bytes_accessed=int(microseconds * 3_500_000), transcendentals=0)


def widen(column, width):
    return jnp.concatenate([column] * (width // LANES), 1)


def factor_strip(strip, base):
    width = strip[0].shape[1]
    sub_ids = lax.broadcasted_iota(jnp.int32, (SUB, 1), 0)
    count = len(strip)
    for p in range(count):
        first = base + p * SUB
        cols = [
            [jnp.broadcast_to(strip[q][:, first + j : first + j + 1], (SUB, LANES)) for j in range(SUB)]
            for q in range(p, count)
        ]
        for j in range(SUB):
            pivot = cols[0][j][j : j + 1, :]
            inv = lax.rsqrt(pivot)
            inv = inv * (1.5 - 0.5 * pivot * inv * inv)
            unit = strip[p][j : j + 1, :] * widen(inv, width)
            scaled = [col[j] * inv for col in cols]
            below = jnp.where(sub_ids > j, scaled[0], 0.0)
            strip[p] = jnp.where(sub_ids == j, unit, strip[p] - widen(below, width) * unit)
            for q in range(p + 1, count):
                strip[q] = strip[q] - widen(scaled[q - p], width) * unit
            for m in range(j + 1, SUB):
                head = scaled[0][m : m + 1, :]
                for q in range(p, count):
                    cols[q - p][m] = cols[q - p][m] - scaled[q - p] * head
    return jnp.concatenate(strip, 0)


def inverse_kernel(count, blocks_ref, inverse_ref, work):
    row_ids = lax.broadcasted_iota(jnp.int32, (TILE, TILE), 0)
    col_ids = lax.broadcasted_iota(jnp.int32, (TILE, TILE), 1)
    for t in range(count):
        work[t, :, :TILE] = blocks_ref[t]
        work[t, :, TILE:] = (row_ids == col_ids).astype(jnp.float32)
    for low in range(0, TILE, STRIP):
        high = low + STRIP
        left = low // LANES * LANES
        right = TILE + (high + LANES - 1) // LANES * LANES
        done = []
        for t in range(count):
            strip = [work[t, low + SUB * q : low + SUB * (q + 1), left:right] for q in range(STRIP // SUB)]
            done.append(factor_strip(strip, low - left))
        for t in range(count):
            inverse_ref[t, low:high, : right - TILE] = done[t][:, TILE - left :]
            if right < 2 * TILE:
                inverse_ref[t, low:high, right - TILE :] = jnp.zeros((STRIP, 2 * TILE - right), jnp.float32)
            if high < TILE:
                rest = high // LANES * LANES
                update = lax.dot_general(
                    done[t][:, rest - left : TILE - left],
                    done[t],
                    (((0,), (0,)), ((), ())),
                    precision=HIGHEST,
                    preferred_element_type=jnp.float32,
                )
                work[t, high:, left:right] = work[t, high:, left:right] - update[high - rest :]


def inverse_factors(blocks):
    count = blocks.shape[0]
    return pl.pallas_call(
        functools.partial(inverse_kernel, count),
        out_shape=jax.ShapeDtypeStruct(blocks.shape, jnp.float32),
        in_specs=[pl.BlockSpec(memory_space=pltpu.VMEM)],
        out_specs=pl.BlockSpec(memory_space=pltpu.VMEM),
        scratch_shapes=[pltpu.VMEM((count, TILE, 2 * TILE), jnp.float32)],
        compiler_params=pltpu.CompilerParams(vmem_limit_bytes=16 * MIB),
        cost_estimate=lasting(10),
    )(blocks)


def halves(value):
    top = value.astype(jnp.bfloat16)
    return top, (value - top.astype(jnp.float32)).astype(jnp.bfloat16)


def dot_nt(left, right):
    return lax.dot_general(left, right, NT, preferred_element_type=jnp.float32)


def dot_nn(left, right):
    return jnp.dot(left, right, preferred_element_type=jnp.float32)


def pad_rows(value, count):
    short = count - value.shape[0]
    return value if short == 0 else jnp.concatenate([value, jnp.zeros((short, value.shape[1]), value.dtype)], 0)


def stacked(value):
    return jnp.concatenate(halves(value), 0)


def add_moved(total_ref, recv_ref, place_ref, hot):
    count = place_ref.shape[1]
    moved = dot_nt(stacked(pad_rows(recv_ref[...], count)), hot).astype(jnp.bfloat16)
    total_ref[...] += dot_nn(place_ref[...], moved[:count]) + dot_nn(place_ref[...], moved[count:])


def pick_rows(total, select_ref, outs):
    keep_ref, send_ref, spare_ref = outs
    rows = total.shape[0]
    sent = send_ref.shape[0]
    top, rest = halves(total)
    top = dot_nn(select_ref[...], top)
    rest = dot_nn(select_ref[...], rest)
    keep_ref[:rows] = top[:rows].astype(jnp.bfloat16)
    keep_ref[rows:] = rest[:rows].astype(jnp.bfloat16)
    both = top[rows:] + rest[rows:]
    send_ref[...] = both[:sent]
    spare_ref[...] = both[sent:]


def low_rank(weights_ref, panel):
    rows = weights_ref.shape[0] // 2
    top, rest = halves(panel)
    main = dot_nt(weights_ref[...], top)
    return main[:rows] + (main[rows:] + dot_nt(weights_ref[:rows], rest))


def update_kernel(rows_ref, panel_ref, weights_ref, select_ref, keep_ref, send_ref, spare_ref, split_ref):
    @pl.when(pl.program_id(0) == 0)
    def _():
        split_ref[...] = stacked(weights_ref[...])

    total = rows_ref[...] - low_rank(split_ref, panel_ref[...])
    pick_rows(total, select_ref, (keep_ref, send_ref, spare_ref))


def assemble_kernel(picks, target, flag, *refs):
    base_ref, keep_ref, recv_ref, spare_ref, place_ref, place_spare_ref, keep_map_ref, recv_map_ref = refs[:8]
    total_ref = refs[-1]
    rows = base_ref.shape[0]
    targets = target(pl.program_id(0)) * TILE + lax.broadcasted_iota(jnp.int32, (TILE, TILE), 0)
    keep_hot = jnp.where(keep_map_ref[...] == targets, 1.0, 0.0).astype(jnp.bfloat16)
    recv_hot = jnp.where(recv_map_ref[...] == targets, 1.0, 0.0).astype(jnp.bfloat16)
    kept = dot_nt(keep_ref[...], keep_hot)
    total_ref[...] = base_ref[...] + (kept[:rows] + kept[rows:])
    add_moved(total_ref, recv_ref, place_ref, recv_hot)

    @pl.when(flag[0] != 0)
    def _():
        add_moved(total_ref, spare_ref, place_spare_ref, recv_hot)

    if picks:
        pick_rows(total_ref[...], refs[8], refs[9:12])
    else:
        refs[8][...] = total_ref[...]


def pick_shapes(rows, sent, width):
    return (
        jax.ShapeDtypeStruct((2 * rows, width), jnp.bfloat16),
        jax.ShapeDtypeStruct((sent, width), jnp.float32),
        jax.ShapeDtypeStruct((rows - sent, width), jnp.float32),
    )


def update_and_pick(rows_mat, panel, weights, plan):
    rows, order = rows_mat.shape
    sent = plan.sent
    fixed = lambda shape: pl.BlockSpec(shape, lambda n: (0, 0))
    moving = lambda count: pl.BlockSpec((count, TILE), lambda n: (0, n))
    return pl.pallas_call(
        update_kernel,
        grid=(order // TILE,),
        out_shape=pick_shapes(rows, sent, order),
        in_specs=[
            moving(rows),
            pl.BlockSpec((TILE, TILE), lambda n: (n, 0)),
            fixed((rows, TILE)),
            fixed((2 * rows, rows)),
        ],
        out_specs=(moving(2 * rows), moving(sent), moving(rows - sent)),
        scratch_shapes=[pltpu.VMEM((2 * rows, TILE), jnp.bfloat16)],
        compiler_params=pltpu.CompilerParams(vmem_limit_bytes=48 * MIB),
        cost_estimate=lasting(order // TILE),
    )(rows_mat, panel, weights, plan.select)


def assemble(base, keep, recv, spare, plan, child_block, picks=None):
    rows, order = base.shape
    sent = recv.shape[0]
    children = order // 2 // TILE
    per = recv.shape[1] // TILE
    target = lambda n: child_block(n % per) + children * (n // per)
    fixed = lambda shape: pl.BlockSpec(shape, lambda n, _: (0, 0))
    child = lambda count: pl.BlockSpec((count, TILE), lambda n, _: (0, n % per))
    mapped = pl.BlockSpec((1, TILE), lambda n, _: (0, child_block(n % per)))
    wide = lambda count: pl.BlockSpec((count, TILE), lambda n, _: (0, n))
    in_specs = [
        pl.BlockSpec((rows, TILE), lambda n, _: (0, target(n))),
        child(2 * rows),
        child(sent),
        pl.BlockSpec((rows - sent, TILE), lambda n, flag: (0, n % per * flag[0])),
        fixed(plan.place.shape),
        fixed(plan.place_spare.shape),
        mapped,
        mapped,
    ]
    args = [base, keep, recv, spare, plan.place, plan.place_spare, plan.own_map[None], plan.other_map[None]]
    width = 2 * per * TILE
    if picks is None:
        out_shape = jax.ShapeDtypeStruct((rows, width), jnp.float32)
        out_specs = wide(rows)
    else:
        in_specs.append(fixed((2 * rows, rows)))
        args.append(picks.select)
        out_shape = pick_shapes(rows, picks.sent, width)
        out_specs = (wide(2 * rows), wide(picks.sent), wide(rows - picks.sent))
    return pl.pallas_call(
        functools.partial(assemble_kernel, picks is not None, target),
        out_shape=out_shape,
        grid_spec=pltpu.PrefetchScalarGridSpec(
            num_scalar_prefetch=1,
            grid=(2 * per,),
            in_specs=in_specs,
            out_specs=out_specs,
            scratch_shapes=[pltpu.VMEM((rows, TILE), jnp.float32)],
        ),
        compiler_params=pltpu.CompilerParams(vmem_limit_bytes=48 * MIB),
        cost_estimate=lasting(2 * per),
    )(plan.overflow, *args)


def finish_kernel(low, high, pair, where_ref, rows_ref, *refs):
    first_refs, second_refs, weights_ref = refs[:2], refs[2:4], refs[4]
    out_ref, split_ref = refs[-2:]
    n = pl.program_id(0)

    @pl.when(n == 0)
    def _():
        split_ref[...] = stacked(weights_ref[...])

    rows = rows_ref.shape[0]
    row_ids = where_ref[0] + lax.broadcasted_iota(jnp.int32, (rows, 1), 0)
    col_ids = pair(n) * 2 * TILE + lax.broadcasted_iota(jnp.int32, (1, 2 * TILE), 1)
    outside = lambda ids: (ids < low) | (ids >= high)
    turned = where_ref[1] % 2 != 0
    even = jnp.where(turned, first_refs[1][...], first_refs[0][...])
    odd = jnp.where(turned, first_refs[0][...], first_refs[1][...])
    panel = jnp.concatenate(
        [jnp.concatenate([even, odd], 0), jnp.concatenate([ref[...] for ref in second_refs], 0)], 1
    )
    change = low_rank(split_ref, panel)
    out_ref[...] = jnp.where(outside(row_ids) & outside(col_ids), rows_ref[...] - change, 0.0)


def finish(before, first, second, second_at, weights, scalars, pair, out=None):
    rows = before.shape[0]
    order = 2 * before.shape[1]
    low, high = order - 3 * TILE, order - TILE
    count = order // (4 * TILE)
    layers = order // TILE // 8
    wide = lambda index: pl.BlockSpec((rows, 2 * TILE), index)
    piece = pl.BlockSpec((TILE, TILE), lambda n, s: (place_of((2 * pair(n)) ^ s[1], layers), 0))
    later = lambda side: pl.BlockSpec((TILE, TILE), lambda n, s: (second_at(2 * pair(n) + side, s[1]), 0))
    in_specs = [wide(lambda n, _: (0, n)), piece, piece, later(0), later(1), wide(lambda n, _: (0, 0))]
    args = [before, *first, second, second, weights]
    if out is not None:
        in_specs.append(pl.BlockSpec(memory_space=pl.ANY))
        args.append(out)
    return pl.pallas_call(
        functools.partial(finish_kernel, low, high, pair),
        out_shape=jax.ShapeDtypeStruct((rows, order), jnp.float32),
        grid_spec=pltpu.PrefetchScalarGridSpec(
            num_scalar_prefetch=1,
            grid=(count,),
            in_specs=in_specs,
            out_specs=wide(lambda n, _: (0, pair(n))),
            scratch_shapes=[pltpu.VMEM((2 * rows, 2 * TILE), jnp.bfloat16)],
        ),
        input_output_aliases={} if out is None else {7: 0},
        compiler_params=pltpu.CompilerParams(vmem_limit_bytes=48 * MIB),
        cost_estimate=lasting(count),
    )(scalars, *args)


def product(left, right, precision=HIGHEST):
    return jnp.dot(left, right, precision=precision, preferred_element_type=jnp.float32)


def product_nt(left, right, precision=HIGHEST):
    return lax.dot_general(left, right, NT, precision=precision, preferred_element_type=jnp.float32)


def swap(value, mask):
    pairs = [(source, source ^ mask) for source in range(lax.axis_size("cube"))]
    return lax.ppermute(value, "cube", pairs)


def group_gather(value, group):
    size = lax.axis_size("cube")
    groups = [[g * group + i for i in range(group)] for g in range(size // group)]
    return lax.all_gather(value, "cube", axis=0, tiled=True, axis_index_groups=groups)


def one_hot(positions, count):
    return (positions[None, :] == jnp.arange(count, dtype=jnp.int32)[:, None]).astype(jnp.float32)


def column_targets(front_map):
    order = front_map.shape[0]
    ids = jnp.arange(order, dtype=jnp.int32)
    gone = (ids >= order - 2 * TILE) & (ids < order - TILE)
    return jnp.where(gone, -1, front_map)


def leaving(front_map, front, group, rows):
    target = (front_map // rows) // group
    return (front_map >= 0) & (target != front % 2)


class Plan:
    def __init__(self, maps, group, rows):
        me = lax.axis_index("cube")
        front = me // group
        block = me % group
        side = front % 2
        targets = jax.vmap(column_targets)(maps)
        self.sent = (rows * 19 // 32 + 7) // 8 * 8
        fronts = jnp.arange(maps.shape[0], dtype=jnp.int32)
        leaves = leaving(targets, fronts[:, None], group, rows).reshape(maps.shape[0], group, rows)
        most = jnp.max(jnp.sum(leaves.astype(jnp.int32), -1))
        self.overflow = (most > self.sent).astype(jnp.int32).reshape(1)
        self.own_map = lax.dynamic_index_in_dim(targets, front, 0, keepdims=False)
        self.other_map = lax.dynamic_index_in_dim(targets, front ^ 1, 0, keepdims=False)
        own = lax.dynamic_slice_in_dim(self.own_map, block * rows, rows, 0)
        other = lax.dynamic_slice_in_dim(self.other_map, block * rows, rows, 0)
        here = (block + group * side) * rows
        there = (block + group * (1 - side)) * rows
        self.keep = one_hot(own - here, rows)
        self.give = one_hot(own - there, rows)
        ids = jnp.arange(rows, dtype=jnp.int32)
        upper = (ids[:, None] <= ids[None, :]).astype(jnp.bfloat16)
        leaves = (own >= there) & (own < there + rows)
        comes = (other >= here) & (other < here + rows)
        flags = jnp.stack([leaves, comes]).astype(jnp.bfloat16)
        ranks = jnp.dot(flags, upper, preferred_element_type=jnp.float32).astype(jnp.int32) - 1
        send = one_hot(jnp.where(leaves, ranks[0], -1), rows)
        self.select = jnp.concatenate([self.keep, send], 0).astype(jnp.bfloat16)
        taken = one_hot(jnp.where(comes, ranks[1], -1), rows).astype(jnp.bfloat16)
        slots = one_hot(other - here, rows).astype(jnp.bfloat16)
        place = lax.dot_general(slots, taken, NT, preferred_element_type=jnp.float32).astype(jnp.bfloat16)
        fill = lambda part: jnp.pad(part, ((0, 0), (0, -part.shape[1] % 16)))
        self.place = fill(place[:, : self.sent])
        self.place_spare = fill(place[:, self.sent :])


def spread_block(block, group, owner_low, rows):
    size = lax.axis_size("cube")
    me = lax.axis_index("cube")
    holders = max(1, TILE // rows)
    has = {d for d in range(size) if owner_low <= d % group < owner_low + holders}
    inside = (me % group >= owner_low) & (me % group < owner_low + holders)
    block = jnp.where(inside, block, 0.0)
    mask = group // 2
    while mask >= holders:
        pairs = [(d, d ^ mask) for d in sorted(has)]
        block = block + lax.ppermute(block, "cube", pairs)
        has |= {d ^ mask for d in has}
        mask //= 2
    return block


def whole_block(part, rows):
    if rows >= TILE:
        return part
    return group_gather(part, TILE // rows)


def place_of(turned, layers):
    span = layers // 2
    layer, y, x = turned // 8, turned // 4 % 2, turned // 2 % 2
    lower = (2 * y + x) * span + layer
    upper = (4 + 2 * x + y) * span + layer - span
    return jnp.where(layer < span, lower, upper)


def cross_planes(block):
    layers = lax.axis_size("cube") // 8
    if block.shape[0] != TILE:
        return [block]
    return [block] + [swap(block, 8 * layer) for layer in range(1, layers)]


def gather_second(stack):
    layers = lax.axis_size("cube") // 8
    if stack[0].shape[0] != TILE:
        return lax.all_gather(stack[0], "cube", axis=0, tiled=True), lambda cb, me: cb
    return group_gather(jnp.concatenate(stack, 0), 8), lambda cb, me: cb % 8 * layers + (cb // 8 ^ me // 8)


def gather_first(block, after):
    size = lax.axis_size("cube")
    layers = size // 8
    rows = block.shape[0]
    if rows != TILE:
        whole = lax.all_gather(block, "cube", axis=0, tiled=True)
        order = whole.shape[0]
        layers = order // TILE // 8
        spots = [0] * (4 * layers)
        for m in range(4 * layers):
            layer, y, x = m // 4, m // 2 % 2, m % 2
            span = layers // 2
            spot = (2 * y + x) * span + layer if layer < span else (4 + 2 * x + y) * span + layer - span
            spots[spot] = m
        blocks = whole.reshape(order // TILE, TILE, TILE)
        sides = [jnp.concatenate([blocks[2 * m + side] for m in spots], 0) for side in range(2)]
        return sides, jnp.int32(0), after
    me = lax.axis_index("cube")
    stack = cross_planes(block)
    stack, after = lax.optimization_barrier((stack, after))
    one = jnp.concatenate(stack[: layers // 2], 0)
    two = jnp.concatenate(stack[layers // 2 :], 0)
    one = jnp.concatenate([one, swap(one, 2)], 0)
    two = jnp.concatenate([two, swap(two, 4)], 0)
    even = jnp.concatenate([one, swap(one, 4), two, swap(two, 2)], 0)
    odd = swap(even, 1)
    return (even, odd), me, after


def local(gfront, cfront, rfront, gmap, cmap):
    devices = lax.axis_size("cube")
    me = lax.axis_index("cube")
    quarter = devices // 4
    half = devices // 2
    rows = gfront.shape[0]
    order_g, order_c, order_r = gfront.shape[1], cfront.shape[1], rfront.shape[1]
    g_low, c_low = order_g - 2 * TILE, order_c - 2 * TILE
    r_low = order_r - 3 * TILE
    r_high = r_low + TILE

    def exchange(send, spare, plan, mask):
        rest = lax.cond(plan.overflow[0] != 0, lambda part: swap(part, mask), jnp.zeros_like, spare)
        return swap(send, mask), rest

    own_g = gfront[:, g_low : g_low + TILE]
    own_c = cfront[:, c_low : c_low + TILE]
    own_second = rfront[:, r_high : r_high + TILE]
    panel_g = group_gather(own_g, quarter)
    panel_c = group_gather(own_c, half)
    crossed = cross_planes(own_second)
    inverse_g = inverse_factors(panel_g[g_low : g_low + TILE][None])[0]
    root_2 = jnp.stack([whole_block(rfront[:, low : low + TILE], rows) for low in (r_low, r_high)])
    plan_g = Plan(gmap, quarter, rows)
    plan_c = Plan(cmap, half, rows)

    gfactor = product_nt(own_g, inverse_g)
    weights_g = product(gfactor, inverse_g)

    g_keep, g_send, g_spare = update_and_pick(gfront, panel_g, weights_g, plan_g)
    panel_c, g_send, root_2 = lax.optimization_barrier((panel_c, g_send, root_2))
    root_2 = spread_block(root_2, devices, r_high // rows, rows)
    inverse_c = inverse_factors(panel_c[c_low : c_low + TILE][None])[0]
    second, second_at = gather_second(crossed)
    cfactor = product_nt(own_c, inverse_c)
    weights_c = product(cfactor, inverse_c)

    g_edge = gfront[:, g_low - TILE : g_low] - product_nt(weights_g, panel_g[g_low - TILE : g_low])
    edge_map = plan_g.own_map[g_low - TILE : g_low]
    g_edge = product_nt(g_edge, one_hot(edge_map - (c_low - TILE), TILE))
    c_edge = cfront[:, c_low - TILE : c_low] - product_nt(weights_c, panel_c[c_low - TILE : c_low])
    c_edge = c_edge + product(plan_g.keep, g_edge) + swap(product(plan_g.give, g_edge), quarter)
    g_recv, g_rest = exchange(g_send, g_spare, plan_g, quarter)
    c_edge, g_recv = lax.optimization_barrier((c_edge, g_recv))
    edge_map = plan_c.own_map[c_low - TILE : c_low]
    c_edge = product_nt(c_edge, one_hot(edge_map - r_low, TILE))
    r_edge = rfront[:, r_low : r_low + TILE] + product(plan_c.keep, c_edge)
    r_come = swap(product(plan_c.give, c_edge), half)
    c_base = cfront - product_nt(weights_c, panel_c, HIGH)
    blocks_g = order_g // TILE
    per = blocks_g // 2
    child_of_c = lambda part: lambda p: part * per + p
    child_of_r = lambda part: lambda p: part * per + p % per + blocks_g * (p // per)
    pieces, sends = [], []
    for part in range(2):
        low, high = part * per * TILE, (part + 1) * per * TILE
        g_part = [value[:, low:high] for value in (g_keep, g_recv, g_rest)]
        keep, send, spare = assemble(c_base, *g_part, plan_g, child_of_c(part), plan_c)
        sends.append(send)
        pieces.append((keep, *exchange(send, spare, plan_c, half)))
    r_come, sends = lax.optimization_barrier((r_come, sends))
    r_edge = r_edge + r_come
    root_1 = spread_block(whole_block(r_edge, rows), devices, r_low // rows, rows)
    keep, recv, rest = pieces[0]
    first, turn, (recv, root_1) = gather_first(r_edge, (recv, root_1))
    pieces[0] = (keep, recv, rest)
    plan_c.place, second = lax.optimization_barrier((plan_c.place, second))

    inv_11 = inverse_factors(root_1[None])[0]
    low_21 = product_nt(root_2[0], inv_11)
    inv_22 = inverse_factors((root_2[1] - product_nt(low_21, low_21))[None])[0]
    inv_21 = -product(inv_22, product(low_21, inv_11))
    factor_1 = product_nt(r_edge, inv_11)
    factor_2 = product_nt(r_edge, inv_21) + product_nt(own_second, inv_22)
    weights_1 = product(factor_1, inv_11) + product(factor_2, inv_21)
    weights_2 = product(factor_2, inv_22)
    row_ids = me * rows + jnp.arange(rows, dtype=jnp.int32)
    above = (row_ids >= r_low) & (row_ids < r_high)
    factor_2 = jnp.where(above[:, None], 0.0, factor_2)
    rfactor = jnp.concatenate([factor_1, factor_2], 1)
    pairs = per // 2

    pair_of = lambda part: lambda n: n % pairs + 2 * pairs * (n // pairs) + pairs * part
    scalars = jnp.stack([me * rows, turn]).astype(jnp.int32)
    weights_r = jnp.concatenate([weights_1, weights_2], 1)
    rschur = None
    for part, (keep, recv, rest) in enumerate(pieces):
        if part:
            rschur, recv = lax.optimization_barrier((rschur, recv))
        before = assemble(rfront, keep, recv, rest, plan_c, child_of_r(part))
        rschur = finish(before, first, second, second_at, weights_r, scalars, pair_of(part), rschur)
    return (gfactor, cfactor, rfactor, rschur)


def solution(mesh):
    placed = (P("cube", None), P("cube", None), P("cube", None), P(), P())
    return jax.shard_map(
        local,
        mesh=mesh,
        in_specs=placed,
        out_specs=(P("cube", None), P("cube", None), P("cube", None), P("cube", None)),
        check_vma=False,
    )
```

```python
import functools

import jax
import jax.numpy as jnp
from jax import lax
from jax.experimental import pallas as pl
from jax.experimental.pallas import tpu as pltpu
from jax.sharding import PartitionSpec as P

TILE = 256
STRIP = 32
SUB = 8
LANES = 128
HIGH = lax.Precision.HIGH
HIGHEST = lax.Precision.HIGHEST
NT = (((1,), (1,)), ((), ()))
MIB = 1024 * 1024


def lasting(microseconds):
    return pl.CostEstimate(flops=1, bytes_accessed=int(microseconds * 3_500_000), transcendentals=0)


def widen(column, width):
    return jnp.concatenate([column] * (width // LANES), 1)


def factor_strip(strip, base):
    width = strip[0].shape[1]
    sub_ids = lax.broadcasted_iota(jnp.int32, (SUB, 1), 0)
    count = len(strip)
    for p in range(count):
        first = base + p * SUB
        cols = [
            [jnp.broadcast_to(strip[q][:, first + j : first + j + 1], (SUB, LANES)) for j in range(SUB)]
            for q in range(p, count)
        ]
        for j in range(SUB):
            pivot = cols[0][j][j : j + 1, :]
            inv = lax.rsqrt(pivot)
            inv = inv * (1.5 - 0.5 * pivot * inv * inv)
            unit = strip[p][j : j + 1, :] * widen(inv, width)
            scaled = [col[j] * inv for col in cols]
            below = jnp.where(sub_ids > j, scaled[0], 0.0)
            strip[p] = jnp.where(sub_ids == j, unit, strip[p] - widen(below, width) * unit)
            for q in range(p + 1, count):
                strip[q] = strip[q] - widen(scaled[q - p], width) * unit
            for m in range(j + 1, SUB):
                head = scaled[0][m : m + 1, :]
                for q in range(p, count):
                    cols[q - p][m] = cols[q - p][m] - scaled[q - p] * head
    return jnp.concatenate(strip, 0)


def inverse_kernel(count, blocks_ref, inverse_ref, work):
    row_ids = lax.broadcasted_iota(jnp.int32, (TILE, TILE), 0)
    col_ids = lax.broadcasted_iota(jnp.int32, (TILE, TILE), 1)
    for t in range(count):
        work[t, :, :TILE] = blocks_ref[t]
        work[t, :, TILE:] = (row_ids == col_ids).astype(jnp.float32)
    for low in range(0, TILE, STRIP):
        high = low + STRIP
        left = low // LANES * LANES
        right = TILE + (high + LANES - 1) // LANES * LANES
        done = []
        for t in range(count):
            strip = [work[t, low + SUB * q : low + SUB * (q + 1), left:right] for q in range(STRIP // SUB)]
            done.append(factor_strip(strip, low - left))
        for t in range(count):
            inverse_ref[t, low:high, : right - TILE] = done[t][:, TILE - left :]
            if right < 2 * TILE:
                inverse_ref[t, low:high, right - TILE :] = jnp.zeros((STRIP, 2 * TILE - right), jnp.float32)
            if high < TILE:
                rest = high // LANES * LANES
                update = lax.dot_general(
                    done[t][:, rest - left : TILE - left],
                    done[t],
                    (((0,), (0,)), ((), ())),
                    precision=HIGHEST,
                    preferred_element_type=jnp.float32,
                )
                work[t, high:, left:right] = work[t, high:, left:right] - update[high - rest :]


def inverse_factors(blocks):
    count = blocks.shape[0]
    return pl.pallas_call(
        functools.partial(inverse_kernel, count),
        out_shape=jax.ShapeDtypeStruct(blocks.shape, jnp.float32),
        in_specs=[pl.BlockSpec(memory_space=pltpu.VMEM)],
        out_specs=pl.BlockSpec(memory_space=pltpu.VMEM),
        scratch_shapes=[pltpu.VMEM((count, TILE, 2 * TILE), jnp.float32)],
        compiler_params=pltpu.CompilerParams(vmem_limit_bytes=16 * MIB),
        cost_estimate=lasting(10),
    )(blocks)


def halves(value):
    top = value.astype(jnp.bfloat16)
    return top, (value - top.astype(jnp.float32)).astype(jnp.bfloat16)


def dot_nt(left, right):
    return lax.dot_general(left, right, NT, preferred_element_type=jnp.float32)


def dot_nn(left, right):
    return jnp.dot(left, right, preferred_element_type=jnp.float32)


def pad_rows(value, count):
    short = count - value.shape[0]
    return value if short == 0 else jnp.concatenate([value, jnp.zeros((short, value.shape[1]), value.dtype)], 0)


def stacked(value):
    return jnp.concatenate(halves(value), 0)


def add_moved(total_ref, recv_ref, place_ref, hot):
    count = place_ref.shape[1]
    moved = dot_nt(stacked(pad_rows(recv_ref[...], count)), hot).astype(jnp.bfloat16)
    total_ref[...] += dot_nn(place_ref[...], moved[:count]) + dot_nn(place_ref[...], moved[count:])


def pick_rows(total, select_ref, outs):
    keep_ref, send_ref, spare_ref = outs
    rows = total.shape[0]
    sent = send_ref.shape[0]
    top, rest = halves(total)
    top = dot_nn(select_ref[...], top)
    rest = dot_nn(select_ref[...], rest)
    keep_ref[:rows] = top[:rows].astype(jnp.bfloat16)
    keep_ref[rows:] = rest[:rows].astype(jnp.bfloat16)
    both = top[rows:] + rest[rows:]
    send_ref[...] = both[:sent]
    spare_ref[...] = both[sent:]


def low_rank(weights_ref, panel):
    rows = weights_ref.shape[0] // 2
    top, rest = halves(panel)
    main = dot_nt(weights_ref[...], top)
    return main[:rows] + (main[rows:] + dot_nt(weights_ref[:rows], rest))


def update_kernel(rows_ref, panel_ref, weights_ref, select_ref, keep_ref, send_ref, spare_ref, split_ref):
    @pl.when(pl.program_id(0) == 0)
    def _():
        split_ref[...] = stacked(weights_ref[...])

    total = rows_ref[...] - low_rank(split_ref, panel_ref[...])
    pick_rows(total, select_ref, (keep_ref, send_ref, spare_ref))


def assemble_kernel(picks, target, flag, *refs):
    base_ref, keep_ref, recv_ref, spare_ref, place_ref, place_spare_ref, keep_map_ref, recv_map_ref = refs[:8]
    total_ref = refs[-1]
    rows = base_ref.shape[0]
    targets = target(pl.program_id(0)) * TILE + lax.broadcasted_iota(jnp.int32, (TILE, TILE), 0)
    keep_hot = jnp.where(keep_map_ref[...] == targets, 1.0, 0.0).astype(jnp.bfloat16)
    recv_hot = jnp.where(recv_map_ref[...] == targets, 1.0, 0.0).astype(jnp.bfloat16)
    kept = dot_nt(keep_ref[...], keep_hot)
    total_ref[...] = base_ref[...] + (kept[:rows] + kept[rows:])
    add_moved(total_ref, recv_ref, place_ref, recv_hot)

    @pl.when(flag[0] != 0)
    def _():
        add_moved(total_ref, spare_ref, place_spare_ref, recv_hot)

    if picks:
        pick_rows(total_ref[...], refs[8], refs[9:12])
    else:
        refs[8][...] = total_ref[...]


def pick_shapes(rows, sent, width):
    return (
        jax.ShapeDtypeStruct((2 * rows, width), jnp.bfloat16),
        jax.ShapeDtypeStruct((sent, width), jnp.float32),
        jax.ShapeDtypeStruct((rows - sent, width), jnp.float32),
    )


def update_and_pick(rows_mat, panel, weights, plan):
    rows, order = rows_mat.shape
    sent = plan.sent
    fixed = lambda shape: pl.BlockSpec(shape, lambda n: (0, 0))
    moving = lambda count: pl.BlockSpec((count, TILE), lambda n: (0, n))
    return pl.pallas_call(
        update_kernel,
        grid=(order // TILE,),
        out_shape=pick_shapes(rows, sent, order),
        in_specs=[
            moving(rows),
            pl.BlockSpec((TILE, TILE), lambda n: (n, 0)),
            fixed((rows, TILE)),
            fixed((2 * rows, rows)),
        ],
        out_specs=(moving(2 * rows), moving(sent), moving(rows - sent)),
        scratch_shapes=[pltpu.VMEM((2 * rows, TILE), jnp.bfloat16)],
        compiler_params=pltpu.CompilerParams(vmem_limit_bytes=48 * MIB),
        cost_estimate=lasting(order // TILE),
    )(rows_mat, panel, weights, plan.select)


def assemble(base, keep, recv, spare, plan, child_block, picks=None):
    rows, order = base.shape
    sent = recv.shape[0]
    children = order // 2 // TILE
    per = recv.shape[1] // TILE
    target = lambda n: child_block(n % per) + children * (n // per)
    fixed = lambda shape: pl.BlockSpec(shape, lambda n, _: (0, 0))
    child = lambda count: pl.BlockSpec((count, TILE), lambda n, _: (0, n % per))
    mapped = pl.BlockSpec((1, TILE), lambda n, _: (0, child_block(n % per)))
    wide = lambda count: pl.BlockSpec((count, TILE), lambda n, _: (0, n))
    in_specs = [
        pl.BlockSpec((rows, TILE), lambda n, _: (0, target(n))),
        child(2 * rows),
        child(sent),
        pl.BlockSpec((rows - sent, TILE), lambda n, flag: (0, n % per * flag[0])),
        fixed(plan.place.shape),
        fixed(plan.place_spare.shape),
        mapped,
        mapped,
    ]
    args = [base, keep, recv, spare, plan.place, plan.place_spare, plan.own_map[None], plan.other_map[None]]
    width = 2 * per * TILE
    if picks is None:
        out_shape = jax.ShapeDtypeStruct((rows, width), jnp.float32)
        out_specs = wide(rows)
    else:
        in_specs.append(fixed((2 * rows, rows)))
        args.append(picks.select)
        out_shape = pick_shapes(rows, picks.sent, width)
        out_specs = (wide(2 * rows), wide(picks.sent), wide(rows - picks.sent))
    return pl.pallas_call(
        functools.partial(assemble_kernel, picks is not None, target),
        out_shape=out_shape,
        grid_spec=pltpu.PrefetchScalarGridSpec(
            num_scalar_prefetch=1,
            grid=(2 * per,),
            in_specs=in_specs,
            out_specs=out_specs,
            scratch_shapes=[pltpu.VMEM((rows, TILE), jnp.float32)],
        ),
        compiler_params=pltpu.CompilerParams(vmem_limit_bytes=48 * MIB),
        cost_estimate=lasting(2 * per),
    )(plan.overflow, *args)


def finish_kernel(low, high, pair, where_ref, rows_ref, *refs):
    first_refs, second_refs, weights_ref = refs[:2], refs[2:4], refs[4]
    out_ref, split_ref = refs[-2:]
    n = pl.program_id(0)

    @pl.when(n == 0)
    def _():
        split_ref[...] = stacked(weights_ref[...])

    rows = rows_ref.shape[0]
    row_ids = where_ref[0] + lax.broadcasted_iota(jnp.int32, (rows, 1), 0)
    col_ids = pair(n) * 2 * TILE + lax.broadcasted_iota(jnp.int32, (1, 2 * TILE), 1)
    outside = lambda ids: (ids < low) | (ids >= high)
    turned = where_ref[1] % 2 != 0
    even = jnp.where(turned, first_refs[1][...], first_refs[0][...])
    odd = jnp.where(turned, first_refs[0][...], first_refs[1][...])
    panel = jnp.concatenate(
        [jnp.concatenate([even, odd], 0), jnp.concatenate([ref[...] for ref in second_refs], 0)], 1
    )
    change = low_rank(split_ref, panel)
    out_ref[...] = jnp.where(outside(row_ids) & outside(col_ids), rows_ref[...] - change, 0.0)


def finish(before, first, second, second_at, weights, scalars, pair, out=None):
    rows = before.shape[0]
    order = 2 * before.shape[1]
    low, high = order - 3 * TILE, order - TILE
    count = order // (4 * TILE)
    layers = order // TILE // 8
    wide = lambda index: pl.BlockSpec((rows, 2 * TILE), index)
    piece = pl.BlockSpec((TILE, TILE), lambda n, s: (place_of((2 * pair(n)) ^ s[1], layers), 0))
    later = lambda side: pl.BlockSpec((TILE, TILE), lambda n, s: (second_at(2 * pair(n) + side, s[1]), 0))
    in_specs = [wide(lambda n, _: (0, n)), piece, piece, later(0), later(1), wide(lambda n, _: (0, 0))]
    args = [before, *first, second, second, weights]
    if out is not None:
        in_specs.append(pl.BlockSpec(memory_space=pl.ANY))
        args.append(out)
    return pl.pallas_call(
        functools.partial(finish_kernel, low, high, pair),
        out_shape=jax.ShapeDtypeStruct((rows, order), jnp.float32),
        grid_spec=pltpu.PrefetchScalarGridSpec(
            num_scalar_prefetch=1,
            grid=(count,),
            in_specs=in_specs,
            out_specs=wide(lambda n, _: (0, pair(n))),
            scratch_shapes=[pltpu.VMEM((2 * rows, 2 * TILE), jnp.bfloat16)],
        ),
        input_output_aliases={} if out is None else {7: 0},
        compiler_params=pltpu.CompilerParams(vmem_limit_bytes=48 * MIB),
        cost_estimate=lasting(count),
    )(scalars, *args)


def product(left, right, precision=HIGHEST):
    return jnp.dot(left, right, precision=precision, preferred_element_type=jnp.float32)


def product_nt(left, right, precision=HIGHEST):
    return lax.dot_general(left, right, NT, precision=precision, preferred_element_type=jnp.float32)


def swap(value, mask):
    pairs = [(source, source ^ mask) for source in range(lax.axis_size("cube"))]
    return lax.ppermute(value, "cube", pairs)


def group_gather(value, group):
    size = lax.axis_size("cube")
    groups = [[g * group + i for i in range(group)] for g in range(size // group)]
    return lax.all_gather(value, "cube", axis=0, tiled=True, axis_index_groups=groups)


def one_hot(positions, count):
    return (positions[None, :] == jnp.arange(count, dtype=jnp.int32)[:, None]).astype(jnp.float32)


def column_targets(front_map):
    order = front_map.shape[0]
    ids = jnp.arange(order, dtype=jnp.int32)
    gone = (ids >= order - 2 * TILE) & (ids < order - TILE)
    return jnp.where(gone, -1, front_map)


def leaving(front_map, front, group, rows):
    target = (front_map // rows) // group
    return (front_map >= 0) & (target != front % 2)


class Plan:
    def __init__(self, maps, group, rows):
        me = lax.axis_index("cube")
        front = me // group
        block = me % group
        side = front % 2
        targets = jax.vmap(column_targets)(maps)
        self.sent = (rows * 19 // 32 + 7) // 8 * 8
        fronts = jnp.arange(maps.shape[0], dtype=jnp.int32)
        leaves = leaving(targets, fronts[:, None], group, rows).reshape(maps.shape[0], group, rows)
        most = jnp.max(jnp.sum(leaves.astype(jnp.int32), -1))
        self.overflow = (most > self.sent).astype(jnp.int32).reshape(1)
        self.own_map = lax.dynamic_index_in_dim(targets, front, 0, keepdims=False)
        self.other_map = lax.dynamic_index_in_dim(targets, front ^ 1, 0, keepdims=False)
        own = lax.dynamic_slice_in_dim(self.own_map, block * rows, rows, 0)
        other = lax.dynamic_slice_in_dim(self.other_map, block * rows, rows, 0)
        here = (block + group * side) * rows
        there = (block + group * (1 - side)) * rows
        self.keep = one_hot(own - here, rows)
        self.give = one_hot(own - there, rows)
        ids = jnp.arange(rows, dtype=jnp.int32)
        upper = (ids[:, None] <= ids[None, :]).astype(jnp.bfloat16)
        leaves = (own >= there) & (own < there + rows)
        comes = (other >= here) & (other < here + rows)
        flags = jnp.stack([leaves, comes]).astype(jnp.bfloat16)
        ranks = jnp.dot(flags, upper, preferred_element_type=jnp.float32).astype(jnp.int32) - 1
        send = one_hot(jnp.where(leaves, ranks[0], -1), rows)
        self.select = jnp.concatenate([self.keep, send], 0).astype(jnp.bfloat16)
        taken = one_hot(jnp.where(comes, ranks[1], -1), rows).astype(jnp.bfloat16)
        slots = one_hot(other - here, rows).astype(jnp.bfloat16)
        place = lax.dot_general(slots, taken, NT, preferred_element_type=jnp.float32).astype(jnp.bfloat16)
        fill = lambda part: jnp.pad(part, ((0, 0), (0, -part.shape[1] % 16)))
        self.place = fill(place[:, : self.sent])
        self.place_spare = fill(place[:, self.sent :])


def spread_block(block, group, owner_low, rows):
    size = lax.axis_size("cube")
    me = lax.axis_index("cube")
    holders = max(1, TILE // rows)
    has = {d for d in range(size) if owner_low <= d % group < owner_low + holders}
    inside = (me % group >= owner_low) & (me % group < owner_low + holders)
    block = jnp.where(inside, block, 0.0)
    mask = group // 2
    while mask >= holders:
        pairs = [(d, d ^ mask) for d in sorted(has)]
        block = block + lax.ppermute(block, "cube", pairs)
        has |= {d ^ mask for d in has}
        mask //= 2
    return block


def whole_block(part, rows):
    if rows >= TILE:
        return part
    return group_gather(part, TILE // rows)


def place_of(turned, layers):
    span = layers // 2
    layer, y, x = turned // 8, turned // 4 % 2, turned // 2 % 2
    lower = (2 * y + x) * span + layer
    upper = (4 + 2 * x + y) * span + layer - span
    return jnp.where(layer < span, lower, upper)


def cross_planes(block):
    layers = lax.axis_size("cube") // 8
    if block.shape[0] != TILE:
        return [block]
    return [block] + [swap(block, 8 * layer) for layer in range(1, layers)]


def spread_crossed(stack, low):
    rows = stack[0].shape[-2]
    if rows != TILE:
        parts = stack[0].reshape(-1, rows, TILE)
        blocks = jnp.stack([whole_block(part, rows) for part in parts]).reshape(*stack[0].shape[:-2], TILE, TILE)
        return spread_block(blocks, lax.axis_size("cube"), low // rows, rows)
    owner = low // rows
    layer = lax.axis_index("cube") // 8 ^ owner // 8
    block = stack[0]
    for number in range(1, len(stack)):
        block = jnp.where(layer == number, stack[number], block)
    return spread_block(block, 8, owner % 8, rows)


def gather_second(stack):
    layers = lax.axis_size("cube") // 8
    if stack[0].shape[0] != TILE:
        return lax.all_gather(stack[0], "cube", axis=0, tiled=True), lambda cb, me: cb
    return group_gather(jnp.concatenate(stack, 0), 8), lambda cb, me: cb % 8 * layers + (cb // 8 ^ me // 8)


def gather_first(stack, after):
    size = lax.axis_size("cube")
    layers = size // 8
    block = stack[0]
    if block.shape[0] != TILE:
        whole = lax.all_gather(block, "cube", axis=0, tiled=True)
        order = whole.shape[0]
        layers = order // TILE // 8
        spots = [0] * (4 * layers)
        for m in range(4 * layers):
            layer, y, x = m // 4, m // 2 % 2, m % 2
            span = layers // 2
            spot = (2 * y + x) * span + layer if layer < span else (4 + 2 * x + y) * span + layer - span
            spots[spot] = m
        blocks = whole.reshape(order // TILE, TILE, TILE)
        sides = [jnp.concatenate([blocks[2 * m + side] for m in spots], 0) for side in range(2)]
        return sides, jnp.int32(0), after
    me = lax.axis_index("cube")
    one = jnp.concatenate(stack[: layers // 2], 0)
    two = jnp.concatenate(stack[layers // 2 :], 0)
    one = jnp.concatenate([one, swap(one, 2)], 0)
    two = jnp.concatenate([two, swap(two, 4)], 0)
    even = jnp.concatenate([one, swap(one, 4), two, swap(two, 2)], 0)
    even, after = lax.optimization_barrier((even, after))
    odd = swap(even, 1)
    return (even, odd), me, after


def local(gfront, cfront, rfront, gmap, cmap):
    devices = lax.axis_size("cube")
    me = lax.axis_index("cube")
    quarter = devices // 4
    half = devices // 2
    rows = gfront.shape[0]
    order_g, order_c, order_r = gfront.shape[1], cfront.shape[1], rfront.shape[1]
    g_low, c_low = order_g - 2 * TILE, order_c - 2 * TILE
    r_low = order_r - 3 * TILE
    r_high = r_low + TILE

    def exchange(send, spare, plan, mask):
        rest = lax.cond(plan.overflow[0] != 0, lambda part: swap(part, mask), jnp.zeros_like, spare)
        return swap(send, mask), rest

    own_g = gfront[:, g_low : g_low + TILE]
    own_c = cfront[:, c_low : c_low + TILE]
    own_second = rfront[:, r_high : r_high + TILE]
    panel_g = group_gather(own_g, quarter)
    panel_c = group_gather(own_c, half)
    crossed = cross_planes(own_second)
    inverse_g = inverse_factors(panel_g[g_low : g_low + TILE][None])[0]
    plan_g = Plan(gmap, quarter, rows)
    plan_c = Plan(cmap, half, rows)

    gfactor = product_nt(own_g, inverse_g)
    weights_g = product(gfactor, inverse_g)

    g_keep, g_send, g_spare = update_and_pick(gfront, panel_g, weights_g, plan_g)
    panel_c, g_send = lax.optimization_barrier((panel_c, g_send))
    inverse_c = inverse_factors(panel_c[c_low : c_low + TILE][None])[0]
    second, second_at = gather_second(crossed)
    cfactor = product_nt(own_c, inverse_c)
    weights_c = product(cfactor, inverse_c)

    g_edge = gfront[:, g_low - TILE : g_low] - product_nt(weights_g, panel_g[g_low - TILE : g_low])
    edge_map = plan_g.own_map[g_low - TILE : g_low]
    g_edge = product_nt(g_edge, one_hot(edge_map - (c_low - TILE), TILE))
    c_edge = cfront[:, c_low - TILE : c_low] - product_nt(weights_c, panel_c[c_low - TILE : c_low])
    c_edge = c_edge + product(plan_g.keep, g_edge) + swap(product(plan_g.give, g_edge), quarter)
    g_recv, g_rest = exchange(g_send, g_spare, plan_g, quarter)
    c_edge, g_recv = lax.optimization_barrier((c_edge, g_recv))
    edge_map = plan_c.own_map[c_low - TILE : c_low]
    c_edge = product_nt(c_edge, one_hot(edge_map - r_low, TILE))
    r_edge = rfront[:, r_low : r_low + TILE] + product(plan_c.keep, c_edge)
    r_come = swap(product(plan_c.give, c_edge), half)
    c_base = cfront - product_nt(weights_c, panel_c, HIGH)
    blocks_g = order_g // TILE
    per = blocks_g // 2
    child_of_c = lambda part: lambda p: part * per + p
    child_of_r = lambda part: lambda p: part * per + p % per + blocks_g * (p // per)
    pieces, sends = [], []
    for part in range(2):
        low, high = part * per * TILE, (part + 1) * per * TILE
        g_part = [value[:, low:high] for value in (g_keep, g_recv, g_rest)]
        keep, send, spare = assemble(c_base, *g_part, plan_g, child_of_c(part), plan_c)
        sends.append(send)
        pieces.append((keep, *exchange(send, spare, plan_c, half)))
    r_come, sends[0] = lax.optimization_barrier((r_come, sends[0]))
    r_edge = r_edge + r_come
    stack = cross_planes(r_edge)
    root_11 = spread_crossed(stack, r_low)
    root_21, root_22 = spread_crossed([jnp.stack(both) for both in zip(stack, crossed)], r_high)

    inv_11 = inverse_factors(root_11[None])[0]
    low_21 = product_nt(root_21, inv_11)
    inv_22 = inverse_factors((root_22 - product_nt(low_21, low_21))[None])[0]
    inv_21 = -product(inv_22, product(low_21, inv_11))

    keep, recv, rest = pieces[0]
    first, turn, (recv, inv_22) = gather_first(stack, (recv, inv_22))
    pieces[0] = (keep, recv, rest)
    plan_c.place, second = lax.optimization_barrier((plan_c.place, second))

    factor_1 = product_nt(r_edge, inv_11)
    factor_2 = product_nt(r_edge, inv_21) + product_nt(own_second, inv_22)
    weights_1 = product(factor_1, inv_11) + product(factor_2, inv_21)
    weights_2 = product(factor_2, inv_22)
    row_ids = me * rows + jnp.arange(rows, dtype=jnp.int32)
    above = (row_ids >= r_low) & (row_ids < r_high)
    factor_2 = jnp.where(above[:, None], 0.0, factor_2)
    rfactor = jnp.concatenate([factor_1, factor_2], 1)
    pairs = per // 2

    pair_of = lambda part: lambda n: n % pairs + 2 * pairs * (n // pairs) + pairs * part
    scalars = jnp.stack([me * rows, turn]).astype(jnp.int32)
    weights_r = jnp.concatenate([weights_1, weights_2], 1)
    rschur = None
    for part, (keep, recv, rest) in enumerate(pieces):
        if part:
            rschur, recv = lax.optimization_barrier((rschur, recv))
        before = assemble(rfront, keep, recv, rest, plan_c, child_of_r(part))
        rschur = finish(before, first, second, second_at, weights_r, scalars, pair_of(part), rschur)
    return (gfactor, cfactor, rfactor, rschur)


def solution(mesh):
    placed = (P("cube", None), P("cube", None), P("cube", None), P(), P())
    return jax.shard_map(
        local,
        mesh=mesh,
        in_specs=placed,
        out_specs=(P("cube", None), P("cube", None), P("cube", None), P("cube", None)),
        check_vma=False,
    )
```

```python
import functools

import jax
import jax.numpy as jnp
from jax import lax
from jax.experimental import pallas as pl
from jax.experimental.pallas import tpu as pltpu
from jax.sharding import PartitionSpec as P

TILE = 256
STRIP = 32
SUB = 8
LANES = 128
HIGH = lax.Precision.HIGH
HIGHEST = lax.Precision.HIGHEST
NT = (((1,), (1,)), ((), ()))
MIB = 1024 * 1024


def lasting(microseconds):
    return pl.CostEstimate(flops=1, bytes_accessed=int(microseconds * 3_500_000), transcendentals=0)


def widen(column, width):
    return jnp.concatenate([column] * (width // LANES), 1)


def factor_strip(strip, base):
    width = strip[0].shape[1]
    sub_ids = lax.broadcasted_iota(jnp.int32, (SUB, 1), 0)
    count = len(strip)
    for p in range(count):
        first = base + p * SUB
        cols = [
            [jnp.broadcast_to(strip[q][:, first + j : first + j + 1], (SUB, LANES)) for j in range(SUB)]
            for q in range(p, count)
        ]
        for j in range(SUB):
            pivot = cols[0][j][j : j + 1, :]
            inv = lax.rsqrt(pivot)
            inv = inv * (1.5 - 0.5 * pivot * inv * inv)
            unit = strip[p][j : j + 1, :] * widen(inv, width)
            scaled = [col[j] * inv for col in cols]
            below = jnp.where(sub_ids > j, scaled[0], 0.0)
            strip[p] = jnp.where(sub_ids == j, unit, strip[p] - widen(below, width) * unit)
            for q in range(p + 1, count):
                strip[q] = strip[q] - widen(scaled[q - p], width) * unit
            for m in range(j + 1, SUB):
                head = scaled[0][m : m + 1, :]
                for q in range(p, count):
                    cols[q - p][m] = cols[q - p][m] - scaled[q - p] * head
    return jnp.concatenate(strip, 0)


def inverse_kernel(count, blocks_ref, inverse_ref, work):
    row_ids = lax.broadcasted_iota(jnp.int32, (TILE, TILE), 0)
    col_ids = lax.broadcasted_iota(jnp.int32, (TILE, TILE), 1)
    for t in range(count):
        work[t, :, :TILE] = blocks_ref[t]
        work[t, :, TILE:] = (row_ids == col_ids).astype(jnp.float32)
    for low in range(0, TILE, STRIP):
        high = low + STRIP
        left = low // LANES * LANES
        right = TILE + (high + LANES - 1) // LANES * LANES
        done = []
        for t in range(count):
            strip = [work[t, low + SUB * q : low + SUB * (q + 1), left:right] for q in range(STRIP // SUB)]
            done.append(factor_strip(strip, low - left))
        for t in range(count):
            inverse_ref[t, low:high, : right - TILE] = done[t][:, TILE - left :]
            if right < 2 * TILE:
                inverse_ref[t, low:high, right - TILE :] = jnp.zeros((STRIP, 2 * TILE - right), jnp.float32)
            if high < TILE:
                rest = high // LANES * LANES
                update = lax.dot_general(
                    done[t][:, rest - left : TILE - left],
                    done[t],
                    (((0,), (0,)), ((), ())),
                    precision=HIGHEST,
                    preferred_element_type=jnp.float32,
                )
                work[t, high:, left:right] = work[t, high:, left:right] - update[high - rest :]


def inverse_factors(blocks):
    count = blocks.shape[0]
    return pl.pallas_call(
        functools.partial(inverse_kernel, count),
        out_shape=jax.ShapeDtypeStruct(blocks.shape, jnp.float32),
        in_specs=[pl.BlockSpec(memory_space=pltpu.VMEM)],
        out_specs=pl.BlockSpec(memory_space=pltpu.VMEM),
        scratch_shapes=[pltpu.VMEM((count, TILE, 2 * TILE), jnp.float32)],
        compiler_params=pltpu.CompilerParams(vmem_limit_bytes=16 * MIB),
        cost_estimate=lasting(10),
    )(blocks)


def halves(value):
    top = value.astype(jnp.bfloat16)
    return top, (value - top.astype(jnp.float32)).astype(jnp.bfloat16)


def dot_nt(left, right):
    return lax.dot_general(left, right, NT, preferred_element_type=jnp.float32)


def dot_nn(left, right):
    return jnp.dot(left, right, preferred_element_type=jnp.float32)


def pad_rows(value, count):
    short = count - value.shape[0]
    return value if short == 0 else jnp.concatenate([value, jnp.zeros((short, value.shape[1]), value.dtype)], 0)


def stacked(value):
    return jnp.concatenate(halves(value), 0)


def add_moved(total_ref, recv_ref, place_ref, hot):
    count = place_ref.shape[1]
    moved = dot_nt(stacked(pad_rows(recv_ref[...], count)), hot).astype(jnp.bfloat16)
    total_ref[...] += dot_nn(place_ref[...], moved[:count]) + dot_nn(place_ref[...], moved[count:])


def pick_rows(total, select_ref, outs):
    keep_ref, send_ref, spare_ref = outs
    rows = total.shape[0]
    sent = send_ref.shape[0]
    top, rest = halves(total)
    top = dot_nn(select_ref[...], top)
    rest = dot_nn(select_ref[...], rest)
    keep_ref[:rows] = top[:rows].astype(jnp.bfloat16)
    keep_ref[rows:] = rest[:rows].astype(jnp.bfloat16)
    both = top[rows:] + rest[rows:]
    send_ref[...] = both[:sent]
    spare_ref[...] = both[sent:]


def low_rank(weights_ref, panel):
    rows = weights_ref.shape[0] // 2
    top, rest = halves(panel)
    main = dot_nt(weights_ref[...], top)
    return main[:rows] + (main[rows:] + dot_nt(weights_ref[:rows], rest))


def update_kernel(rows_ref, panel_ref, weights_ref, select_ref, keep_ref, send_ref, spare_ref, split_ref):
    @pl.when(pl.program_id(0) == 0)
    def _():
        split_ref[...] = stacked(weights_ref[...])

    total = rows_ref[...] - low_rank(split_ref, panel_ref[...])
    pick_rows(total, select_ref, (keep_ref, send_ref, spare_ref))


def assemble_kernel(picks, target, flag, *refs):
    base_ref, keep_ref, recv_ref, spare_ref, place_ref, place_spare_ref, keep_map_ref, recv_map_ref = refs[:8]
    total_ref = refs[-1]
    rows = base_ref.shape[0]
    targets = target(pl.program_id(0)) * TILE + lax.broadcasted_iota(jnp.int32, (TILE, TILE), 0)
    keep_hot = jnp.where(keep_map_ref[...] == targets, 1.0, 0.0).astype(jnp.bfloat16)
    recv_hot = jnp.where(recv_map_ref[...] == targets, 1.0, 0.0).astype(jnp.bfloat16)
    kept = dot_nt(keep_ref[...], keep_hot)
    total_ref[...] = base_ref[...] + (kept[:rows] + kept[rows:])
    add_moved(total_ref, recv_ref, place_ref, recv_hot)

    @pl.when(flag[0] != 0)
    def _():
        add_moved(total_ref, spare_ref, place_spare_ref, recv_hot)

    if picks:
        pick_rows(total_ref[...], refs[8], refs[9:12])
    else:
        refs[8][...] = total_ref[...]


def pick_shapes(rows, sent, width):
    return (
        jax.ShapeDtypeStruct((2 * rows, width), jnp.bfloat16),
        jax.ShapeDtypeStruct((sent, width), jnp.float32),
        jax.ShapeDtypeStruct((rows - sent, width), jnp.float32),
    )


def update_and_pick(rows_mat, panel, weights, plan):
    rows, order = rows_mat.shape
    sent = plan.sent
    fixed = lambda shape: pl.BlockSpec(shape, lambda n: (0, 0))
    moving = lambda count: pl.BlockSpec((count, TILE), lambda n: (0, n))
    return pl.pallas_call(
        update_kernel,
        grid=(order // TILE,),
        out_shape=pick_shapes(rows, sent, order),
        in_specs=[
            moving(rows),
            pl.BlockSpec((TILE, TILE), lambda n: (n, 0)),
            fixed((rows, TILE)),
            fixed((2 * rows, rows)),
        ],
        out_specs=(moving(2 * rows), moving(sent), moving(rows - sent)),
        scratch_shapes=[pltpu.VMEM((2 * rows, TILE), jnp.bfloat16)],
        compiler_params=pltpu.CompilerParams(vmem_limit_bytes=48 * MIB),
        cost_estimate=lasting(order // TILE),
    )(rows_mat, panel, weights, plan.select)


def assemble(base, keep, recv, spare, plan, child_block, picks=None):
    rows, order = base.shape
    sent = recv.shape[0]
    children = order // 2 // TILE
    per = recv.shape[1] // TILE
    target = lambda n: child_block(n % per) + children * (n // per)
    fixed = lambda shape: pl.BlockSpec(shape, lambda n, _: (0, 0))
    child = lambda count: pl.BlockSpec((count, TILE), lambda n, _: (0, n % per))
    mapped = pl.BlockSpec((1, TILE), lambda n, _: (0, child_block(n % per)))
    wide = lambda count: pl.BlockSpec((count, TILE), lambda n, _: (0, n))
    in_specs = [
        pl.BlockSpec((rows, TILE), lambda n, _: (0, target(n))),
        child(2 * rows),
        child(sent),
        pl.BlockSpec((rows - sent, TILE), lambda n, flag: (0, n % per * flag[0])),
        fixed(plan.place.shape),
        fixed(plan.place_spare.shape),
        mapped,
        mapped,
    ]
    args = [base, keep, recv, spare, plan.place, plan.place_spare, plan.own_map[None], plan.other_map[None]]
    width = 2 * per * TILE
    if picks is None:
        out_shape = jax.ShapeDtypeStruct((rows, width), jnp.float32)
        out_specs = wide(rows)
    else:
        in_specs.append(fixed((2 * rows, rows)))
        args.append(picks.select)
        out_shape = pick_shapes(rows, picks.sent, width)
        out_specs = (wide(2 * rows), wide(picks.sent), wide(rows - picks.sent))
    return pl.pallas_call(
        functools.partial(assemble_kernel, picks is not None, target),
        out_shape=out_shape,
        grid_spec=pltpu.PrefetchScalarGridSpec(
            num_scalar_prefetch=1,
            grid=(2 * per,),
            in_specs=in_specs,
            out_specs=out_specs,
            scratch_shapes=[pltpu.VMEM((rows, TILE), jnp.float32)],
        ),
        compiler_params=pltpu.CompilerParams(vmem_limit_bytes=48 * MIB),
        cost_estimate=lasting(2 * per),
    )(plan.overflow, *args)


def finish_kernel(low, high, pair, where_ref, rows_ref, *refs):
    first_refs, second_refs, weights_ref = refs[:2], refs[2:4], refs[4]
    out_ref, split_ref = refs[-2:]
    n = pl.program_id(0)

    @pl.when(n == 0)
    def _():
        split_ref[...] = stacked(weights_ref[...])

    rows = rows_ref.shape[0]
    row_ids = where_ref[0] + lax.broadcasted_iota(jnp.int32, (rows, 1), 0)
    col_ids = pair(n) * 2 * TILE + lax.broadcasted_iota(jnp.int32, (1, 2 * TILE), 1)
    outside = lambda ids: (ids < low) | (ids >= high)
    turned = where_ref[1] % 2 != 0
    even = jnp.where(turned, first_refs[1][...], first_refs[0][...])
    odd = jnp.where(turned, first_refs[0][...], first_refs[1][...])
    panel = jnp.concatenate(
        [jnp.concatenate([even, odd], 0), jnp.concatenate([ref[...] for ref in second_refs], 0)], 1
    )
    change = low_rank(split_ref, panel)
    out_ref[...] = jnp.where(outside(row_ids) & outside(col_ids), rows_ref[...] - change, 0.0)


def finish(before, first, second, second_at, weights, scalars, pair, out=None):
    rows = before.shape[0]
    order = 2 * before.shape[1]
    low, high = order - 3 * TILE, order - TILE
    count = order // (4 * TILE)
    layers = order // TILE // 8
    wide = lambda index: pl.BlockSpec((rows, 2 * TILE), index)
    piece = pl.BlockSpec((TILE, TILE), lambda n, s: (place_of((2 * pair(n)) ^ s[1], layers), 0))
    later = lambda side: pl.BlockSpec((TILE, TILE), lambda n, s: (second_at(2 * pair(n) + side, s[1]), 0))
    in_specs = [wide(lambda n, _: (0, n)), piece, piece, later(0), later(1), wide(lambda n, _: (0, 0))]
    args = [before, *first, second, second, weights]
    if out is not None:
        in_specs.append(pl.BlockSpec(memory_space=pl.ANY))
        args.append(out)
    return pl.pallas_call(
        functools.partial(finish_kernel, low, high, pair),
        out_shape=jax.ShapeDtypeStruct((rows, order), jnp.float32),
        grid_spec=pltpu.PrefetchScalarGridSpec(
            num_scalar_prefetch=1,
            grid=(count,),
            in_specs=in_specs,
            out_specs=wide(lambda n, _: (0, pair(n))),
            scratch_shapes=[pltpu.VMEM((2 * rows, 2 * TILE), jnp.bfloat16)],
        ),
        input_output_aliases={} if out is None else {7: 0},
        compiler_params=pltpu.CompilerParams(vmem_limit_bytes=48 * MIB),
        cost_estimate=lasting(count),
    )(scalars, *args)


def product(left, right, precision=HIGHEST):
    return jnp.dot(left, right, precision=precision, preferred_element_type=jnp.float32)


def product_nt(left, right, precision=HIGHEST):
    return lax.dot_general(left, right, NT, precision=precision, preferred_element_type=jnp.float32)


def swap(value, mask):
    pairs = [(source, source ^ mask) for source in range(lax.axis_size("cube"))]
    return lax.ppermute(value, "cube", pairs)


def group_gather(value, group):
    size = lax.axis_size("cube")
    groups = [[g * group + i for i in range(group)] for g in range(size // group)]
    return lax.all_gather(value, "cube", axis=0, tiled=True, axis_index_groups=groups)


def one_hot(positions, count):
    return (positions[None, :] == jnp.arange(count, dtype=jnp.int32)[:, None]).astype(jnp.float32)


def column_targets(front_map):
    order = front_map.shape[0]
    ids = jnp.arange(order, dtype=jnp.int32)
    gone = (ids >= order - 2 * TILE) & (ids < order - TILE)
    return jnp.where(gone, -1, front_map)


def leaving(front_map, front, group, rows):
    target = (front_map // rows) // group
    return (front_map >= 0) & (target != front % 2)


class Plan:
    def __init__(self, maps, group, rows):
        me = lax.axis_index("cube")
        front = me // group
        block = me % group
        side = front % 2
        targets = jax.vmap(column_targets)(maps)
        self.sent = (rows * 19 // 32 + 7) // 8 * 8
        fronts = jnp.arange(maps.shape[0], dtype=jnp.int32)
        leaves = leaving(targets, fronts[:, None], group, rows).reshape(maps.shape[0], group, rows)
        most = jnp.max(jnp.sum(leaves.astype(jnp.int32), -1))
        self.overflow = (most > self.sent).astype(jnp.int32).reshape(1)
        self.own_map = lax.dynamic_index_in_dim(targets, front, 0, keepdims=False)
        self.other_map = lax.dynamic_index_in_dim(targets, front ^ 1, 0, keepdims=False)
        own = lax.dynamic_slice_in_dim(self.own_map, block * rows, rows, 0)
        other = lax.dynamic_slice_in_dim(self.other_map, block * rows, rows, 0)
        here = (block + group * side) * rows
        there = (block + group * (1 - side)) * rows
        self.keep = one_hot(own - here, rows)
        self.give = one_hot(own - there, rows)
        ids = jnp.arange(rows, dtype=jnp.int32)
        upper = (ids[:, None] <= ids[None, :]).astype(jnp.bfloat16)
        leaves = (own >= there) & (own < there + rows)
        comes = (other >= here) & (other < here + rows)
        flags = jnp.stack([leaves, comes]).astype(jnp.bfloat16)
        ranks = jnp.dot(flags, upper, preferred_element_type=jnp.float32).astype(jnp.int32) - 1
        send = one_hot(jnp.where(leaves, ranks[0], -1), rows)
        self.select = jnp.concatenate([self.keep, send], 0).astype(jnp.bfloat16)
        taken = one_hot(jnp.where(comes, ranks[1], -1), rows).astype(jnp.bfloat16)
        slots = one_hot(other - here, rows).astype(jnp.bfloat16)
        place = lax.dot_general(slots, taken, NT, preferred_element_type=jnp.float32).astype(jnp.bfloat16)
        fill = lambda part: jnp.pad(part, ((0, 0), (0, -part.shape[1] % 16)))
        self.place = fill(place[:, : self.sent])
        self.place_spare = fill(place[:, self.sent :])


def spread_block(block, group, owner_low, rows):
    size = lax.axis_size("cube")
    me = lax.axis_index("cube")
    holders = max(1, TILE // rows)
    has = {d for d in range(size) if owner_low <= d % group < owner_low + holders}
    inside = (me % group >= owner_low) & (me % group < owner_low + holders)
    block = jnp.where(inside, block, 0.0)
    mask = group // 2
    while mask >= holders:
        pairs = [(d, d ^ mask) for d in sorted(has)]
        block = block + lax.ppermute(block, "cube", pairs)
        has |= {d ^ mask for d in has}
        mask //= 2
    return block


def whole_block(part, rows):
    if rows >= TILE:
        return part
    return group_gather(part, TILE // rows)


def place_of(turned, layers):
    span = layers // 2
    layer, y, x = turned // 8, turned // 4 % 2, turned // 2 % 2
    lower = (2 * y + x) * span + layer
    upper = (4 + 2 * x + y) * span + layer - span
    return jnp.where(layer < span, lower, upper)


def cross_planes(block):
    layers = lax.axis_size("cube") // 8
    if block.shape[0] != TILE:
        return [block]
    return [block] + [swap(block, 8 * layer) for layer in range(1, layers)]


def spread_crossed(stack, low):
    rows = stack[0].shape[-2]
    if rows != TILE:
        parts = stack[0].reshape(-1, rows, TILE)
        blocks = jnp.stack([whole_block(part, rows) for part in parts]).reshape(*stack[0].shape[:-2], TILE, TILE)
        return spread_block(blocks, lax.axis_size("cube"), low // rows, rows)
    owner = low // rows
    layer = lax.axis_index("cube") // 8 ^ owner // 8
    block = stack[0]
    for number in range(1, len(stack)):
        block = jnp.where(layer == number, stack[number], block)
    return spread_block(block, 8, owner % 8, rows)


def gather_second(stack):
    layers = lax.axis_size("cube") // 8
    if stack[0].shape[0] != TILE:
        return lax.all_gather(stack[0], "cube", axis=0, tiled=True), lambda cb, me: cb
    return group_gather(jnp.concatenate(stack, 0), 8), lambda cb, me: cb % 8 * layers + (cb // 8 ^ me // 8)


def gather_first(stack, after):
    size = lax.axis_size("cube")
    layers = size // 8
    block = stack[0]
    if block.shape[0] != TILE:
        whole = lax.all_gather(block, "cube", axis=0, tiled=True)
        order = whole.shape[0]
        layers = order // TILE // 8
        spots = [0] * (4 * layers)
        for m in range(4 * layers):
            layer, y, x = m // 4, m // 2 % 2, m % 2
            span = layers // 2
            spot = (2 * y + x) * span + layer if layer < span else (4 + 2 * x + y) * span + layer - span
            spots[spot] = m
        blocks = whole.reshape(order // TILE, TILE, TILE)
        sides = [jnp.concatenate([blocks[2 * m + side] for m in spots], 0) for side in range(2)]
        return sides, jnp.int32(0), after
    me = lax.axis_index("cube")
    one = jnp.concatenate(stack[: layers // 2], 0)
    two = jnp.concatenate(stack[layers // 2 :], 0)
    one = jnp.concatenate([one, swap(one, 2)], 0)
    two = jnp.concatenate([two, swap(two, 4)], 0)
    even = jnp.concatenate([one, swap(one, 4), two, swap(two, 2)], 0)
    even, after = lax.optimization_barrier((even, after))
    odd = swap(even, 1)
    return (even, odd), me, after


def local(gfront, cfront, rfront, gmap, cmap):
    devices = lax.axis_size("cube")
    me = lax.axis_index("cube")
    quarter = devices // 4
    half = devices // 2
    rows = gfront.shape[0]
    order_g, order_c, order_r = gfront.shape[1], cfront.shape[1], rfront.shape[1]
    g_low, c_low = order_g - 2 * TILE, order_c - 2 * TILE
    r_low = order_r - 3 * TILE
    r_high = r_low + TILE

    def exchange(send, spare, plan, mask):
        rest = lax.cond(plan.overflow[0] != 0, lambda part: swap(part, mask), jnp.zeros_like, spare)
        return swap(send, mask), rest

    own_g = gfront[:, g_low : g_low + TILE]
    own_c = cfront[:, c_low : c_low + TILE]
    own_second = rfront[:, r_high : r_high + TILE]
    panel_g = group_gather(own_g, quarter)
    panel_c = group_gather(own_c, half)
    crossed = cross_planes(own_second)
    inverse_g = inverse_factors(panel_g[g_low : g_low + TILE][None])[0]
    plan_g = Plan(gmap, quarter, rows)
    plan_c = Plan(cmap, half, rows)

    gfactor = product_nt(own_g, inverse_g)
    weights_g = product(gfactor, inverse_g)

    g_keep, g_send, g_spare = update_and_pick(gfront, panel_g, weights_g, plan_g)
    panel_c, g_send = lax.optimization_barrier((panel_c, g_send))
    inverse_c = inverse_factors(panel_c[c_low : c_low + TILE][None])[0]
    second, second_at = gather_second(crossed)
    cfactor = product_nt(own_c, inverse_c)
    weights_c = product(cfactor, inverse_c)

    g_edge = gfront[:, g_low - TILE : g_low] - product_nt(weights_g, panel_g[g_low - TILE : g_low])
    edge_map = plan_g.own_map[g_low - TILE : g_low]
    g_edge = product_nt(g_edge, one_hot(edge_map - (c_low - TILE), TILE))
    c_edge = cfront[:, c_low - TILE : c_low] - product_nt(weights_c, panel_c[c_low - TILE : c_low])
    c_edge = c_edge + product(plan_g.keep, g_edge) + swap(product(plan_g.give, g_edge), quarter)
    g_recv, g_rest = exchange(g_send, g_spare, plan_g, quarter)
    c_edge, g_recv = lax.optimization_barrier((c_edge, g_recv))
    edge_map = plan_c.own_map[c_low - TILE : c_low]
    c_edge = product_nt(c_edge, one_hot(edge_map - r_low, TILE))
    r_edge = rfront[:, r_low : r_low + TILE] + product(plan_c.keep, c_edge)
    r_come = swap(product(plan_c.give, c_edge), half)
    c_base = cfront - product_nt(weights_c, panel_c, HIGH)
    blocks_g = order_g // TILE
    per = blocks_g // 2
    child_of_c = lambda part: lambda p: part * per + p
    child_of_r = lambda part: lambda p: part * per + p % per + blocks_g * (p // per)
    pieces, sends = [], []
    for part in range(2):
        low, high = part * per * TILE, (part + 1) * per * TILE
        g_part = [value[:, low:high] for value in (g_keep, g_recv, g_rest)]
        keep, send, spare = assemble(c_base, *g_part, plan_g, child_of_c(part), plan_c)
        sends.append(send)
        pieces.append((keep, *exchange(send, spare, plan_c, half)))
    r_come, sends = lax.optimization_barrier((r_come, sends))
    r_edge = r_edge + r_come
    stack = cross_planes(r_edge)
    root_11 = spread_crossed(stack, r_low)
    root_21, root_22 = spread_crossed([jnp.stack(both) for both in zip(stack, crossed)], r_high)

    inv_11 = inverse_factors(root_11[None])[0]
    low_21 = product_nt(root_21, inv_11)
    inv_22 = inverse_factors((root_22 - product_nt(low_21, low_21))[None])[0]
    inv_21 = -product(inv_22, product(low_21, inv_11))

    recvs = [piece[1] for piece in pieces]
    first, turn, (recvs, inv_22) = gather_first(stack, (recvs, inv_22))
    plan_c.place, second = lax.optimization_barrier((plan_c.place, second))

    factor_1 = product_nt(r_edge, inv_11)
    factor_2 = product_nt(r_edge, inv_21) + product_nt(own_second, inv_22)
    weights_1 = product(factor_1, inv_11) + product(factor_2, inv_21)
    weights_2 = product(factor_2, inv_22)
    row_ids = me * rows + jnp.arange(rows, dtype=jnp.int32)
    above = (row_ids >= r_low) & (row_ids < r_high)
    factor_2 = jnp.where(above[:, None], 0.0, factor_2)
    rfactor = jnp.concatenate([factor_1, factor_2], 1)
    pairs = per // 2

    pair_of = lambda part: lambda n: n % pairs + 2 * pairs * (n // pairs) + pairs * part
    scalars = jnp.stack([me * rows, turn]).astype(jnp.int32)
    weights_r = jnp.concatenate([weights_1, weights_2], 1)
    rschur = None
    parts = []
    for part, (keep, _, rest) in enumerate(pieces):
        parts.append(assemble(rfront, keep, recvs[part], rest, plan_c, child_of_r(part)))
    for part in range(2):
        rschur = finish(parts[part], first, second, second_at, weights_r, scalars, pair_of(part), rschur)
    return (gfactor, cfactor, rfactor, rschur)


def solution(mesh):
    placed = (P("cube", None), P("cube", None), P("cube", None), P(), P())
    return jax.shard_map(
        local,
        mesh=mesh,
        in_specs=placed,
        out_specs=(P("cube", None), P("cube", None), P("cube", None), P("cube", None)),
        check_vma=False,
    )
```

```python
import functools

import jax
import jax.numpy as jnp
from jax import lax
from jax.experimental import pallas as pl
from jax.experimental.pallas import tpu as pltpu
from jax.sharding import PartitionSpec as P

TILE = 256
STRIP = 32
SUB = 8
LANES = 128
HIGH = lax.Precision.HIGH
HIGHEST = lax.Precision.HIGHEST
NT = (((1,), (1,)), ((), ()))
MIB = 1024 * 1024


def lasting(microseconds):
    return pl.CostEstimate(flops=1, bytes_accessed=int(microseconds * 3_500_000), transcendentals=0)


def widen(column, width):
    return jnp.concatenate([column] * (width // LANES), 1)


def factor_strip(strip, base):
    width = strip[0].shape[1]
    sub_ids = lax.broadcasted_iota(jnp.int32, (SUB, 1), 0)
    count = len(strip)
    for p in range(count):
        first = base + p * SUB
        cols = [
            [jnp.broadcast_to(strip[q][:, first + j : first + j + 1], (SUB, LANES)) for j in range(SUB)]
            for q in range(p, count)
        ]
        for j in range(SUB):
            pivot = cols[0][j][j : j + 1, :]
            inv = lax.rsqrt(pivot)
            inv = inv * (1.5 - 0.5 * pivot * inv * inv)
            unit = strip[p][j : j + 1, :] * widen(inv, width)
            scaled = [col[j] * inv for col in cols]
            below = jnp.where(sub_ids > j, scaled[0], 0.0)
            strip[p] = jnp.where(sub_ids == j, unit, strip[p] - widen(below, width) * unit)
            for q in range(p + 1, count):
                strip[q] = strip[q] - widen(scaled[q - p], width) * unit
            for m in range(j + 1, SUB):
                head = scaled[0][m : m + 1, :]
                for q in range(p, count):
                    cols[q - p][m] = cols[q - p][m] - scaled[q - p] * head
    return jnp.concatenate(strip, 0)


def inverse_kernel(count, blocks_ref, inverse_ref, work):
    row_ids = lax.broadcasted_iota(jnp.int32, (TILE, TILE), 0)
    col_ids = lax.broadcasted_iota(jnp.int32, (TILE, TILE), 1)
    for t in range(count):
        work[t, :, :TILE] = blocks_ref[t]
        work[t, :, TILE:] = (row_ids == col_ids).astype(jnp.float32)
    for low in range(0, TILE, STRIP):
        high = low + STRIP
        left = low // LANES * LANES
        right = TILE + (high + LANES - 1) // LANES * LANES
        done = []
        for t in range(count):
            strip = [work[t, low + SUB * q : low + SUB * (q + 1), left:right] for q in range(STRIP // SUB)]
            done.append(factor_strip(strip, low - left))
        for t in range(count):
            inverse_ref[t, low:high, : right - TILE] = done[t][:, TILE - left :]
            if right < 2 * TILE:
                inverse_ref[t, low:high, right - TILE :] = jnp.zeros((STRIP, 2 * TILE - right), jnp.float32)
            if high < TILE:
                rest = high // LANES * LANES
                update = lax.dot_general(
                    done[t][:, rest - left : TILE - left],
                    done[t],
                    (((0,), (0,)), ((), ())),
                    precision=HIGHEST,
                    preferred_element_type=jnp.float32,
                )
                work[t, high:, left:right] = work[t, high:, left:right] - update[high - rest :]


def inverse_factors(blocks):
    count = blocks.shape[0]
    return pl.pallas_call(
        functools.partial(inverse_kernel, count),
        out_shape=jax.ShapeDtypeStruct(blocks.shape, jnp.float32),
        in_specs=[pl.BlockSpec(memory_space=pltpu.VMEM)],
        out_specs=pl.BlockSpec(memory_space=pltpu.VMEM),
        scratch_shapes=[pltpu.VMEM((count, TILE, 2 * TILE), jnp.float32)],
        compiler_params=pltpu.CompilerParams(vmem_limit_bytes=16 * MIB),
        cost_estimate=lasting(1),
    )(blocks)


def halves(value):
    top = value.astype(jnp.bfloat16)
    return top, (value - top.astype(jnp.float32)).astype(jnp.bfloat16)


def dot_nt(left, right):
    return lax.dot_general(left, right, NT, preferred_element_type=jnp.float32)


def dot_nn(left, right):
    return jnp.dot(left, right, preferred_element_type=jnp.float32)


def pad_rows(value, count):
    short = count - value.shape[0]
    return value if short == 0 else jnp.concatenate([value, jnp.zeros((short, value.shape[1]), value.dtype)], 0)


def stacked(value):
    return jnp.concatenate(halves(value), 0)


def add_moved(total_ref, recv_ref, place_ref, hot):
    count = place_ref.shape[1]
    moved = dot_nt(stacked(pad_rows(recv_ref[...], count)), hot).astype(jnp.bfloat16)
    total_ref[...] += dot_nn(place_ref[...], moved[:count]) + dot_nn(place_ref[...], moved[count:])


def pick_rows(total, select_ref, outs):
    keep_ref, send_ref, spare_ref = outs
    rows = total.shape[0]
    sent = send_ref.shape[0]
    top, rest = halves(total)
    top = dot_nn(select_ref[...], top)
    rest = dot_nn(select_ref[...], rest)
    keep_ref[:rows] = top[:rows].astype(jnp.bfloat16)
    keep_ref[rows:] = rest[:rows].astype(jnp.bfloat16)
    both = top[rows:] + rest[rows:]
    send_ref[...] = both[:sent]
    spare_ref[...] = both[sent:]


def low_rank(weights_ref, panel):
    rows = weights_ref.shape[0] // 2
    top, rest = halves(panel)
    main = dot_nt(weights_ref[...], top)
    return main[:rows] + (main[rows:] + dot_nt(weights_ref[:rows], rest))


def update_kernel(rows_ref, panel_ref, weights_ref, select_ref, keep_ref, send_ref, spare_ref, split_ref):
    @pl.when(pl.program_id(0) == 0)
    def _():
        split_ref[...] = stacked(weights_ref[...])

    total = rows_ref[...] - low_rank(split_ref, panel_ref[...])
    pick_rows(total, select_ref, (keep_ref, send_ref, spare_ref))


def assemble_kernel(picks, flag, *refs):
    base_ref, keep_ref, recv_ref, spare_ref, place_ref, place_spare_ref, keep_map_ref, recv_map_ref = refs[:8]
    total_ref = refs[-1]
    rows = base_ref.shape[0]
    targets = pl.program_id(0) * TILE + lax.broadcasted_iota(jnp.int32, (TILE, TILE), 0)
    keep_hot = jnp.where(keep_map_ref[...] == targets, 1.0, 0.0).astype(jnp.bfloat16)
    recv_hot = jnp.where(recv_map_ref[...] == targets, 1.0, 0.0).astype(jnp.bfloat16)
    kept = dot_nt(keep_ref[...], keep_hot)
    total_ref[...] = base_ref[...] + (kept[:rows] + kept[rows:])
    add_moved(total_ref, recv_ref, place_ref, recv_hot)

    @pl.when(flag[0] != 0)
    def _():
        add_moved(total_ref, spare_ref, place_spare_ref, recv_hot)

    if picks:
        pick_rows(total_ref[...], refs[8], refs[9:12])
    else:
        refs[8][...] = total_ref[...]


def pick_shapes(rows, sent, width):
    return (
        jax.ShapeDtypeStruct((2 * rows, width), jnp.bfloat16),
        jax.ShapeDtypeStruct((sent, width), jnp.float32),
        jax.ShapeDtypeStruct((rows - sent, width), jnp.float32),
    )


def update_and_pick(rows_mat, panel, weights, plan):
    rows, order = rows_mat.shape
    sent = plan.sent
    fixed = lambda shape: pl.BlockSpec(shape, lambda n: (0, 0))
    moving = lambda count: pl.BlockSpec((count, TILE), lambda n: (0, n))
    return pl.pallas_call(
        update_kernel,
        grid=(order // TILE,),
        out_shape=pick_shapes(rows, sent, order),
        in_specs=[
            moving(rows),
            pl.BlockSpec((TILE, TILE), lambda n: (n, 0)),
            fixed((rows, TILE)),
            fixed((2 * rows, rows)),
        ],
        out_specs=(moving(2 * rows), moving(sent), moving(rows - sent)),
        scratch_shapes=[pltpu.VMEM((2 * rows, TILE), jnp.bfloat16)],
        compiler_params=pltpu.CompilerParams(vmem_limit_bytes=48 * MIB),
        cost_estimate=lasting(order // TILE),
    )(rows_mat, panel, weights, plan.select)


def assemble(base, keep, recv, spare, plan, picks=None):
    rows, order = base.shape
    sent = recv.shape[0]
    per = recv.shape[1] // TILE
    fixed = lambda shape: pl.BlockSpec(shape, lambda n, _: (0, 0))
    child = lambda count: pl.BlockSpec((count, TILE), lambda n, _: (0, n % per))
    mapped = pl.BlockSpec((1, TILE), lambda n, _: (0, n % per))
    wide = lambda count: pl.BlockSpec((count, TILE), lambda n, _: (0, n))
    in_specs = [
        wide(rows),
        child(2 * rows),
        child(sent),
        pl.BlockSpec((rows - sent, TILE), lambda n, flag: (0, n % per * flag[0])),
        fixed(plan.place.shape),
        fixed(plan.place_spare.shape),
        mapped,
        mapped,
    ]
    args = [base, keep, recv, spare, plan.place, plan.place_spare, plan.own_map[None], plan.other_map[None]]
    width = order
    if picks is None:
        out_shape = jax.ShapeDtypeStruct((rows, width), jnp.float32)
        out_specs = wide(rows)
    else:
        in_specs.append(fixed((2 * rows, rows)))
        args.append(picks.select)
        out_shape = pick_shapes(rows, picks.sent, width)
        out_specs = (wide(2 * rows), wide(picks.sent), wide(rows - picks.sent))
    return pl.pallas_call(
        functools.partial(assemble_kernel, picks is not None),
        out_shape=out_shape,
        grid_spec=pltpu.PrefetchScalarGridSpec(
            num_scalar_prefetch=1,
            grid=(2 * per,),
            in_specs=in_specs,
            out_specs=out_specs,
            scratch_shapes=[pltpu.VMEM((rows, TILE), jnp.float32)],
        ),
        compiler_params=pltpu.CompilerParams(vmem_limit_bytes=48 * MIB),
        cost_estimate=lasting(2 * per),
    )(plan.overflow, *args)


def finish_kernel(low, high, where_ref, rows_ref, *refs):
    first_refs, second_refs, weights_ref = refs[:2], refs[2:4], refs[4]
    out_ref, split_ref = refs[-2:]
    n = pl.program_id(0)

    @pl.when(n == 0)
    def _():
        split_ref[...] = stacked(weights_ref[...])

    rows = rows_ref.shape[0]
    row_ids = where_ref[0] + lax.broadcasted_iota(jnp.int32, (rows, 1), 0)
    col_ids = n * 2 * TILE + lax.broadcasted_iota(jnp.int32, (1, 2 * TILE), 1)
    outside = lambda ids: (ids < low) | (ids >= high)
    turned = where_ref[1] % 2 != 0
    even = jnp.where(turned, first_refs[1][...], first_refs[0][...])
    odd = jnp.where(turned, first_refs[0][...], first_refs[1][...])
    panel = jnp.concatenate(
        [jnp.concatenate([even, odd], 0), jnp.concatenate([ref[...] for ref in second_refs], 0)], 1
    )
    change = low_rank(split_ref, panel)
    out_ref[...] = jnp.where(outside(row_ids) & outside(col_ids), rows_ref[...] - change, 0.0)


def finish(before, first, second, second_at, weights, scalars):
    rows, order = before.shape
    low, high = order - 3 * TILE, order - TILE
    count = order // (2 * TILE)
    layers = order // TILE // 8
    wide = lambda index: pl.BlockSpec((rows, 2 * TILE), index)
    piece = pl.BlockSpec((TILE, TILE), lambda n, s: (place_of((2 * n) ^ s[1], layers), 0))
    later = lambda side: pl.BlockSpec((TILE, TILE), lambda n, s: (second_at(2 * n + side, s[1]), 0))
    in_specs = [wide(lambda n, _: (0, n)), piece, piece, later(0), later(1), wide(lambda n, _: (0, 0))]
    args = [before, *first, second, second, weights]
    return pl.pallas_call(
        functools.partial(finish_kernel, low, high),
        out_shape=jax.ShapeDtypeStruct((rows, order), jnp.float32),
        grid_spec=pltpu.PrefetchScalarGridSpec(
            num_scalar_prefetch=1,
            grid=(count,),
            in_specs=in_specs,
            out_specs=wide(lambda n, _: (0, n)),
            scratch_shapes=[pltpu.VMEM((2 * rows, 2 * TILE), jnp.bfloat16)],
        ),
        compiler_params=pltpu.CompilerParams(vmem_limit_bytes=48 * MIB),
        cost_estimate=lasting(count),
    )(scalars, *args)


def product(left, right, precision=HIGHEST):
    return jnp.dot(left, right, precision=precision, preferred_element_type=jnp.float32)


def product_nt(left, right, precision=HIGHEST):
    return lax.dot_general(left, right, NT, precision=precision, preferred_element_type=jnp.float32)


def swap(value, mask):
    pairs = [(source, source ^ mask) for source in range(lax.axis_size("cube"))]
    return lax.ppermute(value, "cube", pairs)


def group_gather(value, group):
    size = lax.axis_size("cube")
    groups = [[g * group + i for i in range(group)] for g in range(size // group)]
    return lax.all_gather(value, "cube", axis=0, tiled=True, axis_index_groups=groups)


def one_hot(positions, count):
    return (positions[None, :] == jnp.arange(count, dtype=jnp.int32)[:, None]).astype(jnp.float32)


def column_targets(front_map):
    order = front_map.shape[0]
    ids = jnp.arange(order, dtype=jnp.int32)
    gone = (ids >= order - 2 * TILE) & (ids < order - TILE)
    return jnp.where(gone, -1, front_map)


def leaving(front_map, front, group, rows):
    target = (front_map // rows) // group
    return (front_map >= 0) & (target != front % 2)


class Plan:
    def __init__(self, maps, group, rows):
        me = lax.axis_index("cube")
        front = me // group
        block = me % group
        side = front % 2
        targets = jax.vmap(column_targets)(maps)
        self.sent = (rows * 19 // 32 + 7) // 8 * 8
        fronts = jnp.arange(maps.shape[0], dtype=jnp.int32)
        leaves = leaving(targets, fronts[:, None], group, rows).reshape(maps.shape[0], group, rows)
        most = jnp.max(jnp.sum(leaves.astype(jnp.int32), -1))
        self.overflow = (most > self.sent).astype(jnp.int32).reshape(1)
        self.own_map = lax.dynamic_index_in_dim(targets, front, 0, keepdims=False)
        self.other_map = lax.dynamic_index_in_dim(targets, front ^ 1, 0, keepdims=False)
        own = lax.dynamic_slice_in_dim(self.own_map, block * rows, rows, 0)
        other = lax.dynamic_slice_in_dim(self.other_map, block * rows, rows, 0)
        here = (block + group * side) * rows
        there = (block + group * (1 - side)) * rows
        self.keep = one_hot(own - here, rows)
        self.give = one_hot(own - there, rows)
        ids = jnp.arange(rows, dtype=jnp.int32)
        upper = (ids[:, None] <= ids[None, :]).astype(jnp.bfloat16)
        leaves = (own >= there) & (own < there + rows)
        comes = (other >= here) & (other < here + rows)
        flags = jnp.stack([leaves, comes]).astype(jnp.bfloat16)
        ranks = jnp.dot(flags, upper, preferred_element_type=jnp.float32).astype(jnp.int32) - 1
        send = one_hot(jnp.where(leaves, ranks[0], -1), rows)
        self.select = jnp.concatenate([self.keep, send], 0).astype(jnp.bfloat16)
        taken = one_hot(jnp.where(comes, ranks[1], -1), rows).astype(jnp.bfloat16)
        slots = one_hot(other - here, rows).astype(jnp.bfloat16)
        place = lax.dot_general(slots, taken, NT, preferred_element_type=jnp.float32).astype(jnp.bfloat16)
        fill = lambda part: jnp.pad(part, ((0, 0), (0, -part.shape[1] % 16)))
        self.place = fill(place[:, : self.sent])
        self.place_spare = fill(place[:, self.sent :])


def spread_block(block, group, owner_low, rows):
    size = lax.axis_size("cube")
    me = lax.axis_index("cube")
    holders = max(1, TILE // rows)
    has = {d for d in range(size) if owner_low <= d % group < owner_low + holders}
    inside = (me % group >= owner_low) & (me % group < owner_low + holders)
    block = jnp.where(inside, block, 0.0)
    mask = group // 2
    while mask >= holders:
        pairs = [(d, d ^ mask) for d in sorted(has)]
        block = block + lax.ppermute(block, "cube", pairs)
        has |= {d ^ mask for d in has}
        mask //= 2
    return block


def whole_block(part, rows):
    if rows >= TILE:
        return part
    return group_gather(part, TILE // rows)


def place_of(turned, layers):
    span = layers // 2
    layer, y, x = turned // 8, turned // 4 % 2, turned // 2 % 2
    lower = (2 * y + x) * span + layer
    upper = (4 + 2 * x + y) * span + layer - span
    return jnp.where(layer < span, lower, upper)


def cross_planes(block):
    layers = lax.axis_size("cube") // 8
    if block.shape[0] != TILE:
        return [block]
    return [block] + [swap(block, 8 * layer) for layer in range(1, layers)]


def spread_crossed(stack, low):
    rows = stack[0].shape[-2]
    if rows != TILE:
        parts = stack[0].reshape(-1, rows, TILE)
        blocks = jnp.stack([whole_block(part, rows) for part in parts]).reshape(*stack[0].shape[:-2], TILE, TILE)
        return spread_block(blocks, lax.axis_size("cube"), low // rows, rows)
    owner = low // rows
    layer = lax.axis_index("cube") // 8 ^ owner // 8
    block = stack[0]
    for number in range(1, len(stack)):
        block = jnp.where(layer == number, stack[number], block)
    return spread_block(block, 8, owner % 8, rows)


def gather_second(stack):
    layers = lax.axis_size("cube") // 8
    if stack[0].shape[0] != TILE:
        return lax.all_gather(stack[0], "cube", axis=0, tiled=True), lambda cb, me: cb
    return group_gather(jnp.concatenate(stack, 0), 8), lambda cb, me: cb % 8 * layers + (cb // 8 ^ me // 8)


def gather_first(stack, after):
    size = lax.axis_size("cube")
    layers = size // 8
    block = stack[0]
    if block.shape[0] != TILE:
        whole = lax.all_gather(block, "cube", axis=0, tiled=True)
        order = whole.shape[0]
        layers = order // TILE // 8
        spots = [0] * (4 * layers)
        for m in range(4 * layers):
            layer, y, x = m // 4, m // 2 % 2, m % 2
            span = layers // 2
            spot = (2 * y + x) * span + layer if layer < span else (4 + 2 * x + y) * span + layer - span
            spots[spot] = m
        blocks = whole.reshape(order // TILE, TILE, TILE)
        sides = [jnp.concatenate([blocks[2 * m + side] for m in spots], 0) for side in range(2)]
        return sides, jnp.int32(0), after
    me = lax.axis_index("cube")
    one = jnp.concatenate(stack[: layers // 2], 0)
    two = jnp.concatenate(stack[layers // 2 :], 0)
    one = jnp.concatenate([one, swap(one, 2)], 0)
    two = jnp.concatenate([two, swap(two, 4)], 0)
    even = jnp.concatenate([one, swap(one, 4), two, swap(two, 2)], 0)
    even, after = lax.optimization_barrier((even, after))
    odd = swap(even, 1)
    return (even, odd), me, after


def local(gfront, cfront, rfront, gmap, cmap):
    devices = lax.axis_size("cube")
    me = lax.axis_index("cube")
    quarter = devices // 4
    half = devices // 2
    rows = gfront.shape[0]
    order_g, order_c, order_r = gfront.shape[1], cfront.shape[1], rfront.shape[1]
    g_low, c_low = order_g - 2 * TILE, order_c - 2 * TILE
    r_low = order_r - 3 * TILE
    r_high = r_low + TILE

    def exchange(send, spare, plan, mask):
        rest = lax.cond(plan.overflow[0] != 0, lambda part: swap(part, mask), jnp.zeros_like, spare)
        return swap(send, mask), rest

    own_g = gfront[:, g_low : g_low + TILE]
    own_c = cfront[:, c_low : c_low + TILE]
    own_second = rfront[:, r_high : r_high + TILE]
    panel_g = group_gather(own_g, quarter)
    panel_c = group_gather(own_c, half)
    crossed = cross_planes(own_second)
    inverse_g = inverse_factors(panel_g[g_low : g_low + TILE][None])[0]
    plan_g = Plan(gmap, quarter, rows)
    plan_c = Plan(cmap, half, rows)

    gfactor = product_nt(own_g, inverse_g)
    weights_g = product(gfactor, inverse_g)

    g_keep, g_send, g_spare = update_and_pick(gfront, panel_g, weights_g, plan_g)
    panel_c, g_send = lax.optimization_barrier((panel_c, g_send))
    inverse_c = inverse_factors(panel_c[c_low : c_low + TILE][None])[0]
    second, second_at = gather_second(crossed)
    cfactor = product_nt(own_c, inverse_c)
    weights_c = product(cfactor, inverse_c)

    g_edge = gfront[:, g_low - TILE : g_low] - product_nt(weights_g, panel_g[g_low - TILE : g_low])
    edge_map = plan_g.own_map[g_low - TILE : g_low]
    g_edge = product_nt(g_edge, one_hot(edge_map - (c_low - TILE), TILE))
    c_edge = cfront[:, c_low - TILE : c_low] - product_nt(weights_c, panel_c[c_low - TILE : c_low])
    c_edge = c_edge + product(plan_g.keep, g_edge) + swap(product(plan_g.give, g_edge), quarter)
    g_recv, g_rest = exchange(g_send, g_spare, plan_g, quarter)
    c_edge, g_recv = lax.optimization_barrier((c_edge, g_recv))
    edge_map = plan_c.own_map[c_low - TILE : c_low]
    c_edge = product_nt(c_edge, one_hot(edge_map - r_low, TILE))
    r_edge = rfront[:, r_low : r_low + TILE] + product(plan_c.keep, c_edge)
    r_come = swap(product(plan_c.give, c_edge), half)
    c_base = cfront - product_nt(weights_c, panel_c, HIGH)
    c_keep, c_send, c_spare = assemble(c_base, g_keep, g_recv, g_rest, plan_g, plan_c)
    c_recv, c_rest = exchange(c_send, c_spare, plan_c, half)
    r_come, c_send = lax.optimization_barrier((r_come, c_send))
    r_edge = r_edge + r_come
    stack = cross_planes(r_edge)
    root_11 = spread_crossed(stack, r_low)
    root_21, root_22 = spread_crossed([jnp.stack(both) for both in zip(stack, crossed)], r_high)

    inv_11 = inverse_factors(root_11[None])[0]
    low_21 = product_nt(root_21, inv_11)
    inv_22 = inverse_factors((root_22 - product_nt(low_21, low_21))[None])[0]
    inv_21 = -product(inv_22, product(low_21, inv_11))

    first, turn, (c_recv, inv_22) = gather_first(stack, (c_recv, inv_22))
    plan_c.place, second = lax.optimization_barrier((plan_c.place, second))

    factor_1 = product_nt(r_edge, inv_11)
    factor_2 = product_nt(r_edge, inv_21) + product_nt(own_second, inv_22)
    weights_1 = product(factor_1, inv_11) + product(factor_2, inv_21)
    weights_2 = product(factor_2, inv_22)
    row_ids = me * rows + jnp.arange(rows, dtype=jnp.int32)
    above = (row_ids >= r_low) & (row_ids < r_high)
    factor_2 = jnp.where(above[:, None], 0.0, factor_2)
    rfactor = jnp.concatenate([factor_1, factor_2], 1)
    scalars = jnp.stack([me * rows, turn]).astype(jnp.int32)
    weights_r = jnp.concatenate([weights_1, weights_2], 1)
    r_rows = assemble(rfront, c_keep, c_recv, c_rest, plan_c)
    rschur = finish(r_rows, first, second, second_at, weights_r, scalars)
    return (gfactor, cfactor, rfactor, rschur)


def solution(mesh):
    placed = (P("cube", None), P("cube", None), P("cube", None), P(), P())
    return jax.shard_map(
        local,
        mesh=mesh,
        in_specs=placed,
        out_specs=(P("cube", None), P("cube", None), P("cube", None), P("cube", None)),
        check_vma=False,
    )
```

```python
import functools

import jax
import jax.numpy as jnp
from jax import lax
from jax.experimental import pallas as pl
from jax.experimental.pallas import tpu as pltpu
from jax.sharding import PartitionSpec as P

TILE = 256
STRIP = 32
SUB = 8
LANES = 128
HIGH = lax.Precision.HIGH
HIGHEST = lax.Precision.HIGHEST
NT = (((1,), (1,)), ((), ()))
MIB = 1024 * 1024


def lasting(microseconds):
    return pl.CostEstimate(flops=1, bytes_accessed=int(microseconds * 3_500_000), transcendentals=0)


def widen(column, width):
    return jnp.concatenate([column] * (width // LANES), 1)


def factor_strip(strip, base):
    width = strip[0].shape[1]
    sub_ids = lax.broadcasted_iota(jnp.int32, (SUB, 1), 0)
    count = len(strip)
    for p in range(count):
        first = base + p * SUB
        cols = [
            [jnp.broadcast_to(strip[q][:, first + j : first + j + 1], (SUB, LANES)) for j in range(SUB)]
            for q in range(p, count)
        ]
        for j in range(SUB):
            pivot = cols[0][j][j : j + 1, :]
            inv = lax.rsqrt(pivot)
            inv = inv * (1.5 - 0.5 * pivot * inv * inv)
            unit = strip[p][j : j + 1, :] * widen(inv, width)
            scaled = [col[j] * inv for col in cols]
            below = jnp.where(sub_ids > j, scaled[0], 0.0)
            strip[p] = jnp.where(sub_ids == j, unit, strip[p] - widen(below, width) * unit)
            for q in range(p + 1, count):
                strip[q] = strip[q] - widen(scaled[q - p], width) * unit
            for m in range(j + 1, SUB):
                head = scaled[0][m : m + 1, :]
                for q in range(p, count):
                    cols[q - p][m] = cols[q - p][m] - scaled[q - p] * head
    return jnp.concatenate(strip, 0)


def inverse_kernel(count, blocks_ref, inverse_ref, work):
    row_ids = lax.broadcasted_iota(jnp.int32, (TILE, TILE), 0)
    col_ids = lax.broadcasted_iota(jnp.int32, (TILE, TILE), 1)
    for t in range(count):
        work[t, :, :TILE] = blocks_ref[t]
        work[t, :, TILE:] = (row_ids == col_ids).astype(jnp.float32)
    for low in range(0, TILE, STRIP):
        high = low + STRIP
        left = low // LANES * LANES
        right = TILE + (high + LANES - 1) // LANES * LANES
        done = []
        for t in range(count):
            strip = [work[t, low + SUB * q : low + SUB * (q + 1), left:right] for q in range(STRIP // SUB)]
            done.append(factor_strip(strip, low - left))
        for t in range(count):
            inverse_ref[t, low:high, : right - TILE] = done[t][:, TILE - left :]
            if right < 2 * TILE:
                inverse_ref[t, low:high, right - TILE :] = jnp.zeros((STRIP, 2 * TILE - right), jnp.float32)
            if high < TILE:
                rest = high // LANES * LANES
                update = lax.dot_general(
                    done[t][:, rest - left : TILE - left],
                    done[t],
                    (((0,), (0,)), ((), ())),
                    precision=HIGHEST,
                    preferred_element_type=jnp.float32,
                )
                work[t, high:, left:right] = work[t, high:, left:right] - update[high - rest :]


def inverse_factors(blocks):
    count = blocks.shape[0]
    return pl.pallas_call(
        functools.partial(inverse_kernel, count),
        out_shape=jax.ShapeDtypeStruct(blocks.shape, jnp.float32),
        in_specs=[pl.BlockSpec(memory_space=pltpu.VMEM)],
        out_specs=pl.BlockSpec(memory_space=pltpu.VMEM),
        scratch_shapes=[pltpu.VMEM((count, TILE, 2 * TILE), jnp.float32)],
        compiler_params=pltpu.CompilerParams(vmem_limit_bytes=16 * MIB),
        cost_estimate=lasting(1),
    )(blocks)


def halves(value):
    top = value.astype(jnp.bfloat16)
    return top, (value - top.astype(jnp.float32)).astype(jnp.bfloat16)


def dot_nt(left, right):
    return lax.dot_general(left, right, NT, preferred_element_type=jnp.float32)


def dot_nn(left, right):
    return jnp.dot(left, right, preferred_element_type=jnp.float32)


def pad_rows(value, count):
    short = count - value.shape[0]
    return value if short == 0 else jnp.concatenate([value, jnp.zeros((short, value.shape[1]), value.dtype)], 0)


def stacked(value):
    return jnp.concatenate(halves(value), 0)


def add_moved(total_ref, recv_ref, place_ref, hot, cols):
    count = place_ref.shape[1]
    moved = dot_nt(stacked(pad_rows(recv_ref[:, cols], count)), hot).astype(jnp.bfloat16)
    total_ref[:, cols] += dot_nn(place_ref[...], moved[:count]) + dot_nn(place_ref[...], moved[count:])


def pick_rows(total, select_ref, outs, cols):
    keep_ref, send_ref, spare_ref = outs
    rows = total.shape[0]
    sent = send_ref.shape[0]
    top, rest = halves(total)
    top = dot_nn(select_ref[...], top)
    rest = dot_nn(select_ref[...], rest)
    keep_ref[:rows, cols] = top[:rows].astype(jnp.bfloat16)
    keep_ref[rows:, cols] = rest[:rows].astype(jnp.bfloat16)
    both = top[rows:] + rest[rows:]
    send_ref[:, cols] = both[:sent]
    spare_ref[:, cols] = both[sent:]


def low_rank(weights_ref, panel):
    rows = weights_ref.shape[0] // 2
    top, rest = halves(panel)
    main = dot_nt(weights_ref[...], top)
    return main[:rows] + (main[rows:] + dot_nt(weights_ref[:rows], rest))


def update_kernel(rows_ref, panel_ref, weights_ref, select_ref, keep_ref, send_ref, spare_ref, split_ref):
    @pl.when(pl.program_id(0) == 0)
    def _():
        split_ref[...] = stacked(weights_ref[...])

    total = rows_ref[...] - low_rank(split_ref, panel_ref[...])
    pick_rows(total, select_ref, (keep_ref, send_ref, spare_ref), slice(0, TILE))


def assemble_kernel(picks, flag, *refs):
    base_ref, keep_ref, recv_ref, spare_ref, place_ref, place_spare_ref, keep_map_ref, recv_map_ref = refs[:8]
    total_ref = refs[-1]
    rows = base_ref.shape[0]
    for side in range(2):
        cols = slice(side * TILE, (side + 1) * TILE)
        first = (2 * pl.program_id(0) + side) * TILE
        targets = first + lax.broadcasted_iota(jnp.int32, (TILE, TILE), 0)
        keep_hot = jnp.where(keep_map_ref[:, cols] == targets, 1.0, 0.0).astype(jnp.bfloat16)
        recv_hot = jnp.where(recv_map_ref[:, cols] == targets, 1.0, 0.0).astype(jnp.bfloat16)
        kept = dot_nt(keep_ref[:, cols], keep_hot)
        total_ref[:, cols] = base_ref[:, cols] + (kept[:rows] + kept[rows:])
        add_moved(total_ref, recv_ref, place_ref, recv_hot, cols)

        @pl.when(flag[0] != 0)
        def _(recv_hot=recv_hot, cols=cols):
            add_moved(total_ref, spare_ref, place_spare_ref, recv_hot, cols)

        if picks:
            pick_rows(total_ref[:, cols], refs[8], refs[9:12], cols)
        else:
            refs[8][:, cols] = total_ref[:, cols]


def pick_shapes(rows, sent, width):
    return (
        jax.ShapeDtypeStruct((2 * rows, width), jnp.bfloat16),
        jax.ShapeDtypeStruct((sent, width), jnp.float32),
        jax.ShapeDtypeStruct((rows - sent, width), jnp.float32),
    )


def update_and_pick(rows_mat, panel, weights, plan):
    rows, order = rows_mat.shape
    sent = plan.sent
    fixed = lambda shape: pl.BlockSpec(shape, lambda n: (0, 0))
    moving = lambda count: pl.BlockSpec((count, TILE), lambda n: (0, n))
    return pl.pallas_call(
        update_kernel,
        grid=(order // TILE,),
        out_shape=pick_shapes(rows, sent, order),
        in_specs=[
            moving(rows),
            pl.BlockSpec((TILE, TILE), lambda n: (n, 0)),
            fixed((rows, TILE)),
            fixed((2 * rows, rows)),
        ],
        out_specs=(moving(2 * rows), moving(sent), moving(rows - sent)),
        scratch_shapes=[pltpu.VMEM((2 * rows, TILE), jnp.bfloat16)],
        compiler_params=pltpu.CompilerParams(vmem_limit_bytes=48 * MIB),
        cost_estimate=lasting(order // TILE),
    )(rows_mat, panel, weights, plan.select)


def assemble(base, keep, recv, spare, plan, picks=None):
    rows, order = base.shape
    sent = recv.shape[0]
    per = recv.shape[1] // (2 * TILE)
    fixed = lambda shape: pl.BlockSpec(shape, lambda n, _: (0, 0))
    child = lambda count: pl.BlockSpec((count, 2 * TILE), lambda n, _: (0, n % per))
    mapped = pl.BlockSpec((1, 2 * TILE), lambda n, _: (0, n % per))
    wide = lambda count: pl.BlockSpec((count, 2 * TILE), lambda n, _: (0, n))
    in_specs = [
        wide(rows),
        child(2 * rows),
        child(sent),
        pl.BlockSpec((rows - sent, 2 * TILE), lambda n, flag: (0, n % per * flag[0])),
        fixed(plan.place.shape),
        fixed(plan.place_spare.shape),
        mapped,
        mapped,
    ]
    args = [base, keep, recv, spare, plan.place, plan.place_spare, plan.own_map[None], plan.other_map[None]]
    width = order
    if picks is None:
        out_shape = jax.ShapeDtypeStruct((rows, width), jnp.float32)
        out_specs = wide(rows)
    else:
        in_specs.append(fixed((2 * rows, rows)))
        args.append(picks.select)
        out_shape = pick_shapes(rows, picks.sent, width)
        out_specs = (wide(2 * rows), wide(picks.sent), wide(rows - picks.sent))
    return pl.pallas_call(
        functools.partial(assemble_kernel, picks is not None),
        out_shape=out_shape,
        grid_spec=pltpu.PrefetchScalarGridSpec(
            num_scalar_prefetch=1,
            grid=(2 * per,),
            in_specs=in_specs,
            out_specs=out_specs,
            scratch_shapes=[pltpu.VMEM((rows, 2 * TILE), jnp.float32)],
        ),
        compiler_params=pltpu.CompilerParams(vmem_limit_bytes=48 * MIB),
        cost_estimate=lasting(4 * per),
    )(plan.overflow, *args)


def finish_kernel(low, high, where_ref, rows_ref, *refs):
    first_refs, second_refs, weights_ref = refs[:2], refs[2:4], refs[4]
    out_ref, split_ref = refs[-2:]
    n = pl.program_id(0)

    @pl.when(n == 0)
    def _():
        split_ref[...] = stacked(weights_ref[...])

    rows = rows_ref.shape[0]
    row_ids = where_ref[0] + lax.broadcasted_iota(jnp.int32, (rows, 1), 0)
    col_ids = n * 2 * TILE + lax.broadcasted_iota(jnp.int32, (1, 2 * TILE), 1)
    outside = lambda ids: (ids < low) | (ids >= high)
    turned = where_ref[1] % 2 != 0
    even = jnp.where(turned, first_refs[1][...], first_refs[0][...])
    odd = jnp.where(turned, first_refs[0][...], first_refs[1][...])
    panel = jnp.concatenate(
        [jnp.concatenate([even, odd], 0), jnp.concatenate([ref[...] for ref in second_refs], 0)], 1
    )
    change = low_rank(split_ref, panel)
    out_ref[...] = jnp.where(outside(row_ids) & outside(col_ids), rows_ref[...] - change, 0.0)


def finish(before, first, second, second_at, weights, scalars):
    rows, order = before.shape
    low, high = order - 3 * TILE, order - TILE
    count = order // (2 * TILE)
    layers = order // TILE // 8
    wide = lambda index: pl.BlockSpec((rows, 2 * TILE), index)
    piece = pl.BlockSpec((TILE, TILE), lambda n, s: (place_of((2 * n) ^ s[1], layers), 0))
    later = lambda side: pl.BlockSpec((TILE, TILE), lambda n, s: (second_at(2 * n + side, s[1]), 0))
    in_specs = [wide(lambda n, _: (0, n)), piece, piece, later(0), later(1), wide(lambda n, _: (0, 0))]
    args = [before, *first, second, second, weights]
    return pl.pallas_call(
        functools.partial(finish_kernel, low, high),
        out_shape=jax.ShapeDtypeStruct((rows, order), jnp.float32),
        grid_spec=pltpu.PrefetchScalarGridSpec(
            num_scalar_prefetch=1,
            grid=(count,),
            in_specs=in_specs,
            out_specs=wide(lambda n, _: (0, n)),
            scratch_shapes=[pltpu.VMEM((2 * rows, 2 * TILE), jnp.bfloat16)],
        ),
        compiler_params=pltpu.CompilerParams(vmem_limit_bytes=48 * MIB),
        cost_estimate=lasting(count),
    )(scalars, *args)


def product(left, right, precision=HIGHEST):
    return jnp.dot(left, right, precision=precision, preferred_element_type=jnp.float32)


def product_nt(left, right, precision=HIGHEST):
    return lax.dot_general(left, right, NT, precision=precision, preferred_element_type=jnp.float32)


def swap(value, mask):
    pairs = [(source, source ^ mask) for source in range(lax.axis_size("cube"))]
    return lax.ppermute(value, "cube", pairs)


def group_gather(value, group):
    size = lax.axis_size("cube")
    groups = [[g * group + i for i in range(group)] for g in range(size // group)]
    return lax.all_gather(value, "cube", axis=0, tiled=True, axis_index_groups=groups)


def one_hot(positions, count):
    return (positions[None, :] == jnp.arange(count, dtype=jnp.int32)[:, None]).astype(jnp.float32)


def column_targets(front_map):
    order = front_map.shape[0]
    ids = jnp.arange(order, dtype=jnp.int32)
    gone = (ids >= order - 2 * TILE) & (ids < order - TILE)
    return jnp.where(gone, -1, front_map)


def leaving(front_map, front, group, rows):
    target = (front_map // rows) // group
    return (front_map >= 0) & (target != front % 2)


class Plan:
    def __init__(self, maps, group, rows):
        me = lax.axis_index("cube")
        front = me // group
        block = me % group
        side = front % 2
        targets = jax.vmap(column_targets)(maps)
        self.sent = (rows * 19 // 32 + 7) // 8 * 8
        fronts = jnp.arange(maps.shape[0], dtype=jnp.int32)
        leaves = leaving(targets, fronts[:, None], group, rows).reshape(maps.shape[0], group, rows)
        most = jnp.max(jnp.sum(leaves.astype(jnp.int32), -1))
        self.overflow = (most > self.sent).astype(jnp.int32).reshape(1)
        self.own_map = lax.dynamic_index_in_dim(targets, front, 0, keepdims=False)
        self.other_map = lax.dynamic_index_in_dim(targets, front ^ 1, 0, keepdims=False)
        own = lax.dynamic_slice_in_dim(self.own_map, block * rows, rows, 0)
        other = lax.dynamic_slice_in_dim(self.other_map, block * rows, rows, 0)
        here = (block + group * side) * rows
        there = (block + group * (1 - side)) * rows
        self.keep = one_hot(own - here, rows)
        self.give = one_hot(own - there, rows)
        ids = jnp.arange(rows, dtype=jnp.int32)
        upper = (ids[:, None] <= ids[None, :]).astype(jnp.bfloat16)
        leaves = (own >= there) & (own < there + rows)
        comes = (other >= here) & (other < here + rows)
        flags = jnp.stack([leaves, comes]).astype(jnp.bfloat16)
        ranks = jnp.dot(flags, upper, preferred_element_type=jnp.float32).astype(jnp.int32) - 1
        send = one_hot(jnp.where(leaves, ranks[0], -1), rows)
        self.select = jnp.concatenate([self.keep, send], 0).astype(jnp.bfloat16)
        taken = one_hot(jnp.where(comes, ranks[1], -1), rows).astype(jnp.bfloat16)
        slots = one_hot(other - here, rows).astype(jnp.bfloat16)
        place = lax.dot_general(slots, taken, NT, preferred_element_type=jnp.float32).astype(jnp.bfloat16)
        fill = lambda part: jnp.pad(part, ((0, 0), (0, -part.shape[1] % 16)))
        self.place = fill(place[:, : self.sent])
        self.place_spare = fill(place[:, self.sent :])


def spread_block(block, group, owner_low, rows):
    size = lax.axis_size("cube")
    me = lax.axis_index("cube")
    holders = max(1, TILE // rows)
    has = {d for d in range(size) if owner_low <= d % group < owner_low + holders}
    inside = (me % group >= owner_low) & (me % group < owner_low + holders)
    block = jnp.where(inside, block, 0.0)
    mask = group // 2
    while mask >= holders:
        pairs = [(d, d ^ mask) for d in sorted(has)]
        block = block + lax.ppermute(block, "cube", pairs)
        has |= {d ^ mask for d in has}
        mask //= 2
    return block


def whole_block(part, rows):
    if rows >= TILE:
        return part
    return group_gather(part, TILE // rows)


def place_of(turned, layers):
    span = layers // 2
    layer, y, x = turned // 8, turned // 4 % 2, turned // 2 % 2
    lower = (2 * y + x) * span + layer
    upper = (4 + 2 * x + y) * span + layer - span
    return jnp.where(layer < span, lower, upper)


def cross_planes(block):
    layers = lax.axis_size("cube") // 8
    if block.shape[0] != TILE:
        return [block]
    return [block] + [swap(block, 8 * layer) for layer in range(1, layers)]


def spread_crossed(stack, low):
    rows = stack[0].shape[-2]
    if rows != TILE:
        parts = stack[0].reshape(-1, rows, TILE)
        blocks = jnp.stack([whole_block(part, rows) for part in parts]).reshape(*stack[0].shape[:-2], TILE, TILE)
        return spread_block(blocks, lax.axis_size("cube"), low // rows, rows)
    owner = low // rows
    layer = lax.axis_index("cube") // 8 ^ owner // 8
    block = stack[0]
    for number in range(1, len(stack)):
        block = jnp.where(layer == number, stack[number], block)
    return spread_block(block, 8, owner % 8, rows)


def gather_second(stack):
    layers = lax.axis_size("cube") // 8
    if stack[0].shape[0] != TILE:
        return lax.all_gather(stack[0], "cube", axis=0, tiled=True), lambda cb, me: cb
    return group_gather(jnp.concatenate(stack, 0), 8), lambda cb, me: cb % 8 * layers + (cb // 8 ^ me // 8)


def gather_first(stack, after):
    size = lax.axis_size("cube")
    layers = size // 8
    block = stack[0]
    if block.shape[0] != TILE:
        whole = lax.all_gather(block, "cube", axis=0, tiled=True)
        order = whole.shape[0]
        layers = order // TILE // 8
        spots = [0] * (4 * layers)
        for m in range(4 * layers):
            layer, y, x = m // 4, m // 2 % 2, m % 2
            span = layers // 2
            spot = (2 * y + x) * span + layer if layer < span else (4 + 2 * x + y) * span + layer - span
            spots[spot] = m
        blocks = whole.reshape(order // TILE, TILE, TILE)
        sides = [jnp.concatenate([blocks[2 * m + side] for m in spots], 0) for side in range(2)]
        return sides, jnp.int32(0), after
    me = lax.axis_index("cube")
    one = jnp.concatenate(stack[: layers // 2], 0)
    two = jnp.concatenate(stack[layers // 2 :], 0)
    one = jnp.concatenate([one, swap(one, 2)], 0)
    two = jnp.concatenate([two, swap(two, 4)], 0)
    even = jnp.concatenate([one, swap(one, 4), two, swap(two, 2)], 0)
    even, after = lax.optimization_barrier((even, after))
    odd = swap(even, 1)
    return (even, odd), me, after


def local(gfront, cfront, rfront, gmap, cmap):
    devices = lax.axis_size("cube")
    me = lax.axis_index("cube")
    quarter = devices // 4
    half = devices // 2
    rows = gfront.shape[0]
    order_g, order_c, order_r = gfront.shape[1], cfront.shape[1], rfront.shape[1]
    g_low, c_low = order_g - 2 * TILE, order_c - 2 * TILE
    r_low = order_r - 3 * TILE
    r_high = r_low + TILE

    def exchange(send, spare, plan, mask):
        rest = lax.cond(plan.overflow[0] != 0, lambda part: swap(part, mask), jnp.zeros_like, spare)
        return swap(send, mask), rest

    own_g = gfront[:, g_low : g_low + TILE]
    own_c = cfront[:, c_low : c_low + TILE]
    own_second = rfront[:, r_high : r_high + TILE]
    panel_g = group_gather(own_g, quarter)
    panel_c = group_gather(own_c, half)
    crossed = cross_planes(own_second)
    inverse_g = inverse_factors(panel_g[g_low : g_low + TILE][None])[0]
    plan_g = Plan(gmap, quarter, rows)
    plan_c = Plan(cmap, half, rows)

    gfactor = product_nt(own_g, inverse_g)
    weights_g = product(gfactor, inverse_g)

    g_keep, g_send, g_spare = update_and_pick(gfront, panel_g, weights_g, plan_g)
    panel_c, g_send = lax.optimization_barrier((panel_c, g_send))
    inverse_c = inverse_factors(panel_c[c_low : c_low + TILE][None])[0]
    second, second_at = gather_second(crossed)
    cfactor = product_nt(own_c, inverse_c)
    weights_c = product(cfactor, inverse_c)

    g_edge = gfront[:, g_low - TILE : g_low] - product_nt(weights_g, panel_g[g_low - TILE : g_low])
    edge_map = plan_g.own_map[g_low - TILE : g_low]
    g_edge = product_nt(g_edge, one_hot(edge_map - (c_low - TILE), TILE))
    c_edge = cfront[:, c_low - TILE : c_low] - product_nt(weights_c, panel_c[c_low - TILE : c_low])
    c_edge = c_edge + product(plan_g.keep, g_edge) + swap(product(plan_g.give, g_edge), quarter)
    g_recv, g_rest = exchange(g_send, g_spare, plan_g, quarter)
    c_edge, g_recv = lax.optimization_barrier((c_edge, g_recv))
    edge_map = plan_c.own_map[c_low - TILE : c_low]
    c_edge = product_nt(c_edge, one_hot(edge_map - r_low, TILE))
    r_edge = rfront[:, r_low : r_low + TILE] + product(plan_c.keep, c_edge)
    r_come = swap(product(plan_c.give, c_edge), half)
    c_base = cfront - product_nt(weights_c, panel_c, HIGH)
    c_keep, c_send, c_spare = assemble(c_base, g_keep, g_recv, g_rest, plan_g, plan_c)
    c_recv, c_rest = exchange(c_send, c_spare, plan_c, half)
    r_come, c_send = lax.optimization_barrier((r_come, c_send))
    r_edge = r_edge + r_come
    stack = cross_planes(r_edge)
    root_11 = spread_crossed(stack, r_low)
    root_21, root_22 = spread_crossed([jnp.stack(both) for both in zip(stack, crossed)], r_high)

    inv_11 = inverse_factors(root_11[None])[0]
    low_21 = product_nt(root_21, inv_11)
    inv_22 = inverse_factors((root_22 - product_nt(low_21, low_21))[None])[0]
    inv_21 = -product(inv_22, product(low_21, inv_11))

    factor_1 = product_nt(r_edge, inv_11)
    factor_2 = product_nt(r_edge, inv_21) + product_nt(own_second, inv_22)
    weights_1 = product(factor_1, inv_11) + product(factor_2, inv_21)
    weights_2 = product(factor_2, inv_22)
    row_ids = me * rows + jnp.arange(rows, dtype=jnp.int32)
    above = (row_ids >= r_low) & (row_ids < r_high)
    factor_2 = jnp.where(above[:, None], 0.0, factor_2)
    rfactor = jnp.concatenate([factor_1, factor_2], 1)
    weights_r = jnp.concatenate([weights_1, weights_2], 1)
    after = (c_recv, c_rest, weights_r, second)
    first, turn, (c_recv, c_rest, weights_r, second) = gather_first(stack, after)
    scalars = jnp.stack([me * rows, turn]).astype(jnp.int32)
    r_rows = assemble(rfront, c_keep, c_recv, c_rest, plan_c)
    rschur = finish(r_rows, first, second, second_at, weights_r, scalars)
    return (gfactor, cfactor, rfactor, rschur)


def solution(mesh):
    placed = (P("cube", None), P("cube", None), P("cube", None), P(), P())
    return jax.shard_map(
        local,
        mesh=mesh,
        in_specs=placed,
        out_specs=(P("cube", None), P("cube", None), P("cube", None), P("cube", None)),
        check_vma=False,
    )
```

```python
import functools

import jax
import jax.numpy as jnp
from jax import lax
from jax.experimental import pallas as pl
from jax.experimental.pallas import tpu as pltpu
from jax.sharding import PartitionSpec as P

TILE = 256
STRIP = 32
SUB = 8
LANES = 128
HIGH = lax.Precision.HIGH
HIGHEST = lax.Precision.HIGHEST
NT = (((1,), (1,)), ((), ()))
MIB = 1024 * 1024


def lasting(microseconds):
    return pl.CostEstimate(flops=1, bytes_accessed=int(microseconds * 3_500_000), transcendentals=0)


def widen(column, width):
    return jnp.concatenate([column] * (width // LANES), 1)


def factor_strip(strip, base):
    width = strip[0].shape[1]
    sub_ids = lax.broadcasted_iota(jnp.int32, (SUB, 1), 0)
    count = len(strip)
    for p in range(count):
        first = base + p * SUB
        cols = [
            [jnp.broadcast_to(strip[q][:, first + j : first + j + 1], (SUB, LANES)) for j in range(SUB)]
            for q in range(p, count)
        ]
        for j in range(SUB):
            pivot = cols[0][j][j : j + 1, :]
            inv = lax.rsqrt(pivot)
            inv = inv * (1.5 - 0.5 * pivot * inv * inv)
            unit = strip[p][j : j + 1, :] * widen(inv, width)
            scaled = [col[j] * inv for col in cols]
            below = jnp.where(sub_ids > j, scaled[0], 0.0)
            strip[p] = jnp.where(sub_ids == j, unit, strip[p] - widen(below, width) * unit)
            for q in range(p + 1, count):
                strip[q] = strip[q] - widen(scaled[q - p], width) * unit
            for m in range(j + 1, SUB):
                head = scaled[0][m : m + 1, :]
                for q in range(p, count):
                    cols[q - p][m] = cols[q - p][m] - scaled[q - p] * head
    return jnp.concatenate(strip, 0)


def inverse_kernel(count, blocks_ref, inverse_ref, work):
    row_ids = lax.broadcasted_iota(jnp.int32, (TILE, TILE), 0)
    col_ids = lax.broadcasted_iota(jnp.int32, (TILE, TILE), 1)
    for t in range(count):
        work[t, :, :TILE] = blocks_ref[t]
        work[t, :, TILE:] = (row_ids == col_ids).astype(jnp.float32)
    for low in range(0, TILE, STRIP):
        high = low + STRIP
        left = low // LANES * LANES
        right = TILE + (high + LANES - 1) // LANES * LANES
        done = []
        for t in range(count):
            strip = [work[t, low + SUB * q : low + SUB * (q + 1), left:right] for q in range(STRIP // SUB)]
            done.append(factor_strip(strip, low - left))
        for t in range(count):
            inverse_ref[t, low:high, : right - TILE] = done[t][:, TILE - left :]
            if right < 2 * TILE:
                inverse_ref[t, low:high, right - TILE :] = jnp.zeros((STRIP, 2 * TILE - right), jnp.float32)
            if high < TILE:
                rest = high // LANES * LANES
                update = lax.dot_general(
                    done[t][:, rest - left : TILE - left],
                    done[t],
                    (((0,), (0,)), ((), ())),
                    precision=HIGHEST,
                    preferred_element_type=jnp.float32,
                )
                work[t, high:, left:right] = work[t, high:, left:right] - update[high - rest :]


def inverse_factors(blocks):
    count = blocks.shape[0]
    return pl.pallas_call(
        functools.partial(inverse_kernel, count),
        out_shape=jax.ShapeDtypeStruct(blocks.shape, jnp.float32),
        in_specs=[pl.BlockSpec(memory_space=pltpu.VMEM)],
        out_specs=pl.BlockSpec(memory_space=pltpu.VMEM),
        scratch_shapes=[pltpu.VMEM((count, TILE, 2 * TILE), jnp.float32)],
        compiler_params=pltpu.CompilerParams(vmem_limit_bytes=16 * MIB),
        cost_estimate=lasting(1),
    )(blocks)


def halves(value):
    top = value.astype(jnp.bfloat16)
    return top, (value - top.astype(jnp.float32)).astype(jnp.bfloat16)


def dot_nt(left, right):
    return lax.dot_general(left, right, NT, preferred_element_type=jnp.float32)


def dot_nn(left, right):
    return jnp.dot(left, right, preferred_element_type=jnp.float32)


def pad_rows(value, count):
    short = count - value.shape[0]
    return value if short == 0 else jnp.concatenate([value, jnp.zeros((short, value.shape[1]), value.dtype)], 0)


def stacked(value):
    return jnp.concatenate(halves(value), 0)


def add_moved(total_ref, recv_ref, place_ref, hot, cols):
    count = place_ref.shape[1]
    moved = dot_nt(stacked(pad_rows(recv_ref[:, cols], count)), hot).astype(jnp.bfloat16)
    total_ref[:, cols] += dot_nn(place_ref[...], moved[:count]) + dot_nn(place_ref[...], moved[count:])


def pick_rows(total, select_ref, outs, cols):
    keep_ref, send_ref, spare_ref = outs
    rows = total.shape[0]
    sent = send_ref.shape[0]
    top, rest = halves(total)
    top = dot_nn(select_ref[...], top)
    rest = dot_nn(select_ref[...], rest)
    keep_ref[:rows, cols] = top[:rows].astype(jnp.bfloat16)
    keep_ref[rows:, cols] = rest[:rows].astype(jnp.bfloat16)
    both = top[rows:] + rest[rows:]
    send_ref[:, cols] = both[:sent]
    spare_ref[:, cols] = both[sent:]


def low_rank(weights_ref, panel):
    rows = weights_ref.shape[0] // 2
    top, rest = halves(panel)
    main = dot_nt(weights_ref[...], top)
    return main[:rows] + (main[rows:] + dot_nt(weights_ref[:rows], rest))


def update_kernel(rows_ref, panel_ref, weights_ref, select_ref, keep_ref, send_ref, spare_ref, split_ref):
    @pl.when(pl.program_id(0) == 0)
    def _():
        split_ref[...] = stacked(weights_ref[...])

    total = rows_ref[...] - low_rank(split_ref, panel_ref[...])
    pick_rows(total, select_ref, (keep_ref, send_ref, spare_ref), slice(0, TILE))


def assemble_kernel(picks, flag, *refs):
    base_ref, keep_ref, recv_ref, spare_ref, place_ref, place_spare_ref, keep_map_ref, recv_map_ref = refs[:8]
    total_ref = refs[-1]
    rows = base_ref.shape[0]
    for side in range(2):
        cols = slice(side * TILE, (side + 1) * TILE)
        first = (2 * pl.program_id(0) + side) * TILE
        targets = first + lax.broadcasted_iota(jnp.int32, (TILE, TILE), 0)
        keep_hot = jnp.where(keep_map_ref[:, cols] == targets, 1.0, 0.0).astype(jnp.bfloat16)
        recv_hot = jnp.where(recv_map_ref[:, cols] == targets, 1.0, 0.0).astype(jnp.bfloat16)
        kept = dot_nt(keep_ref[:, cols], keep_hot)
        total_ref[:, cols] = base_ref[:, cols] + (kept[:rows] + kept[rows:])
        add_moved(total_ref, recv_ref, place_ref, recv_hot, cols)

        @pl.when(flag[0] != 0)
        def _(recv_hot=recv_hot, cols=cols):
            add_moved(total_ref, spare_ref, place_spare_ref, recv_hot, cols)

        if picks:
            pick_rows(total_ref[:, cols], refs[8], refs[9:12], cols)
        else:
            refs[8][:, cols] = total_ref[:, cols]


def pick_shapes(rows, sent, width):
    return (
        jax.ShapeDtypeStruct((2 * rows, width), jnp.bfloat16),
        jax.ShapeDtypeStruct((sent, width), jnp.float32),
        jax.ShapeDtypeStruct((rows - sent, width), jnp.float32),
    )


def update_and_pick(rows_mat, panel, weights, plan):
    rows, order = rows_mat.shape
    sent = plan.sent
    fixed = lambda shape: pl.BlockSpec(shape, lambda n: (0, 0))
    moving = lambda count: pl.BlockSpec((count, TILE), lambda n: (0, n))
    return pl.pallas_call(
        update_kernel,
        grid=(order // TILE,),
        out_shape=pick_shapes(rows, sent, order),
        in_specs=[
            moving(rows),
            pl.BlockSpec((TILE, TILE), lambda n: (n, 0)),
            fixed((rows, TILE)),
            fixed((2 * rows, rows)),
        ],
        out_specs=(moving(2 * rows), moving(sent), moving(rows - sent)),
        scratch_shapes=[pltpu.VMEM((2 * rows, TILE), jnp.bfloat16)],
        compiler_params=pltpu.CompilerParams(vmem_limit_bytes=48 * MIB),
        cost_estimate=lasting(order // TILE),
    )(rows_mat, panel, weights, plan.select)


def assemble(base, keep, recv, spare, plan, picks=None):
    rows, order = base.shape
    sent = recv.shape[0]
    per = recv.shape[1] // (2 * TILE)
    fixed = lambda shape: pl.BlockSpec(shape, lambda n, _: (0, 0))
    child = lambda count: pl.BlockSpec((count, 2 * TILE), lambda n, _: (0, n % per))
    mapped = pl.BlockSpec((1, 2 * TILE), lambda n, _: (0, n % per))
    wide = lambda count: pl.BlockSpec((count, 2 * TILE), lambda n, _: (0, n))
    in_specs = [
        wide(rows),
        child(2 * rows),
        child(sent),
        pl.BlockSpec((rows - sent, 2 * TILE), lambda n, flag: (0, n % per * flag[0])),
        fixed(plan.place.shape),
        fixed(plan.place_spare.shape),
        mapped,
        mapped,
    ]
    args = [base, keep, recv, spare, plan.place, plan.place_spare, plan.own_map[None], plan.other_map[None]]
    width = order
    if picks is None:
        out_shape = jax.ShapeDtypeStruct((rows, width), jnp.float32)
        out_specs = wide(rows)
    else:
        in_specs.append(fixed((2 * rows, rows)))
        args.append(picks.select)
        out_shape = pick_shapes(rows, picks.sent, width)
        out_specs = (wide(2 * rows), wide(picks.sent), wide(rows - picks.sent))
    return pl.pallas_call(
        functools.partial(assemble_kernel, picks is not None),
        out_shape=out_shape,
        grid_spec=pltpu.PrefetchScalarGridSpec(
            num_scalar_prefetch=1,
            grid=(2 * per,),
            in_specs=in_specs,
            out_specs=out_specs,
            scratch_shapes=[pltpu.VMEM((rows, 2 * TILE), jnp.float32)],
        ),
        compiler_params=pltpu.CompilerParams(vmem_limit_bytes=48 * MIB),
        cost_estimate=lasting(4 * per),
    )(plan.overflow, *args)


def finish_kernel(low, high, where_ref, rows_ref, *refs):
    first_refs, second_refs, weights_ref = refs[:2], refs[2:4], refs[4]
    out_ref, split_ref = refs[-2:]
    n = pl.program_id(0)

    @pl.when(n == 0)
    def _():
        split_ref[...] = stacked(weights_ref[...])

    rows = rows_ref.shape[0]
    row_ids = where_ref[0] + lax.broadcasted_iota(jnp.int32, (rows, 1), 0)
    col_ids = n * 2 * TILE + lax.broadcasted_iota(jnp.int32, (1, 2 * TILE), 1)
    outside = lambda ids: (ids < low) | (ids >= high)
    turned = where_ref[1] % 2 != 0
    even = jnp.where(turned, first_refs[1][...], first_refs[0][...])
    odd = jnp.where(turned, first_refs[0][...], first_refs[1][...])
    panel = jnp.concatenate(
        [jnp.concatenate([even, odd], 0), jnp.concatenate([ref[...] for ref in second_refs], 0)], 1
    )
    change = low_rank(split_ref, panel)
    out_ref[...] = jnp.where(outside(row_ids) & outside(col_ids), rows_ref[...] - change, 0.0)


def finish(before, first, second, second_at, weights, scalars):
    rows, order = before.shape
    low, high = order - 3 * TILE, order - TILE
    count = order // (2 * TILE)
    layers = order // TILE // 8
    wide = lambda index: pl.BlockSpec((rows, 2 * TILE), index)
    piece = pl.BlockSpec((TILE, TILE), lambda n, s: (place_of((2 * n) ^ s[1], layers), 0))
    later = lambda side: pl.BlockSpec((TILE, TILE), lambda n, s: (second_at(2 * n + side, s[1]), 0))
    in_specs = [wide(lambda n, _: (0, n)), piece, piece, later(0), later(1), wide(lambda n, _: (0, 0))]
    args = [before, *first, second, second, weights]
    return pl.pallas_call(
        functools.partial(finish_kernel, low, high),
        out_shape=jax.ShapeDtypeStruct((rows, order), jnp.float32),
        grid_spec=pltpu.PrefetchScalarGridSpec(
            num_scalar_prefetch=1,
            grid=(count,),
            in_specs=in_specs,
            out_specs=wide(lambda n, _: (0, n)),
            scratch_shapes=[pltpu.VMEM((2 * rows, 2 * TILE), jnp.bfloat16)],
        ),
        compiler_params=pltpu.CompilerParams(vmem_limit_bytes=48 * MIB),
        cost_estimate=lasting(count),
    )(scalars, *args)


def product(left, right, precision=HIGHEST):
    return jnp.dot(left, right, precision=precision, preferred_element_type=jnp.float32)


def product_nt(left, right, precision=HIGHEST):
    return lax.dot_general(left, right, NT, precision=precision, preferred_element_type=jnp.float32)


def swap(value, mask):
    pairs = [(source, source ^ mask) for source in range(lax.axis_size("cube"))]
    return lax.ppermute(value, "cube", pairs)


def group_gather(value, group):
    size = lax.axis_size("cube")
    groups = [[g * group + i for i in range(group)] for g in range(size // group)]
    return lax.all_gather(value, "cube", axis=0, tiled=True, axis_index_groups=groups)


def one_hot(positions, count):
    return (positions[None, :] == jnp.arange(count, dtype=jnp.int32)[:, None]).astype(jnp.float32)


def column_targets(front_map):
    order = front_map.shape[0]
    ids = jnp.arange(order, dtype=jnp.int32)
    gone = (ids >= order - 2 * TILE) & (ids < order - TILE)
    return jnp.where(gone, -1, front_map)


def leaving(front_map, front, group, rows):
    target = (front_map // rows) // group
    return (front_map >= 0) & (target != front % 2)


class Plan:
    def __init__(self, maps, group, rows):
        me = lax.axis_index("cube")
        front = me // group
        block = me % group
        side = front % 2
        targets = jax.vmap(column_targets)(maps)
        self.sent = (rows * 19 // 32 + 7) // 8 * 8
        fronts = jnp.arange(maps.shape[0], dtype=jnp.int32)
        leaves = leaving(targets, fronts[:, None], group, rows).reshape(maps.shape[0], group, rows)
        most = jnp.max(jnp.sum(leaves.astype(jnp.int32), -1))
        self.overflow = (most > self.sent).astype(jnp.int32).reshape(1)
        self.own_map = lax.dynamic_index_in_dim(targets, front, 0, keepdims=False)
        self.other_map = lax.dynamic_index_in_dim(targets, front ^ 1, 0, keepdims=False)
        own = lax.dynamic_slice_in_dim(self.own_map, block * rows, rows, 0)
        other = lax.dynamic_slice_in_dim(self.other_map, block * rows, rows, 0)
        here = (block + group * side) * rows
        there = (block + group * (1 - side)) * rows
        self.keep = one_hot(own - here, rows)
        self.give = one_hot(own - there, rows)
        ids = jnp.arange(rows, dtype=jnp.int32)
        upper = (ids[:, None] <= ids[None, :]).astype(jnp.bfloat16)
        leaves = (own >= there) & (own < there + rows)
        comes = (other >= here) & (other < here + rows)
        flags = jnp.stack([leaves, comes]).astype(jnp.bfloat16)
        ranks = jnp.dot(flags, upper, preferred_element_type=jnp.float32).astype(jnp.int32) - 1
        send = one_hot(jnp.where(leaves, ranks[0], -1), rows)
        self.select = jnp.concatenate([self.keep, send], 0).astype(jnp.bfloat16)
        taken = one_hot(jnp.where(comes, ranks[1], -1), rows).astype(jnp.bfloat16)
        slots = one_hot(other - here, rows).astype(jnp.bfloat16)
        place = lax.dot_general(slots, taken, NT, preferred_element_type=jnp.float32).astype(jnp.bfloat16)
        fill = lambda part: jnp.pad(part, ((0, 0), (0, -part.shape[1] % 16)))
        self.place = fill(place[:, : self.sent])
        self.place_spare = fill(place[:, self.sent :])


def spread_block(block, group, owner_low, rows):
    size = lax.axis_size("cube")
    me = lax.axis_index("cube")
    holders = max(1, TILE // rows)
    has = {d for d in range(size) if owner_low <= d % group < owner_low + holders}
    inside = (me % group >= owner_low) & (me % group < owner_low + holders)
    block = jnp.where(inside, block, 0.0)
    mask = group // 2
    while mask >= holders:
        pairs = [(d, d ^ mask) for d in sorted(has)]
        block = block + lax.ppermute(block, "cube", pairs)
        has |= {d ^ mask for d in has}
        mask //= 2
    return block


def whole_block(part, rows):
    if rows >= TILE:
        return part
    return group_gather(part, TILE // rows)


def place_of(turned, layers):
    span = layers // 2
    layer, y, x = turned // 8, turned // 4 % 2, turned // 2 % 2
    lower = (2 * y + x) * span + layer
    upper = (4 + 2 * x + y) * span + layer - span
    return jnp.where(layer < span, lower, upper)


def cross_planes(block):
    layers = lax.axis_size("cube") // 8
    if block.shape[0] != TILE:
        return [block]
    return [block] + [swap(block, 8 * layer) for layer in range(1, layers)]


def spread_crossed(stack, low):
    rows = stack[0].shape[-2]
    if rows != TILE:
        parts = stack[0].reshape(-1, rows, TILE)
        blocks = jnp.stack([whole_block(part, rows) for part in parts]).reshape(*stack[0].shape[:-2], TILE, TILE)
        return spread_block(blocks, lax.axis_size("cube"), low // rows, rows)
    owner = low // rows
    layer = lax.axis_index("cube") // 8 ^ owner // 8
    block = stack[0]
    for number in range(1, len(stack)):
        block = jnp.where(layer == number, stack[number], block)
    return spread_block(block, 8, owner % 8, rows)


def gather_second(stack):
    layers = lax.axis_size("cube") // 8
    if stack[0].shape[0] != TILE:
        return lax.all_gather(stack[0], "cube", axis=0, tiled=True), lambda cb, me: cb
    return group_gather(jnp.concatenate(stack, 0), 8), lambda cb, me: cb % 8 * layers + (cb // 8 ^ me // 8)


def gather_first(stack, after):
    size = lax.axis_size("cube")
    layers = size // 8
    block = stack[0]
    if block.shape[0] != TILE:
        whole = lax.all_gather(block, "cube", axis=0, tiled=True)
        order = whole.shape[0]
        layers = order // TILE // 8
        spots = [0] * (4 * layers)
        for m in range(4 * layers):
            layer, y, x = m // 4, m // 2 % 2, m % 2
            span = layers // 2
            spot = (2 * y + x) * span + layer if layer < span else (4 + 2 * x + y) * span + layer - span
            spots[spot] = m
        blocks = whole.reshape(order // TILE, TILE, TILE)
        sides = [jnp.concatenate([blocks[2 * m + side] for m in spots], 0) for side in range(2)]
        return sides, jnp.int32(0), after
    me = lax.axis_index("cube")
    one = jnp.concatenate(stack[: layers // 2], 0)
    two = jnp.concatenate(stack[layers // 2 :], 0)
    one = jnp.concatenate([one, swap(one, 2)], 0)
    two = jnp.concatenate([two, swap(two, 4)], 0)
    even = jnp.concatenate([one, swap(one, 4), two, swap(two, 2)], 0)
    even, after = lax.optimization_barrier((even, after))
    odd = swap(even, 1)
    return (even, odd), me, after


def local(gfront, cfront, rfront, gmap, cmap):
    devices = lax.axis_size("cube")
    me = lax.axis_index("cube")
    quarter = devices // 4
    half = devices // 2
    rows = gfront.shape[0]
    order_g, order_c, order_r = gfront.shape[1], cfront.shape[1], rfront.shape[1]
    g_low, c_low = order_g - 2 * TILE, order_c - 2 * TILE
    r_low = order_r - 3 * TILE
    r_high = r_low + TILE

    def exchange(send, spare, plan, mask):
        rest = lax.cond(plan.overflow[0] != 0, lambda part: swap(part, mask), jnp.zeros_like, spare)
        return swap(send, mask), rest

    own_g = gfront[:, g_low : g_low + TILE]
    own_c = cfront[:, c_low : c_low + TILE]
    own_second = rfront[:, r_high : r_high + TILE]
    panel_g = group_gather(own_g, quarter)
    panel_c = group_gather(own_c, half)
    crossed = cross_planes(own_second)
    inverse_g = inverse_factors(panel_g[g_low : g_low + TILE][None])[0]
    plan_g = Plan(gmap, quarter, rows)
    plan_c = Plan(cmap, half, rows)

    gfactor = product_nt(own_g, inverse_g)
    weights_g = product(gfactor, inverse_g)

    g_keep, g_send, g_spare = update_and_pick(gfront, panel_g, weights_g, plan_g)
    panel_c, g_send = lax.optimization_barrier((panel_c, g_send))
    inverse_c = inverse_factors(panel_c[c_low : c_low + TILE][None])[0]
    second, second_at = gather_second(crossed)
    cfactor = product_nt(own_c, inverse_c)
    weights_c = product(cfactor, inverse_c)

    g_edge = gfront[:, g_low - TILE : g_low] - product_nt(weights_g, panel_g[g_low - TILE : g_low])
    edge_map = plan_g.own_map[g_low - TILE : g_low]
    g_edge = product_nt(g_edge, one_hot(edge_map - (c_low - TILE), TILE))
    c_edge = cfront[:, c_low - TILE : c_low] - product_nt(weights_c, panel_c[c_low - TILE : c_low])
    c_edge = c_edge + product(plan_g.keep, g_edge) + swap(product(plan_g.give, g_edge), quarter)
    g_recv, g_rest = exchange(g_send, g_spare, plan_g, quarter)
    c_edge, g_recv = lax.optimization_barrier((c_edge, g_recv))
    edge_map = plan_c.own_map[c_low - TILE : c_low]
    c_edge = product_nt(c_edge, one_hot(edge_map - r_low, TILE))
    r_edge = rfront[:, r_low : r_low + TILE] + product(plan_c.keep, c_edge)
    r_come = swap(product(plan_c.give, c_edge), half)
    c_base = cfront - product_nt(weights_c, panel_c, HIGH)
    c_keep, c_send, c_spare = assemble(c_base, g_keep, g_recv, g_rest, plan_g, plan_c)
    c_recv, c_rest = exchange(c_send, c_spare, plan_c, half)
    r_come, c_send = lax.optimization_barrier((r_come, c_send))
    r_edge = r_edge + r_come
    stack = cross_planes(r_edge)
    root_11 = spread_crossed(stack, r_low)
    root_21, root_22 = spread_crossed([jnp.stack(both) for both in zip(stack, crossed)], r_high)

    inv_11 = inverse_factors(root_11[None])[0]
    low_21 = product_nt(root_21, inv_11)
    inv_22 = inverse_factors((root_22 - product_nt(low_21, low_21))[None])[0]
    inv_21 = -product(inv_22, product(low_21, inv_11))

    factor_1 = product_nt(r_edge, inv_11)
    factor_2 = product_nt(r_edge, inv_21) + product_nt(own_second, inv_22)
    weights_1 = product(factor_1, inv_11) + product(factor_2, inv_21)
    weights_2 = product(factor_2, inv_22)
    row_ids = me * rows + jnp.arange(rows, dtype=jnp.int32)
    above = (row_ids >= r_low) & (row_ids < r_high)
    factor_2 = jnp.where(above[:, None], 0.0, factor_2)
    rfactor = jnp.concatenate([factor_1, factor_2], 1)
    weights_r = jnp.concatenate([weights_1, weights_2], 1)
    first, turn, (c_recv, _, second) = gather_first(stack, (c_recv, inv_22, second))
    scalars = jnp.stack([me * rows, turn]).astype(jnp.int32)
    r_rows = assemble(rfront, c_keep, c_recv, c_rest, plan_c)
    rschur = finish(r_rows, first, second, second_at, weights_r, scalars)
    return (gfactor, cfactor, rfactor, rschur)


def solution(mesh):
    placed = (P("cube", None), P("cube", None), P("cube", None), P(), P())
    return jax.shard_map(
        local,
        mesh=mesh,
        in_specs=placed,
        out_specs=(P("cube", None), P("cube", None), P("cube", None), P("cube", None)),
        check_vma=False,
    )
```
